32 devices in a mesh: group: 2 (over x), expert: 16 (over z, y, core).
Axes of the slice: x: 2, y: 2, z: 4, core: 2. Of those that a mesh axis runs over, the one named last changes fastest.
Arguments:
- tokens: bfloat16 [4096, 1536], P(('group', 'expert')), parts along dimension 0, may hold values from -6 to 6
- expert_ids: int32 [4096, 4], P(('group', 'expert')), parts along dimension 0, may hold values from 0 to 15, all different within a row; in each aligned block of 128 rows (0 to 127, 128 to 255, ...) at most 64 rows name the same one
- gate_levels: int32 [4096, 4], P(('group', 'expert')), parts along dimension 0, may hold values from 1 to 1023
- failed_device: int32 [1], replicated, may hold values from 0 to 15
- replica_holders: int32 [16, 4], replicated, may hold values from 0 to 15, as said below
- w_gate: bfloat16 [16, 1536, 1536], P('expert'), may hold values from -0.15625 to 0.15625
- w_down: bfloat16 [16, 1536, 1536], P('expert'), may hold values from -0.15625 to 0.15625
- spare_gate: bfloat16 [16, 1536, 384], P('expert'), may hold values from -0.15625 to 0.15625
- spare_down: bfloat16 [16, 384, 1536], P('expert'), may hold values from -0.15625 to 0.15625
Outputs:
- layer_out: bfloat16 [4096, 1536], P(('group', 'expert')), parts along dimension 0
The draws below stay inside these ranges and needn't reach their ends.
There are 2 independent parts, one for each index of `group`. The reference program is written for one: setup_inputs(seed, part) draws one part's arguments, and reference() takes and returns one part's arrays. A program takes and returns all parts, laid end to end along the dimension named above; an argument that names none is the same for every part. Nothing has to cross between parts.
Inputs may be any that keep to these rules, and one draw needn't show every extreme that they name: `expert_ids`: within the rows of one device, no expert is named more than 64 times, and in some device's rows one expert is named exactly 64 times. `replica_holders`: each row e lists 4 distinct devices, none equal to e; every device appears in exactly 4 rows.
All inputs are finite; a program needn't handle non-finite values.
Results may differ from the reference program's by a relative error of at most 0.0059.
Values may be sent and summed in bfloat16 or wider, within the bound.
No kernel may reach another device: no remote copies, remote signals or barrier semaphores. Data moves between devices by JAX's collectives and lax.ppermute only.
A program may use at most 128 MiB of HBM per device.

```python
import math
import jax
import jax.numpy as jnp
import numpy as np
from jax import lax

D = 1536
F = 1536
TOP = 4
REPL = 4
TOK_DEV = 128
EXPERTS = 16
TOKENS = 2048
CAPACITY = 64
FQ = 384
N_EXPERT = 16


def draw_replica_holders(key, part):
    key = jax.random.fold_in(key, 11)
    order = jax.random.permutation(key, EXPERTS).astype(jnp.int32)
    places = jnp.arange(EXPERTS, dtype=jnp.int32)
    ahead = jnp.arange(1, REPL + 1, dtype=jnp.int32)
    following = order[(places[:, None] + ahead[None, :]) % EXPERTS]
    return jnp.zeros((EXPERTS, REPL), jnp.int32).at[order].set(following)


def place_ends(array, key, least, largest):
    extent = array.shape
    place = [jax.random.randint(jax.random.fold_in(key, axis), (), 0, extent[axis]) for axis in range(len(extent))]
    array = array.at[tuple(place)].set(least)
    longest = extent.index(max(extent))
    place[longest] = (place[longest] + 1) % extent[longest]
    return array.at[tuple(place)].set(largest)


def shard_levels(rng, shape, pieces, smallest, largest):
    def one(axis_at, shards_of):
        steps = jax.random.uniform(jax.random.fold_in(jax.random.fold_in(rng, 6), axis_at), (shards_of,), jnp.float32, smallest / len(pieces), largest / len(pieces))
        return jnp.repeat(jnp.exp(steps), shape[axis_at] // shards_of).reshape((-1,) + (1,) * (len(shape) - axis_at - 1))

    loudness = one(*pieces[0])
    for cut in pieces[1:]:
        loudness = loudness * one(*cut)
    return loudness


def deal_out(stream_key, own, number, rows, number_of, top, limit, slope):
    order = jax.random.permutation(stream_key, number_of)
    heavy_load, common = load_shares(number_of, rows * top, limit, slope, True), load_shares(number_of, rows * top, limit, slope, False)
    places = jnp.arange(number_of)

    def named(lengths, rotation):
        used = int((lengths > 0).sum())
        fixed = max(1, used // 4)
        passed = fixed + (places - fixed + rotation * (used - fixed)) % max(1, number_of - fixed)
        return jnp.zeros((number_of,), jnp.int32).at[order[jnp.where(places < fixed, places, passed)]].set(jnp.asarray(lengths, jnp.int32))

    lengths = jnp.where(number % 4 == 0, named(heavy_load, number // 4), named(common, number - number // 4 - 1))
    mixed = jax.random.permutation(jax.random.fold_in(own, 3), number_of)
    donor, taker = mixed[0:number_of // 2 * 2:2], mixed[1:number_of // 2 * 2:2]
    margin = jnp.minimum(lengths[donor] - 1, limit - lengths[taker]) // 2
    margin = jnp.where((donor == order[0]) | (taker == order[0]) | (lengths[taker] == 0), 0, jnp.maximum(margin, 0))
    passed = jax.random.randint(jax.random.fold_in(own, 4), (number_of // 2,), 0, 1 << 20) % (margin + 1)
    lengths = lengths.at[donor].add(-passed).at[taker].add(passed)
    labels = jnp.searchsorted(jnp.cumsum(lengths), jnp.arange(rows * top), side="right").astype(jnp.int32)
    table = labels.reshape(top, rows).T
    table = table[jax.random.permutation(jax.random.fold_in(own, 1), rows)]
    rotation = jax.random.randint(jax.random.fold_in(own, 2), (rows, 1), 0, top)
    return jnp.take_along_axis(table, (jnp.arange(top)[None, :] + rotation) % top, axis=1)


def load_shares(number_of, total, bound, skew, full):
    loads = [(1 << 20) // math.isqrt(grade ** skew) + 1 for grade in range(1, number_of + 1)]
    largest = bound if full else min(bound, max(-(-total // number_of), total * loads[0] // sum(loads)))
    least = 1 if total - largest >= number_of - 1 else 0
    counts, surplus = [largest] + [least] * (number_of - 1), total - largest - least * (number_of - 1)
    while surplus > 0:
        movable = [i for i in range(1, number_of) if counts[i] < largest] or [i for i in range(1, number_of) if counts[i] < bound]
        whole, left = sum([loads[i] for i in movable]), surplus
        for i in movable:
            extra = min(bound - counts[i], max(1, left * loads[i] // whole), surplus)
            counts[i] = counts[i] + extra
            surplus = surplus - extra
    return np.array(counts)


def scatter_about(rng, dims, deviation, reach, pieces=(), kind=jnp.bfloat16):
    drawn = jax.random.normal(rng, dims, jnp.float32) * deviation
    if len(pieces) > 0:
        drawn = shard_levels(rng, dims, pieces, -0.22, 0.18) * drawn
    return jnp.clip(drawn, min=-reach, max=reach).astype(kind)


def setup_inputs(seed: int = 0, part: int = 0) -> dict:
    key_of = jax.random.split(jax.random.key(seed), 10)
    own_keys = jax.random.split(jax.random.fold_in(key_of[9], part), 10)
    tokens = scatter_about(own_keys[0], (TOKENS, D), 1.0, 6.0, ((0, 16),))
    expert_ids_keys = jax.random.split(jax.random.fold_in(own_keys[1], 1), TOKENS // TOK_DEV)
    expert_ids_turns = jax.random.permutation(jax.random.fold_in(own_keys[1], 3), TOKENS // TOK_DEV)
    expert_ids = jax.vmap(lambda own, number: deal_out(jax.random.fold_in(own_keys[1], 2), own, number, TOK_DEV, EXPERTS, TOP, CAPACITY, 2))(expert_ids_keys, expert_ids_turns).reshape((TOKENS, TOP))
    gate_levels = place_ends(jax.random.randint(own_keys[2], (TOKENS, TOP), 1, 1024), jax.random.fold_in(own_keys[2], 1), 1, 1023).astype(jnp.int32)
    failed_device = jax.random.randint(key_of[3], (1,), 0, EXPERTS).astype(jnp.int32)
    replica_holders = draw_replica_holders(jax.random.fold_in(key_of[9], 71), part)
    w_gate = scatter_about(key_of[5], (EXPERTS, D, F), D ** -0.5, 0.15625, ((0, 16),))
    w_down = scatter_about(key_of[6], (EXPERTS, F, D), F ** -0.5, 0.15625, ((0, 16),))
    spare_gate = scatter_about(key_of[7], (EXPERTS, D, FQ), D ** -0.5, 0.15625, ((0, 16),))
    spare_down = scatter_about(key_of[8], (EXPERTS, FQ, D), F ** -0.5, 0.15625, ((0, 16),))
    return dict(tokens=tokens, expert_ids=expert_ids, gate_levels=gate_levels, failed_device=failed_device, replica_holders=replica_holders, w_gate=w_gate, w_down=w_down, spare_gate=spare_gate, spare_down=spare_down)


def gated_unit(values):
    return values * jax.nn.sigmoid(1.702 * values)


def reference(tokens, expert_ids, gate_levels, failed_device, replica_holders, w_gate, w_down, spare_gate, spare_down):
    blocks = N_EXPERT
    pair_count = TOK_DEV * TOP
    pair_ids = expert_ids.reshape(blocks, pair_count)
    expert_iota = jnp.arange(EXPERTS, dtype=jnp.int32)
    onehot_pairs = (pair_ids[:, :, None] == expert_iota[None, None, :]).astype(jnp.int32)
    earlier = jnp.cumsum(onehot_pairs, axis=1) - onehot_pairs
    slot_index = jnp.sum(earlier * onehot_pairs, axis=2).astype(jnp.int32)
    block_ids = jnp.broadcast_to(jnp.arange(blocks, dtype=jnp.int32)[:, None], (blocks, pair_count))
    token_ids = block_ids * TOK_DEV + jnp.arange(pair_count, dtype=jnp.int32)[None, :] // TOP
    levels = gate_levels.reshape(blocks, pair_count).astype(jnp.float32) / 1024.0
    token_table = jnp.zeros((EXPERTS, blocks, CAPACITY), jnp.int32).at[pair_ids, block_ids, slot_index].set(token_ids)
    weight_table = jnp.zeros((EXPERTS, blocks, CAPACITY), jnp.float32).at[pair_ids, block_ids, slot_index].set(levels)
    failed_id = failed_device[0]
    keep_mask = (expert_iota != failed_id).astype(jnp.float32)

    def expert_step(summed, expert):
        rows_at = token_table[expert].reshape(-1)
        rows_in = tokens[rows_at]
        hidden = gated_unit(jnp.dot(rows_in, w_gate[expert], preferred_element_type=jnp.float32)).astype(jnp.bfloat16)
        result = jnp.dot(hidden, w_down[expert], preferred_element_type=jnp.float32).astype(jnp.bfloat16)
        scale = weight_table[expert].reshape(-1) * keep_mask[expert]
        return summed.at[rows_at].add(result.astype(jnp.float32) * scale[:, None]), None

    summed, _ = lax.scan(expert_step, jnp.zeros((TOKENS, D), jnp.float32), expert_iota)
    rows_at = token_table[failed_id].reshape(-1)
    rows_in = tokens[rows_at]
    standby = jnp.zeros((blocks * CAPACITY, D), jnp.float32)
    for holder_slot in range(REPL):
        holder = replica_holders[failed_id, holder_slot]
        hidden = gated_unit(jnp.dot(rows_in, spare_gate[holder], preferred_element_type=jnp.float32)).astype(jnp.bfloat16)
        standby = standby + jnp.dot(hidden, spare_down[holder], preferred_element_type=jnp.float32)
    standby_out = standby.astype(jnp.bfloat16)
    summed = summed.at[rows_at].add(standby_out.astype(jnp.float32) * weight_table[failed_id].reshape(-1)[:, None])
    return summed.astype(jnp.bfloat16)
```

```python
import functools
import jax
import jax.numpy as jnp
from jax import lax
from jax.experimental import pallas as pl
from jax.experimental.pallas import tpu as pltpu
from jax.sharding import PartitionSpec as P

LEVELS = 1024


def gated_unit(values):
    return values * jax.nn.sigmoid(1.702 * values)


def expert_kernel(
    scalars,
    codes,
    tokens,
    w_gate,
    w_down,
    spare_gate,
    spare_down,
    out,
    rows_in,
    spare_in,
    hidden,
    spare_hidden,
    rows_out,
    *,
    subs,
    sources,
    capacity,
):
    tok = codes.shape[2]
    part = sources * tok
    rows = sources * capacity
    width = tokens.shape[1]
    tile = 512
    my_id, failed_id, holds = scalars[0], scalars[1], scalars[2]
    serves = my_id != failed_id

    before = (
        lax.broadcasted_iota(jnp.int32, (tok, tok), 0)
        < lax.broadcasted_iota(jnp.int32, (tok, tok), 1)
    ).astype(jnp.bfloat16)
    row_iota = lax.broadcasted_iota(jnp.int32, (rows, tok), 0)

    def picker(code, wanted, live):
        named = ((code // LEVELS) == wanted) & live
        mask = jnp.sum(named.astype(jnp.float32), axis=1)
        level = jnp.sum(jnp.where(named, (code % LEVELS), 0).astype(jnp.float32), axis=1) / LEVELS
        rank = jnp.dot(mask.astype(jnp.bfloat16), before, preferred_element_type=jnp.float32)
        picks, weights = [], None
        for s in range(sources):
            place = jnp.where(mask[s : s + 1] > 0, rank[s : s + 1].astype(jnp.int32) + s * capacity, -1)
            hit = row_iota == place
            scaled = jnp.sum(jnp.where(hit, level[s : s + 1], 0.0), axis=1, keepdims=True)
            weights = scaled if weights is None else weights + scaled
            picks.append(hit.astype(jnp.float32).astype(jnp.bfloat16))
        return jnp.concatenate(picks, axis=1), weights

    picks, weights, spare_weights = [], [], []
    for j in range(subs):
        code = codes[j * sources : (j + 1) * sources]
        pick, weight = picker(code, my_id, serves)
        spare_pick, spare_weight = picker(code, failed_id, holds > 0)
        both = jnp.concatenate([pick, spare_pick], axis=0)
        picks.append(both)
        weights.append(weight)
        spare_weights.append(spare_weight)
        for n in range(0, width, tile):
            got = jnp.dot(
                both, tokens[j * part : (j + 1) * part, n : n + tile], preferred_element_type=jnp.float32
            ).astype(jnp.bfloat16)
            rows_in[j * rows : (j + 1) * rows, n : n + tile] = got[:rows]
            spare_in[j * rows : (j + 1) * rows, n : n + tile] = got[rows:]

    for n in range(0, hidden.shape[1], tile):
        hidden[:, n : n + tile] = gated_unit(
            jnp.dot(rows_in[...], w_gate[0, :, n : n + tile], preferred_element_type=jnp.float32)
        ).astype(jnp.bfloat16)
    for n in range(0, width, tile):
        result = jnp.dot(hidden[...], w_down[0, :, n : n + tile], preferred_element_type=jnp.float32)
        result = result.astype(jnp.bfloat16).astype(jnp.float32)
        for j in range(subs):
            rows_out[j, :rows, n : n + tile] = (result[j * rows : (j + 1) * rows] * weights[j]).astype(
                jnp.bfloat16
            )

    @pl.when(holds > 0)
    def _():
        spare_hidden[...] = gated_unit(
            jnp.dot(spare_in[...], spare_gate[0], preferred_element_type=jnp.float32)
        ).astype(jnp.bfloat16)
        for n in range(0, width, tile):
            result = jnp.dot(
                spare_hidden[...], spare_down[0, :, n : n + tile], preferred_element_type=jnp.float32
            )
            for j in range(subs):
                rows_out[j, rows:, n : n + tile] = (
                    result[j * rows : (j + 1) * rows] * spare_weights[j]
                ).astype(jnp.bfloat16)

    @pl.when(holds <= 0)
    def _():
        rows_out[:, rows:, :] = jnp.zeros((subs, rows, width), jnp.bfloat16)

    for j in range(subs):
        for n in range(0, width, tile):
            out[j * part : (j + 1) * part, n : n + tile] = lax.dot_general(
                picks[j],
                rows_out[j, :, n : n + tile],
                (((0,), (0,)), ((), ())),
                preferred_element_type=jnp.float32,
            ).astype(jnp.bfloat16)


def run_experts(scalars, codes, tokens, w_gate, w_down, spare_gate, spare_down, capacity):
    owners, top, tok = codes.shape
    width, inner, spare = w_gate.shape[1], w_gate.shape[2], spare_gate.shape[2]
    sources = max(1, 128 // capacity)
    subs = 2 if sources * tok <= 512 else 1
    step = subs * sources
    rows = sources * capacity
    whole = lambda a: pl.BlockSpec(a.shape, lambda i: (0, 0, 0), pipeline_mode=pl.Buffered(1))
    return pl.pallas_call(
        functools.partial(expert_kernel, subs=subs, sources=sources, capacity=capacity),
        grid=(owners // step,),
        out_shape=jax.ShapeDtypeStruct((owners * tok, width), jnp.bfloat16),
        in_specs=[
            pl.BlockSpec(memory_space=pltpu.SMEM),
            pl.BlockSpec((step, top, tok), lambda i: (i, 0, 0)),
            pl.BlockSpec((step * tok, width), lambda i: (i, 0)),
            whole(w_gate),
            whole(w_down),
            whole(spare_gate),
            whole(spare_down),
        ],
        out_specs=pl.BlockSpec((step * tok, width), lambda i: (i, 0)),
        scratch_shapes=[
            pltpu.VMEM((subs * rows, width), jnp.bfloat16),
            pltpu.VMEM((subs * rows, width), jnp.bfloat16),
            pltpu.VMEM((subs * rows, inner), jnp.bfloat16),
            pltpu.VMEM((subs * rows, spare), jnp.bfloat16),
            pltpu.VMEM((subs, 2 * rows, width), jnp.bfloat16),
        ],
        compiler_params=pltpu.CompilerParams(vmem_limit_bytes=56 * 1024 * 1024),
        cost_estimate=pl.CostEstimate(
            flops=owners * capacity * 4 * width * (inner + spare),
            bytes_accessed=4 * width * (inner + spare) + 4 * owners * tok * width,
            transcendentals=owners * capacity * inner,
        ),
        name="experts",
    )(scalars, codes, tokens, w_gate, w_down, spare_gate, spare_down)


def shards(
    tokens,
    expert_ids,
    gate_levels,
    failed_device,
    replica_holders,
    w_gate,
    w_down,
    spare_gate,
    spare_down,
):
    owners = lax.axis_size("expert")
    tok_count, top_count = expert_ids.shape
    capacity = 2 * tok_count * top_count // owners
    my_index = lax.axis_index("expert").astype(jnp.int32)
    failed_id = failed_device[0]
    holder_row = lax.dynamic_index_in_dim(replica_holders, failed_id, 0, keepdims=False)
    holds = jnp.any(holder_row == my_index).astype(jnp.int32)
    scalars = jnp.stack([my_index, failed_id, holds])
    codes = (expert_ids * LEVELS + gate_levels).T
    all_codes = lax.all_gather(codes, "expert", axis=0)
    all_tokens = lax.all_gather(tokens, "expert", axis=0, tiled=True)
    dense = run_experts(
        scalars, all_codes, all_tokens, w_gate, w_down, spare_gate, spare_down, capacity
    )
    return lax.psum_scatter(dense, "expert", scatter_dimension=0, tiled=True)


def solution(mesh):
    in_specs = (
        P(("group", "expert"), None),
        P(("group", "expert"), None),
        P(("group", "expert"), None),
        P(),
        P(),
        P("expert", None, None),
        P("expert", None, None),
        P("expert", None, None),
        P("expert", None, None),
    )
    out_specs = P(("group", "expert"), None)
    return jax.shard_map(shards, mesh=mesh, in_specs=in_specs, out_specs=out_specs, check_vma=False)
```

```python
import functools
import jax
import jax.numpy as jnp
from jax import lax
from jax.experimental import pallas as pl
from jax.experimental.pallas import tpu as pltpu
from jax.sharding import PartitionSpec as P

LEVELS = 1024


def gated_unit(values):
    return values * jax.nn.sigmoid(1.702 * values)


def expert_kernel(
    scalars,
    codes,
    tokens,
    w_gate,
    w_down,
    spare_gate,
    spare_down,
    out,
    rows_in,
    spare_in,
    hidden,
    spare_hidden,
    rows_out,
    *,
    subs,
    sources,
    capacity,
):
    tok = codes.shape[2]
    part = sources * tok
    rows = sources * capacity
    width = tokens.shape[1]
    tile = 512
    my_id, failed_id, holds = scalars[0], scalars[1], scalars[2]
    serves = my_id != failed_id

    before = (
        lax.broadcasted_iota(jnp.int32, (tok, tok), 0)
        < lax.broadcasted_iota(jnp.int32, (tok, tok), 1)
    ).astype(jnp.bfloat16)
    row_iota = lax.broadcasted_iota(jnp.int32, (rows, tok), 0)

    def picker(code, wanted, live):
        named = ((code // LEVELS) == wanted) & live
        mask = jnp.sum(named.astype(jnp.float32), axis=1)
        level = jnp.sum(jnp.where(named, (code % LEVELS), 0).astype(jnp.float32), axis=1) / LEVELS
        rank = jnp.dot(mask.astype(jnp.bfloat16), before, preferred_element_type=jnp.float32)
        picks, weights = [], None
        for s in range(sources):
            place = jnp.where(mask[s : s + 1] > 0, rank[s : s + 1].astype(jnp.int32) + s * capacity, -1)
            hit = row_iota == place
            scaled = jnp.sum(jnp.where(hit, level[s : s + 1], 0.0), axis=1, keepdims=True)
            weights = scaled if weights is None else weights + scaled
            picks.append(hit.astype(jnp.float32).astype(jnp.bfloat16))
        return jnp.concatenate(picks, axis=1), weights

    picks, weights, spare_weights = [], [], []
    for j in range(subs):
        code = codes[j * sources : (j + 1) * sources]
        pick, weight = picker(code, my_id, serves)
        spare_pick, spare_weight = picker(code, failed_id, holds > 0)
        both = jnp.concatenate([pick, spare_pick], axis=0)
        picks.append(both)
        weights.append(weight)
        spare_weights.append(spare_weight)
        for n in range(0, width, tile):
            got = jnp.dot(
                both, tokens[j * part : (j + 1) * part, n : n + tile], preferred_element_type=jnp.float32
            ).astype(jnp.bfloat16)
            rows_in[j * rows : (j + 1) * rows, n : n + tile] = got[:rows]
            spare_in[j * rows : (j + 1) * rows, n : n + tile] = got[rows:]

    for n in range(0, hidden.shape[1], tile):
        hidden[:, n : n + tile] = gated_unit(
            jnp.dot(rows_in[...], w_gate[0, :, n : n + tile], preferred_element_type=jnp.float32)
        ).astype(jnp.bfloat16)
    for n in range(0, width, tile):
        result = jnp.dot(hidden[...], w_down[0, :, n : n + tile], preferred_element_type=jnp.float32)
        result = result.astype(jnp.bfloat16).astype(jnp.float32)
        for j in range(subs):
            rows_out[j, :rows, n : n + tile] = (result[j * rows : (j + 1) * rows] * weights[j]).astype(
                jnp.bfloat16
            )

    @pl.when(holds > 0)
    def _():
        spare_hidden[...] = gated_unit(
            jnp.dot(spare_in[...], spare_gate[0], preferred_element_type=jnp.float32)
        ).astype(jnp.bfloat16)
        for n in range(0, width, tile):
            result = jnp.dot(
                spare_hidden[...], spare_down[0, :, n : n + tile], preferred_element_type=jnp.float32
            )
            for j in range(subs):
                rows_out[j, rows:, n : n + tile] = (
                    result[j * rows : (j + 1) * rows] * spare_weights[j]
                ).astype(jnp.bfloat16)

    @pl.when(holds <= 0)
    def _():
        rows_out[:, rows:, :] = jnp.zeros((subs, rows, width), jnp.bfloat16)

    for j in range(subs):
        for n in range(0, width, tile):
            out[j * part : (j + 1) * part, n : n + tile] = lax.dot_general(
                picks[j],
                rows_out[j, :, n : n + tile],
                (((0,), (0,)), ((), ())),
                preferred_element_type=jnp.float32,
            ).astype(jnp.bfloat16)


def run_experts(scalars, codes, tokens, w_gate, w_down, spare_gate, spare_down, capacity):
    owners, top, tok = codes.shape
    width, inner, spare = w_gate.shape[1], w_gate.shape[2], spare_gate.shape[2]
    sources = max(1, 128 // capacity)
    subs = 2 if sources * tok <= 512 else 1
    step = subs * sources
    rows = sources * capacity
    whole = lambda a: pl.BlockSpec(a.shape, lambda i: (0, 0, 0), pipeline_mode=pl.Buffered(1))
    return pl.pallas_call(
        functools.partial(expert_kernel, subs=subs, sources=sources, capacity=capacity),
        grid=(owners // step,),
        out_shape=jax.ShapeDtypeStruct((owners * tok, width), jnp.bfloat16),
        in_specs=[
            pl.BlockSpec(memory_space=pltpu.SMEM),
            pl.BlockSpec((step, top, tok), lambda i: (i, 0, 0)),
            pl.BlockSpec((step * tok, width), lambda i: (i, 0)),
            whole(w_gate),
            whole(w_down),
            whole(spare_gate),
            whole(spare_down),
        ],
        out_specs=pl.BlockSpec((step * tok, width), lambda i: (i, 0)),
        scratch_shapes=[
            pltpu.VMEM((subs * rows, width), jnp.bfloat16),
            pltpu.VMEM((subs * rows, width), jnp.bfloat16),
            pltpu.VMEM((subs * rows, inner), jnp.bfloat16),
            pltpu.VMEM((subs * rows, spare), jnp.bfloat16),
            pltpu.VMEM((subs, 2 * rows, width), jnp.bfloat16),
        ],
        compiler_params=pltpu.CompilerParams(vmem_limit_bytes=56 * 1024 * 1024),
        cost_estimate=pl.CostEstimate(
            flops=owners * capacity * 4 * width * (inner + spare),
            bytes_accessed=4 * width * (inner + spare) + 4 * owners * tok * width,
            transcendentals=owners * capacity * inner,
        ),
        name="experts",
    )(scalars, codes, tokens, w_gate, w_down, spare_gate, spare_down)


def group_kernel(
    scalars,
    block0,
    block1,
    block2,
    block3,
    w_gate_hbm,
    w_down_hbm,
    spare_gate_hbm,
    spare_down_hbm,
    keep0,
    keep1,
    send,
    w_gate,
    w_down,
    spare_gate,
    spare_down,
    rows_in,
    spare_in,
    hidden,
    spare_hidden,
    rows_out,
    sems,
    *,
    tok,
    top,
    capacity,
):
    width, inner = w_gate.shape
    tile = 512
    my_id, failed_id, holds = scalars[0], scalars[1], scalars[2]
    copies = []

    def fetch(source, target):
        copy = pltpu.make_async_copy(source, target, sems.at[len(copies)])
        copy.start()
        copies.append(copy)
        return copy

    gate_tiles = [
        fetch(w_gate_hbm.at[0, :, n : n + tile], w_gate.at[:, n : n + tile]) for n in range(0, inner, tile)
    ]
    down_tiles = [
        fetch(w_down_hbm.at[0, :, n : n + tile], w_down.at[:, n : n + tile]) for n in range(0, width, tile)
    ]
    spare_tiles = [fetch(spare_gate_hbm.at[0], spare_gate), fetch(spare_down_hbm.at[0], spare_down)]

    before = (
        lax.broadcasted_iota(jnp.int32, (tok, tok), 0)
        < lax.broadcasted_iota(jnp.int32, (tok, tok), 1)
    ).astype(jnp.float32).astype(jnp.bfloat16)
    row_iota = lax.broadcasted_iota(jnp.int32, (capacity, tok), 0)

    def picker(meta, wanted, live):
        mask = jnp.zeros((8, tok), jnp.float32)
        level = jnp.zeros((8, tok), jnp.float32)
        for k in range(top):
            named = (meta[:, k * tok : (k + 1) * tok] == wanted) & live
            high = meta[:, (top + k) * tok : (top + k + 1) * tok]
            low = meta[:, (2 * top + k) * tok : (2 * top + k + 1) * tok]
            mask = mask + jnp.where(named, 1.0, 0.0)
            level = level + jnp.where(named, (high * 32.0 + low) / LEVELS, 0.0)
        rank = jnp.dot(mask.astype(jnp.bfloat16), before, preferred_element_type=jnp.float32)
        place = jnp.where(mask[:1] > 0, rank[:1].astype(jnp.int32), -1)
        hit = row_iota == place
        weight = jnp.sum(jnp.where(hit, level[:1], 0.0), axis=1, keepdims=True)
        return hit.astype(jnp.float32).astype(jnp.bfloat16), weight

    blocks = (block0, block1, block2, block3)
    picks, weights, spare_weights = [], [], []
    for s, block in enumerate(blocks):
        meta = block[tok : tok + 8, :].astype(jnp.float32)
        pick, weight = picker(meta, my_id.astype(jnp.float32), my_id != failed_id)
        spare_pick, spare_weight = picker(meta, failed_id.astype(jnp.float32), holds > 0)
        both = jnp.concatenate([pick, spare_pick], axis=0)
        picks.append(both)
        weights.append(weight)
        spare_weights.append(spare_weight)
        for n in range(0, width, tile):
            got = jnp.dot(both, block[:tok, n : n + tile], preferred_element_type=jnp.float32).astype(
                jnp.bfloat16
            )
            rows_in[s * capacity : (s + 1) * capacity, n : n + tile] = got[:capacity]
            spare_in[s * capacity : (s + 1) * capacity, n : n + tile] = got[capacity:]

    for i, n in enumerate(range(0, inner, tile)):
        gate_tiles[i].wait()
        hidden[:, n : n + tile] = gated_unit(
            jnp.dot(rows_in[...], w_gate[:, n : n + tile], preferred_element_type=jnp.float32)
        ).astype(jnp.bfloat16)
    for i, n in enumerate(range(0, width, tile)):
        down_tiles[i].wait()
        result = jnp.dot(hidden[...], w_down[:, n : n + tile], preferred_element_type=jnp.float32)
        result = result.astype(jnp.bfloat16).astype(jnp.float32)
        for s in range(len(blocks)):
            rows_out[s, :capacity, n : n + tile] = (
                result[s * capacity : (s + 1) * capacity] * weights[s]
            ).astype(jnp.bfloat16)
    for copy in spare_tiles:
        copy.wait()

    @pl.when(holds > 0)
    def _():
        spare_hidden[...] = gated_unit(
            jnp.dot(spare_in[...], spare_gate[...], preferred_element_type=jnp.float32)
        ).astype(jnp.bfloat16)
        for n in range(0, width, tile):
            result = jnp.dot(
                spare_hidden[...], spare_down[:, n : n + tile], preferred_element_type=jnp.float32
            )
            for s in range(len(blocks)):
                rows_out[s, capacity:, n : n + tile] = (
                    result[s * capacity : (s + 1) * capacity] * spare_weights[s]
                ).astype(jnp.bfloat16)

    @pl.when(holds <= 0)
    def _():
        rows_out[:, capacity:, :] = jnp.zeros((len(blocks), capacity, width), jnp.bfloat16)

    for s, target in enumerate((keep0, keep1, send.at[0], send.at[1])):
        for n in range(0, width, tile):
            target[:, n : n + tile] = lax.dot_general(
                picks[s],
                rows_out[s, :, n : n + tile],
                (((0,), (0,)), ((), ())),
                preferred_element_type=jnp.float32,
            ).astype(jnp.bfloat16)


def run_group(scalars, blocks, w_gate, w_down, spare_gate, spare_down, tok, top, capacity):
    width, inner, spare = w_gate.shape[1], w_gate.shape[2], spare_gate.shape[2]
    rows = len(blocks) * capacity
    vmem = pl.BlockSpec(memory_space=pltpu.VMEM)
    hbm = pl.BlockSpec(memory_space=pl.ANY)
    block = jax.ShapeDtypeStruct((tok, width), jnp.bfloat16)
    return pl.pallas_call(
        functools.partial(group_kernel, tok=tok, top=top, capacity=capacity),
        out_shape=(block, block, jax.ShapeDtypeStruct((2, tok, width), jnp.bfloat16)),
        in_specs=[pl.BlockSpec(memory_space=pltpu.SMEM)] + [vmem] * 4 + [hbm] * 4,
        out_specs=(vmem, vmem, vmem),
        scratch_shapes=[
            pltpu.VMEM((width, inner), jnp.bfloat16),
            pltpu.VMEM((inner, width), jnp.bfloat16),
            pltpu.VMEM((width, spare), jnp.bfloat16),
            pltpu.VMEM((spare, width), jnp.bfloat16),
            pltpu.VMEM((rows, width), jnp.bfloat16),
            pltpu.VMEM((rows, width), jnp.bfloat16),
            pltpu.VMEM((rows, inner), jnp.bfloat16),
            pltpu.VMEM((rows, spare), jnp.bfloat16),
            pltpu.VMEM((len(blocks), 2 * capacity, width), jnp.bfloat16),
            pltpu.SemaphoreType.DMA((inner // 512 + width // 512 + 2,)),
        ],
        compiler_params=pltpu.CompilerParams(vmem_limit_bytes=40 * 1024 * 1024),
        cost_estimate=pl.CostEstimate(
            flops=rows * 4 * width * (inner + spare),
            bytes_accessed=4 * width * (inner + spare) + 4 * len(blocks) * tok * width,
            transcendentals=rows * inner,
        ),
        name="group",
    )(scalars, *blocks, w_gate, w_down, spare_gate, spare_down)


def folded_ring(length):
    return [0] + list(range(1, length, 2)) + list(range(2, length, 2))[::-1]


def by_permutes(scalars, tokens, expert_ids, gate_levels, weights, owners, capacity):
    tok, top = expert_ids.shape
    width = tokens.shape[1]
    order = folded_ring(owners // 4)
    steps = len(order)
    after = {a: order[(i + 1) % steps] for i, a in enumerate(order)}
    round_ring = [(d, after[d // 4] * 4 + d % 4) for d in range(owners)]
    over_y = [(d, d ^ 2) for d in range(owners)]
    over_core = [(d, d ^ 1) for d in range(owners)]
    move = lambda a, pairs: lax.ppermute(a, "expert", pairs)

    meta = jnp.concatenate([expert_ids.T, gate_levels.T >> 5, gate_levels.T & 31], axis=0)
    meta = meta.astype(jnp.bfloat16).reshape(1, 3 * top * tok)
    meta = jnp.pad(meta, ((0, 7), (0, width - 3 * top * tok)))
    held = jnp.concatenate([tokens, meta], axis=0)

    groups = []
    for k in range(steps):
        across = move(held, over_y)
        groups.append((held, across, move(held, over_core), move(across, over_core)))
        if k < steps - 1:
            held = move(held, round_ring)

    f32 = lambda a: a.astype(jnp.float32)
    passing = None
    for k in list(range(1, steps)) + [0]:
        keep0, keep1, send = run_group(scalars, groups[k], *weights, tok, top, capacity)
        got = move(send, over_core)
        far = (f32(keep1) + f32(got[1])).astype(jnp.bfloat16)
        total = f32(keep0) + f32(got[0]) + f32(move(far, over_y))
        if passing is not None:
            total = total + f32(move(passing, round_ring))
        passing = total.astype(jnp.bfloat16)
    return passing


def shards(
    tokens,
    expert_ids,
    gate_levels,
    failed_device,
    replica_holders,
    w_gate,
    w_down,
    spare_gate,
    spare_down,
):
    owners = lax.axis_size("expert")
    tok_count, top_count = expert_ids.shape
    capacity = 2 * tok_count * top_count // owners
    my_index = lax.axis_index("expert").astype(jnp.int32)
    failed_id = failed_device[0]
    holder_row = lax.dynamic_index_in_dim(replica_holders, failed_id, 0, keepdims=False)
    holds = jnp.any(holder_row == my_index).astype(jnp.int32)
    scalars = jnp.stack([my_index, failed_id, holds])
    weights = (w_gate, w_down, spare_gate, spare_down)
    if owners % 4 == 0 and owners <= 32 and 3 * top_count * tok_count <= tokens.shape[1]:
        return by_permutes(scalars, tokens, expert_ids, gate_levels, weights, owners, capacity)
    codes = (expert_ids * LEVELS + gate_levels).T
    all_codes = lax.all_gather(codes, "expert", axis=0)
    all_tokens = lax.all_gather(tokens, "expert", axis=0, tiled=True)
    dense = run_experts(scalars, all_codes, all_tokens, *weights, capacity)
    return lax.psum_scatter(dense, "expert", scatter_dimension=0, tiled=True)


def solution(mesh):
    in_specs = (
        P(("group", "expert"), None),
        P(("group", "expert"), None),
        P(("group", "expert"), None),
        P(),
        P(),
        P("expert", None, None),
        P("expert", None, None),
        P("expert", None, None),
        P("expert", None, None),
    )
    out_specs = P(("group", "expert"), None)
    return jax.shard_map(shards, mesh=mesh, in_specs=in_specs, out_specs=out_specs, check_vma=False)
```

```python
import functools
import jax
import jax.numpy as jnp
from jax import lax
from jax.experimental import pallas as pl
from jax.experimental.pallas import tpu as pltpu
from jax.sharding import PartitionSpec as P

LEVELS = 1024


def gated_unit(values):
    return values * jax.nn.sigmoid(1.702 * values)


def expert_kernel(
    scalars,
    codes,
    tokens,
    w_gate,
    w_down,
    spare_gate,
    spare_down,
    out,
    rows_in,
    spare_in,
    hidden,
    spare_hidden,
    rows_out,
    *,
    subs,
    sources,
    capacity,
):
    tok = codes.shape[2]
    part = sources * tok
    rows = sources * capacity
    width = tokens.shape[1]
    tile = 512
    my_id, failed_id, holds = scalars[0], scalars[1], scalars[2]
    serves = my_id != failed_id

    before = (
        lax.broadcasted_iota(jnp.int32, (tok, tok), 0)
        < lax.broadcasted_iota(jnp.int32, (tok, tok), 1)
    ).astype(jnp.bfloat16)
    row_iota = lax.broadcasted_iota(jnp.int32, (rows, tok), 0)

    def picker(code, wanted, live):
        named = ((code // LEVELS) == wanted) & live
        mask = jnp.sum(named.astype(jnp.float32), axis=1)
        level = jnp.sum(jnp.where(named, (code % LEVELS), 0).astype(jnp.float32), axis=1) / LEVELS
        rank = jnp.dot(mask.astype(jnp.bfloat16), before, preferred_element_type=jnp.float32)
        picks, weights = [], None
        for s in range(sources):
            place = jnp.where(mask[s : s + 1] > 0, rank[s : s + 1].astype(jnp.int32) + s * capacity, -1)
            hit = row_iota == place
            scaled = jnp.sum(jnp.where(hit, level[s : s + 1], 0.0), axis=1, keepdims=True)
            weights = scaled if weights is None else weights + scaled
            picks.append(hit.astype(jnp.float32).astype(jnp.bfloat16))
        return jnp.concatenate(picks, axis=1), weights

    picks, weights, spare_weights = [], [], []
    for j in range(subs):
        code = codes[j * sources : (j + 1) * sources]
        pick, weight = picker(code, my_id, serves)
        spare_pick, spare_weight = picker(code, failed_id, holds > 0)
        both = jnp.concatenate([pick, spare_pick], axis=0)
        picks.append(both)
        weights.append(weight)
        spare_weights.append(spare_weight)
        for n in range(0, width, tile):
            got = jnp.dot(
                both, tokens[j * part : (j + 1) * part, n : n + tile], preferred_element_type=jnp.float32
            ).astype(jnp.bfloat16)
            rows_in[j * rows : (j + 1) * rows, n : n + tile] = got[:rows]
            spare_in[j * rows : (j + 1) * rows, n : n + tile] = got[rows:]

    for n in range(0, hidden.shape[1], tile):
        hidden[:, n : n + tile] = gated_unit(
            jnp.dot(rows_in[...], w_gate[0, :, n : n + tile], preferred_element_type=jnp.float32)
        ).astype(jnp.bfloat16)
    for n in range(0, width, tile):
        result = jnp.dot(hidden[...], w_down[0, :, n : n + tile], preferred_element_type=jnp.float32)
        result = result.astype(jnp.bfloat16).astype(jnp.float32)
        for j in range(subs):
            rows_out[j, :rows, n : n + tile] = (result[j * rows : (j + 1) * rows] * weights[j]).astype(
                jnp.bfloat16
            )

    @pl.when(holds > 0)
    def _():
        spare_hidden[...] = gated_unit(
            jnp.dot(spare_in[...], spare_gate[0], preferred_element_type=jnp.float32)
        ).astype(jnp.bfloat16)
        for n in range(0, width, tile):
            result = jnp.dot(
                spare_hidden[...], spare_down[0, :, n : n + tile], preferred_element_type=jnp.float32
            )
            for j in range(subs):
                rows_out[j, rows:, n : n + tile] = (
                    result[j * rows : (j + 1) * rows] * spare_weights[j]
                ).astype(jnp.bfloat16)

    @pl.when(holds <= 0)
    def _():
        rows_out[:, rows:, :] = jnp.zeros((subs, rows, width), jnp.bfloat16)

    for j in range(subs):
        for n in range(0, width, tile):
            out[j * part : (j + 1) * part, n : n + tile] = lax.dot_general(
                picks[j],
                rows_out[j, :, n : n + tile],
                (((0,), (0,)), ((), ())),
                preferred_element_type=jnp.float32,
            ).astype(jnp.bfloat16)


def run_experts(scalars, codes, tokens, w_gate, w_down, spare_gate, spare_down, capacity):
    owners, top, tok = codes.shape
    width, inner, spare = w_gate.shape[1], w_gate.shape[2], spare_gate.shape[2]
    sources = max(1, 128 // capacity)
    subs = 2 if sources * tok <= 512 else 1
    step = subs * sources
    rows = sources * capacity
    whole = lambda a: pl.BlockSpec(a.shape, lambda i: (0, 0, 0), pipeline_mode=pl.Buffered(1))
    return pl.pallas_call(
        functools.partial(expert_kernel, subs=subs, sources=sources, capacity=capacity),
        grid=(owners // step,),
        out_shape=jax.ShapeDtypeStruct((owners * tok, width), jnp.bfloat16),
        in_specs=[
            pl.BlockSpec(memory_space=pltpu.SMEM),
            pl.BlockSpec((step, top, tok), lambda i: (i, 0, 0)),
            pl.BlockSpec((step * tok, width), lambda i: (i, 0)),
            whole(w_gate),
            whole(w_down),
            whole(spare_gate),
            whole(spare_down),
        ],
        out_specs=pl.BlockSpec((step * tok, width), lambda i: (i, 0)),
        scratch_shapes=[
            pltpu.VMEM((subs * rows, width), jnp.bfloat16),
            pltpu.VMEM((subs * rows, width), jnp.bfloat16),
            pltpu.VMEM((subs * rows, inner), jnp.bfloat16),
            pltpu.VMEM((subs * rows, spare), jnp.bfloat16),
            pltpu.VMEM((subs, 2 * rows, width), jnp.bfloat16),
        ],
        compiler_params=pltpu.CompilerParams(vmem_limit_bytes=56 * 1024 * 1024),
        cost_estimate=pl.CostEstimate(
            flops=owners * capacity * 4 * width * (inner + spare),
            bytes_accessed=4 * width * (inner + spare) + 4 * owners * tok * width,
            transcendentals=owners * capacity * inner,
        ),
        name="experts",
    )(scalars, codes, tokens, w_gate, w_down, spare_gate, spare_down)


def group_kernel(
    scalars,
    block0,
    block1,
    block2,
    block3,
    w_gate_hbm,
    w_down_hbm,
    spare_gate_hbm,
    spare_down_hbm,
    keep0,
    keep1,
    send,
    w_gate,
    w_down,
    spare_gate,
    spare_down,
    rows_in,
    spare_in,
    hidden,
    spare_hidden,
    rows_out,
    sems,
    *,
    tok,
    top,
    capacity,
):
    width, inner = w_gate.shape
    tile = 512
    my_id, failed_id, holds = scalars[0], scalars[1], scalars[2]
    copies = []

    def fetch(source, target):
        copy = pltpu.make_async_copy(source, target, sems.at[len(copies)])
        copy.start()
        copies.append(copy)
        return copy

    gate_tiles = [
        fetch(w_gate_hbm.at[0, :, n : n + tile], w_gate.at[:, n : n + tile]) for n in range(0, inner, tile)
    ]
    down_tiles = [
        fetch(w_down_hbm.at[0, :, n : n + tile], w_down.at[:, n : n + tile]) for n in range(0, width, tile)
    ]
    spare_tiles = [fetch(spare_gate_hbm.at[0], spare_gate), fetch(spare_down_hbm.at[0], spare_down)]

    before = (
        lax.broadcasted_iota(jnp.int32, (tok, tok), 0)
        < lax.broadcasted_iota(jnp.int32, (tok, tok), 1)
    ).astype(jnp.float32).astype(jnp.bfloat16)
    row_iota = lax.broadcasted_iota(jnp.int32, (capacity, tok), 0)

    def picker(meta, wanted, live):
        mask = jnp.zeros((8, tok), jnp.float32)
        level = jnp.zeros((8, tok), jnp.float32)
        for k in range(top):
            named = (meta[:, k * tok : (k + 1) * tok] == wanted) & live
            high = meta[:, (top + k) * tok : (top + k + 1) * tok]
            low = meta[:, (2 * top + k) * tok : (2 * top + k + 1) * tok]
            mask = mask + jnp.where(named, 1.0, 0.0)
            level = level + jnp.where(named, (high * 32.0 + low) / LEVELS, 0.0)
        rank = jnp.dot(mask.astype(jnp.bfloat16), before, preferred_element_type=jnp.float32)
        place = jnp.where(mask[:1] > 0, rank[:1].astype(jnp.int32), -1)
        hit = row_iota == place
        weight = jnp.sum(jnp.where(hit, level[:1], 0.0), axis=1, keepdims=True)
        return hit.astype(jnp.float32).astype(jnp.bfloat16), weight

    blocks = (block0, block1, block2, block3)
    picks, weights, spare_weights = [], [], []
    for s, block in enumerate(blocks):
        meta = block[tok : tok + 8, :].astype(jnp.float32)
        pick, weight = picker(meta, my_id.astype(jnp.float32), my_id != failed_id)
        spare_pick, spare_weight = picker(meta, failed_id.astype(jnp.float32), holds > 0)
        both = jnp.concatenate([pick, spare_pick], axis=0)
        picks.append(both)
        weights.append(weight)
        spare_weights.append(spare_weight)
        for n in range(0, width, tile):
            got = jnp.dot(both, block[:tok, n : n + tile], preferred_element_type=jnp.float32).astype(
                jnp.bfloat16
            )
            rows_in[s * capacity : (s + 1) * capacity, n : n + tile] = got[:capacity]
            spare_in[s * capacity : (s + 1) * capacity, n : n + tile] = got[capacity:]

    for i, n in enumerate(range(0, inner, tile)):
        gate_tiles[i].wait()
        hidden[:, n : n + tile] = gated_unit(
            jnp.dot(rows_in[...], w_gate[:, n : n + tile], preferred_element_type=jnp.float32)
        ).astype(jnp.bfloat16)
    for i, n in enumerate(range(0, width, tile)):
        down_tiles[i].wait()
        result = jnp.dot(hidden[...], w_down[:, n : n + tile], preferred_element_type=jnp.float32)
        result = result.astype(jnp.bfloat16).astype(jnp.float32)
        for s in range(len(blocks)):
            rows_out[s, :capacity, n : n + tile] = (
                result[s * capacity : (s + 1) * capacity] * weights[s]
            ).astype(jnp.bfloat16)
    for copy in spare_tiles:
        copy.wait()

    @pl.when(holds > 0)
    def _():
        spare_hidden[...] = gated_unit(
            jnp.dot(spare_in[...], spare_gate[...], preferred_element_type=jnp.float32)
        ).astype(jnp.bfloat16)
        for n in range(0, width, tile):
            result = jnp.dot(
                spare_hidden[...], spare_down[:, n : n + tile], preferred_element_type=jnp.float32
            )
            for s in range(len(blocks)):
                rows_out[s, capacity:, n : n + tile] = (
                    result[s * capacity : (s + 1) * capacity] * spare_weights[s]
                ).astype(jnp.bfloat16)

    @pl.when(holds <= 0)
    def _():
        rows_out[:, capacity:, :] = jnp.zeros((len(blocks), capacity, width), jnp.bfloat16)

    for s, target in enumerate((keep0, keep1, send.at[0], send.at[1])):
        for n in range(0, width, tile):
            target[:, n : n + tile] = lax.dot_general(
                picks[s],
                rows_out[s, :, n : n + tile],
                (((0,), (0,)), ((), ())),
                preferred_element_type=jnp.float32,
            ).astype(jnp.bfloat16)


def run_group(scalars, blocks, w_gate, w_down, spare_gate, spare_down, tok, top, capacity):
    width, inner, spare = w_gate.shape[1], w_gate.shape[2], spare_gate.shape[2]
    rows = len(blocks) * capacity
    vmem = pl.BlockSpec(memory_space=pltpu.VMEM)
    hbm = pl.BlockSpec(memory_space=pl.ANY)
    block = jax.ShapeDtypeStruct((tok, width), jnp.bfloat16)
    return pl.pallas_call(
        functools.partial(group_kernel, tok=tok, top=top, capacity=capacity),
        out_shape=(block, block, jax.ShapeDtypeStruct((2, tok, width), jnp.bfloat16)),
        in_specs=[pl.BlockSpec(memory_space=pltpu.SMEM)] + [vmem] * 4 + [hbm] * 4,
        out_specs=(vmem, vmem, vmem),
        scratch_shapes=[
            pltpu.VMEM((width, inner), jnp.bfloat16),
            pltpu.VMEM((inner, width), jnp.bfloat16),
            pltpu.VMEM((width, spare), jnp.bfloat16),
            pltpu.VMEM((spare, width), jnp.bfloat16),
            pltpu.VMEM((rows, width), jnp.bfloat16),
            pltpu.VMEM((rows, width), jnp.bfloat16),
            pltpu.VMEM((rows, inner), jnp.bfloat16),
            pltpu.VMEM((rows, spare), jnp.bfloat16),
            pltpu.VMEM((len(blocks), 2 * capacity, width), jnp.bfloat16),
            pltpu.SemaphoreType.DMA((inner // 512 + width // 512 + 2,)),
        ],
        compiler_params=pltpu.CompilerParams(vmem_limit_bytes=60 * 1024 * 1024),
        cost_estimate=pl.CostEstimate(
            flops=1000,
            bytes_accessed=1000,
            transcendentals=0,
        ),
        name="group",
    )(scalars, *blocks, w_gate, w_down, spare_gate, spare_down)


def folded_ring(length):
    return [0] + list(range(1, length, 2)) + list(range(2, length, 2))[::-1]


def by_permutes(scalars, tokens, expert_ids, gate_levels, weights, owners, capacity):
    tok, top = expert_ids.shape
    width = tokens.shape[1]
    order = folded_ring(owners // 4)
    steps = len(order)
    after = {a: order[(i + 1) % steps] for i, a in enumerate(order)}
    round_ring = [(d, after[d // 4] * 4 + d % 4) for d in range(owners)]
    over_y = [(d, d ^ 2) for d in range(owners)]
    over_core = [(d, d ^ 1) for d in range(owners)]
    move = lambda a, pairs: lax.ppermute(a, "expert", pairs)

    meta = jnp.concatenate([expert_ids.T, gate_levels.T >> 5, gate_levels.T & 31], axis=0)
    meta = meta.astype(jnp.bfloat16).reshape(1, 3 * top * tok)
    meta = jnp.pad(meta, ((0, 7), (0, width - 3 * top * tok)))
    held = jnp.concatenate([tokens, meta], axis=0)

    groups = []
    for k in range(steps):
        across = move(held, over_y)
        groups.append((held, across, move(held, over_core), move(across, over_core)))
        if k < steps - 1:
            held = move(held, round_ring)

    f32 = lambda a: a.astype(jnp.float32)
    results = []
    for k in range(steps):
        results.append(run_group(scalars, groups[k], *weights, tok, top, capacity))
        if k < steps - 1:
            later = groups[min(k + 2, steps - 1)][0]
            scalars = lax.optimization_barrier((scalars, results[-1][0], later))[0]
    passing = None
    for k in list(range(1, steps)) + [0]:
        keep0, keep1, send = results[k]
        got = move(send, over_core)
        far = (f32(keep1) + f32(got[1])).astype(jnp.bfloat16)
        total = f32(keep0) + f32(got[0]) + f32(move(far, over_y))
        if passing is not None:
            total = total + f32(move(passing, round_ring))
        passing = total.astype(jnp.bfloat16)
    return passing


def shards(
    tokens,
    expert_ids,
    gate_levels,
    failed_device,
    replica_holders,
    w_gate,
    w_down,
    spare_gate,
    spare_down,
):
    owners = lax.axis_size("expert")
    tok_count, top_count = expert_ids.shape
    capacity = 2 * tok_count * top_count // owners
    my_index = lax.axis_index("expert").astype(jnp.int32)
    failed_id = failed_device[0]
    holder_row = lax.dynamic_index_in_dim(replica_holders, failed_id, 0, keepdims=False)
    holds = jnp.any(holder_row == my_index).astype(jnp.int32)
    scalars = jnp.stack([my_index, failed_id, holds])
    weights = (w_gate, w_down, spare_gate, spare_down)
    if owners % 4 == 0 and owners <= 32 and 3 * top_count * tok_count <= tokens.shape[1]:
        return by_permutes(scalars, tokens, expert_ids, gate_levels, weights, owners, capacity)
    codes = (expert_ids * LEVELS + gate_levels).T
    all_codes = lax.all_gather(codes, "expert", axis=0)
    all_tokens = lax.all_gather(tokens, "expert", axis=0, tiled=True)
    dense = run_experts(scalars, all_codes, all_tokens, *weights, capacity)
    return lax.psum_scatter(dense, "expert", scatter_dimension=0, tiled=True)


def solution(mesh):
    in_specs = (
        P(("group", "expert"), None),
        P(("group", "expert"), None),
        P(("group", "expert"), None),
        P(),
        P(),
        P("expert", None, None),
        P("expert", None, None),
        P("expert", None, None),
        P("expert", None, None),
    )
    out_specs = P(("group", "expert"), None)
    return jax.shard_map(shards, mesh=mesh, in_specs=in_specs, out_specs=out_specs, check_vma=False)
```

```python
import functools
import jax
import jax.numpy as jnp
from jax import lax
from jax.experimental import pallas as pl
from jax.experimental.pallas import tpu as pltpu
from jax.sharding import PartitionSpec as P

LEVELS = 1024


def gated_unit(values):
    return values * jax.nn.sigmoid(1.702 * values)


def expert_kernel(
    scalars,
    codes,
    tokens,
    w_gate,
    w_down,
    spare_gate,
    spare_down,
    out,
    rows_in,
    spare_in,
    hidden,
    spare_hidden,
    rows_out,
    *,
    subs,
    sources,
    capacity,
):
    tok = codes.shape[2]
    part = sources * tok
    rows = sources * capacity
    width = tokens.shape[1]
    tile = 512
    my_id, failed_id, holds = scalars[0], scalars[1], scalars[2]
    serves = my_id != failed_id

    before = (
        lax.broadcasted_iota(jnp.int32, (tok, tok), 0)
        < lax.broadcasted_iota(jnp.int32, (tok, tok), 1)
    ).astype(jnp.bfloat16)
    row_iota = lax.broadcasted_iota(jnp.int32, (rows, tok), 0)

    def picker(code, wanted, live):
        named = ((code // LEVELS) == wanted) & live
        mask = jnp.sum(named.astype(jnp.float32), axis=1)
        level = jnp.sum(jnp.where(named, (code % LEVELS), 0).astype(jnp.float32), axis=1) / LEVELS
        rank = jnp.dot(mask.astype(jnp.bfloat16), before, preferred_element_type=jnp.float32)
        picks, weights = [], None
        for s in range(sources):
            place = jnp.where(mask[s : s + 1] > 0, rank[s : s + 1].astype(jnp.int32) + s * capacity, -1)
            hit = row_iota == place
            scaled = jnp.sum(jnp.where(hit, level[s : s + 1], 0.0), axis=1, keepdims=True)
            weights = scaled if weights is None else weights + scaled
            picks.append(hit.astype(jnp.float32).astype(jnp.bfloat16))
        return jnp.concatenate(picks, axis=1), weights

    picks, weights, spare_weights = [], [], []
    for j in range(subs):
        code = codes[j * sources : (j + 1) * sources]
        pick, weight = picker(code, my_id, serves)
        spare_pick, spare_weight = picker(code, failed_id, holds > 0)
        both = jnp.concatenate([pick, spare_pick], axis=0)
        picks.append(both)
        weights.append(weight)
        spare_weights.append(spare_weight)
        for n in range(0, width, tile):
            got = jnp.dot(
                both, tokens[j * part : (j + 1) * part, n : n + tile], preferred_element_type=jnp.float32
            ).astype(jnp.bfloat16)
            rows_in[j * rows : (j + 1) * rows, n : n + tile] = got[:rows]
            spare_in[j * rows : (j + 1) * rows, n : n + tile] = got[rows:]

    for n in range(0, hidden.shape[1], tile):
        hidden[:, n : n + tile] = gated_unit(
            jnp.dot(rows_in[...], w_gate[0, :, n : n + tile], preferred_element_type=jnp.float32)
        ).astype(jnp.bfloat16)
    for n in range(0, width, tile):
        result = jnp.dot(hidden[...], w_down[0, :, n : n + tile], preferred_element_type=jnp.float32)
        result = result.astype(jnp.bfloat16).astype(jnp.float32)
        for j in range(subs):
            rows_out[j, :rows, n : n + tile] = (result[j * rows : (j + 1) * rows] * weights[j]).astype(
                jnp.bfloat16
            )

    @pl.when(holds > 0)
    def _():
        spare_hidden[...] = gated_unit(
            jnp.dot(spare_in[...], spare_gate[0], preferred_element_type=jnp.float32)
        ).astype(jnp.bfloat16)
        for n in range(0, width, tile):
            result = jnp.dot(
                spare_hidden[...], spare_down[0, :, n : n + tile], preferred_element_type=jnp.float32
            )
            for j in range(subs):
                rows_out[j, rows:, n : n + tile] = (
                    result[j * rows : (j + 1) * rows] * spare_weights[j]
                ).astype(jnp.bfloat16)

    @pl.when(holds <= 0)
    def _():
        rows_out[:, rows:, :] = jnp.zeros((subs, rows, width), jnp.bfloat16)

    for j in range(subs):
        for n in range(0, width, tile):
            out[j * part : (j + 1) * part, n : n + tile] = lax.dot_general(
                picks[j],
                rows_out[j, :, n : n + tile],
                (((0,), (0,)), ((), ())),
                preferred_element_type=jnp.float32,
            ).astype(jnp.bfloat16)


def run_experts(scalars, codes, tokens, w_gate, w_down, spare_gate, spare_down, capacity):
    owners, top, tok = codes.shape
    width, inner, spare = w_gate.shape[1], w_gate.shape[2], spare_gate.shape[2]
    sources = max(1, 128 // capacity)
    subs = 2 if sources * tok <= 512 else 1
    step = subs * sources
    rows = sources * capacity
    whole = lambda a: pl.BlockSpec(a.shape, lambda i: (0, 0, 0), pipeline_mode=pl.Buffered(1))
    return pl.pallas_call(
        functools.partial(expert_kernel, subs=subs, sources=sources, capacity=capacity),
        grid=(owners // step,),
        out_shape=jax.ShapeDtypeStruct((owners * tok, width), jnp.bfloat16),
        in_specs=[
            pl.BlockSpec(memory_space=pltpu.SMEM),
            pl.BlockSpec((step, top, tok), lambda i: (i, 0, 0)),
            pl.BlockSpec((step * tok, width), lambda i: (i, 0)),
            whole(w_gate),
            whole(w_down),
            whole(spare_gate),
            whole(spare_down),
        ],
        out_specs=pl.BlockSpec((step * tok, width), lambda i: (i, 0)),
        scratch_shapes=[
            pltpu.VMEM((subs * rows, width), jnp.bfloat16),
            pltpu.VMEM((subs * rows, width), jnp.bfloat16),
            pltpu.VMEM((subs * rows, inner), jnp.bfloat16),
            pltpu.VMEM((subs * rows, spare), jnp.bfloat16),
            pltpu.VMEM((subs, 2 * rows, width), jnp.bfloat16),
        ],
        compiler_params=pltpu.CompilerParams(vmem_limit_bytes=56 * 1024 * 1024),
        cost_estimate=pl.CostEstimate(
            flops=owners * capacity * 4 * width * (inner + spare),
            bytes_accessed=4 * width * (inner + spare) + 4 * owners * tok * width,
            transcendentals=owners * capacity * inner,
        ),
        name="experts",
    )(scalars, codes, tokens, w_gate, w_down, spare_gate, spare_down)


def group_kernel(
    failed,
    holders,
    block0,
    block1,
    block2,
    block3,
    w_gate,
    w_down,
    spare_gate,
    spare_down,
    *rest,
    tok,
    top,
    capacity,
):
    keep0, keep1, send, rows_in, spare_in, hidden, spare_hidden, rows_out = rest[-8:]
    width, inner = w_gate.shape[1:]
    tile = 512
    my_id, failed_id = lax.axis_index("expert"), failed[0]
    holds = holders[failed_id, 0] == my_id
    for j in range(1, holders.shape[1]):
        holds = holds | (holders[failed_id, j] == my_id)

    before = (
        lax.broadcasted_iota(jnp.int32, (tok, tok), 0)
        < lax.broadcasted_iota(jnp.int32, (tok, tok), 1)
    ).astype(jnp.float32).astype(jnp.bfloat16)
    row_iota = lax.broadcasted_iota(jnp.int32, (capacity, tok), 0)

    def picker(meta, wanted, live):
        mask = jnp.zeros((8, tok), jnp.float32)
        level = jnp.zeros((8, tok), jnp.float32)
        for k in range(top):
            named = (meta[:, k * tok : (k + 1) * tok] == wanted.astype(jnp.float32)) & live
            high = meta[:, (top + k) * tok : (top + k + 1) * tok]
            low = meta[:, (2 * top + k) * tok : (2 * top + k + 1) * tok]
            mask = mask + jnp.where(named, 1.0, 0.0)
            level = level + jnp.where(named, (high * 32.0 + low) / LEVELS, 0.0)
        rank = jnp.dot(mask.astype(jnp.bfloat16), before, preferred_element_type=jnp.float32)
        place = jnp.where(mask[:1] > 0, rank[:1].astype(jnp.int32), -1)
        hit = row_iota == place
        weight = jnp.sum(jnp.where(hit, level[:1], 0.0), axis=1, keepdims=True)
        return hit.astype(jnp.float32).astype(jnp.bfloat16), weight

    blocks = (block0, block1, block2, block3)
    picks, weights, spare_weights = [], [], []
    for s, block in enumerate(blocks):
        meta = block[tok : tok + 8, :].astype(jnp.float32)
        pick, weight = picker(meta, my_id, my_id != failed_id)
        spare_pick, spare_weight = picker(meta, failed_id, holds)
        both = jnp.concatenate([pick, spare_pick], axis=0)
        picks.append(both)
        weights.append(weight)
        spare_weights.append(spare_weight)
        for n in range(0, width, tile):
            got = jnp.dot(both, block[:tok, n : n + tile], preferred_element_type=jnp.float32).astype(
                jnp.bfloat16
            )
            rows_in[s * capacity : (s + 1) * capacity, n : n + tile] = got[:capacity]
            spare_in[s * capacity : (s + 1) * capacity, n : n + tile] = got[capacity:]

    for n in range(0, inner, tile):
        hidden[:, n : n + tile] = gated_unit(
            jnp.dot(rows_in[...], w_gate[0, :, n : n + tile], preferred_element_type=jnp.float32)
        ).astype(jnp.bfloat16)
    for n in range(0, width, tile):
        result = jnp.dot(hidden[...], w_down[0, :, n : n + tile], preferred_element_type=jnp.float32)
        result = result.astype(jnp.bfloat16).astype(jnp.float32)
        for s in range(len(blocks)):
            rows_out[s, :capacity, n : n + tile] = (
                result[s * capacity : (s + 1) * capacity] * weights[s]
            ).astype(jnp.bfloat16)

    @pl.when(holds)
    def _():
        spare_hidden[...] = gated_unit(
            jnp.dot(spare_in[...], spare_gate[0], preferred_element_type=jnp.float32)
        ).astype(jnp.bfloat16)
        for n in range(0, width, tile):
            result = jnp.dot(
                spare_hidden[...], spare_down[0, :, n : n + tile], preferred_element_type=jnp.float32
            )
            for s in range(len(blocks)):
                rows_out[s, capacity:, n : n + tile] = (
                    result[s * capacity : (s + 1) * capacity] * spare_weights[s]
                ).astype(jnp.bfloat16)

    @pl.when(jnp.logical_not(holds))
    def _():
        rows_out[:, capacity:, :] = jnp.zeros((len(blocks), capacity, width), jnp.bfloat16)

    for s, target in enumerate((keep0, keep1, send.at[0], send.at[1])):
        for n in range(0, width, tile):
            target[:, n : n + tile] = lax.dot_general(
                picks[s],
                rows_out[s, :, n : n + tile],
                (((0,), (0,)), ((), ())),
                preferred_element_type=jnp.float32,
            ).astype(jnp.bfloat16)


def run_group(failed, holders, blocks, weights, earlier, tok, top, capacity):
    width, inner, spare = weights[0].shape[1], weights[0].shape[2], weights[2].shape[2]
    rows = len(blocks) * capacity
    vmem = pl.BlockSpec(memory_space=pltpu.VMEM)
    smem = pl.BlockSpec(memory_space=pltpu.SMEM)
    block = jax.ShapeDtypeStruct((tok, width), jnp.bfloat16)
    return pl.pallas_call(
        functools.partial(group_kernel, tok=tok, top=top, capacity=capacity),
        out_shape=(block, block, jax.ShapeDtypeStruct((2, tok, width), jnp.bfloat16)),
        in_specs=[smem, smem] + [vmem] * 8 + [pl.BlockSpec(memory_space=pl.ANY)] * len(earlier),
        out_specs=(vmem, vmem, vmem),
        scratch_shapes=[
            pltpu.VMEM((rows, width), jnp.bfloat16),
            pltpu.VMEM((rows, width), jnp.bfloat16),
            pltpu.VMEM((rows, inner), jnp.bfloat16),
            pltpu.VMEM((rows, spare), jnp.bfloat16),
            pltpu.VMEM((len(blocks), 2 * capacity, width), jnp.bfloat16),
        ],
        compiler_params=pltpu.CompilerParams(vmem_limit_bytes=30 * 1024 * 1024),
        cost_estimate=pl.CostEstimate(
            flops=rows * 4 * width * (inner + spare),
            bytes_accessed=4 * width * (inner + spare) + 4 * len(blocks) * tok * width,
            transcendentals=rows * inner,
        ),
        name="group",
    )(failed, holders, *blocks, *weights, *earlier)


def nothing(*refs):
    pass


def come_after(value, *others, flops=0):
    return pl.pallas_call(
        nothing,
        out_shape=jax.ShapeDtypeStruct(value.shape, value.dtype),
        in_specs=[pl.BlockSpec(memory_space=pl.ANY)] * (1 + len(others)),
        out_specs=pl.BlockSpec(memory_space=pl.ANY),
        input_output_aliases={0: 0},
        cost_estimate=pl.CostEstimate(flops=flops, bytes_accessed=0, transcendentals=0),
        name="after",
    )(value, *others)


def folded_ring(length):
    return [0] + list(range(1, length, 2)) + list(range(2, length, 2))[::-1]


def by_permutes(failed, holders, tokens, expert_ids, gate_levels, weights, owners, capacity):
    tok, top = expert_ids.shape
    width = tokens.shape[1]
    order = folded_ring(owners // 4)
    steps = len(order)
    after = {a: order[(i + 1) % steps] for i, a in enumerate(order)}
    round_ring = [(d, after[d // 4] * 4 + d % 4) for d in range(owners)]
    over_y = [(d, d ^ 2) for d in range(owners)]
    over_core = [(d, d ^ 1) for d in range(owners)]
    move = lambda a, pairs: lax.ppermute(a, "expert", pairs)

    meta = jnp.concatenate([expert_ids.T, gate_levels.T >> 5, gate_levels.T & 31], axis=0)
    meta = meta.astype(jnp.bfloat16).reshape(1, 3 * top * tok)
    meta = jnp.pad(meta, ((0, 7), (0, width - 3 * top * tok)))
    held = [come_after(jnp.concatenate([tokens, meta], axis=0), flops=8 * 10**9)]
    across, results = [], []
    for k in range(steps):
        if k > 0:
            held.append(move(held[-1], round_ring))
            if k > 1:
                held[k] = come_after(held[k], results[k - 2][0])
        across.append(move(held[k], over_y))
        blocks = (held[k], across[k], move(held[k], over_core), move(across[k], over_core))
        earlier = [results[-1][0]] if results else []
        results.append(run_group(failed, holders, blocks, weights, earlier, tok, top, capacity))

    f32 = lambda a: a.astype(jnp.float32)
    passing = None
    for k in list(range(1, steps)) + [0]:
        keep0, keep1, send = results[k]
        if k < steps - 1:
            send = come_after(send, across[k + 1], held[min(k + 2, steps - 1)])
        got = move(send, over_core)
        far = (f32(keep1) + f32(got[1])).astype(jnp.bfloat16)
        total = f32(keep0) + f32(got[0]) + f32(move(far, over_y))
        if passing is not None:
            total = total + f32(move(passing, round_ring))
        passing = total.astype(jnp.bfloat16)
    return passing


def shards(
    tokens,
    expert_ids,
    gate_levels,
    failed_device,
    replica_holders,
    w_gate,
    w_down,
    spare_gate,
    spare_down,
):
    owners = lax.axis_size("expert")
    tok_count, top_count = expert_ids.shape
    capacity = 2 * tok_count * top_count // owners
    my_index = lax.axis_index("expert").astype(jnp.int32)
    failed_id = failed_device[0]
    holder_row = lax.dynamic_index_in_dim(replica_holders, failed_id, 0, keepdims=False)
    holds = jnp.any(holder_row == my_index).astype(jnp.int32)
    scalars = jnp.stack([my_index, failed_id, holds])
    weights = (w_gate, w_down, spare_gate, spare_down)
    if owners % 4 == 0 and owners <= 32 and 3 * top_count * tok_count <= tokens.shape[1]:
        return by_permutes(
            failed_device, replica_holders, tokens, expert_ids, gate_levels, weights, owners, capacity
        )
    codes = (expert_ids * LEVELS + gate_levels).T
    all_codes = lax.all_gather(codes, "expert", axis=0)
    all_tokens = lax.all_gather(tokens, "expert", axis=0, tiled=True)
    dense = run_experts(scalars, all_codes, all_tokens, *weights, capacity)
    return lax.psum_scatter(dense, "expert", scatter_dimension=0, tiled=True)


def solution(mesh):
    in_specs = (
        P(("group", "expert"), None),
        P(("group", "expert"), None),
        P(("group", "expert"), None),
        P(),
        P(),
        P("expert", None, None),
        P("expert", None, None),
        P("expert", None, None),
        P("expert", None, None),
    )
    out_specs = P(("group", "expert"), None)
    return jax.shard_map(shards, mesh=mesh, in_specs=in_specs, out_specs=out_specs, check_vma=False)
```

```python
import functools
import jax
import jax.numpy as jnp
from jax import lax
from jax.experimental import pallas as pl
from jax.experimental.pallas import tpu as pltpu
from jax.sharding import PartitionSpec as P

LEVELS = 1024
VMEM_GRANT = 65200 * 1024


def gated_unit(values):
    return values * (0.5 + 0.5 * jnp.tanh(0.851 * values))


def expert_kernel(
    scalars,
    codes,
    tokens,
    w_gate,
    w_down,
    spare_gate,
    spare_down,
    out,
    rows_in,
    spare_in,
    hidden,
    spare_hidden,
    rows_out,
    *,
    subs,
    sources,
    capacity,
):
    tok = codes.shape[2]
    part = sources * tok
    rows = sources * capacity
    width = tokens.shape[1]
    tile = 512
    my_id, failed_id, holds = scalars[0], scalars[1], scalars[2]
    serves = my_id != failed_id

    before = (
        lax.broadcasted_iota(jnp.int32, (tok, tok), 0)
        < lax.broadcasted_iota(jnp.int32, (tok, tok), 1)
    ).astype(jnp.bfloat16)
    row_iota = lax.broadcasted_iota(jnp.int32, (rows, tok), 0)

    def picker(code, wanted, live):
        named = ((code // LEVELS) == wanted) & live
        mask = jnp.sum(named.astype(jnp.float32), axis=1)
        level = jnp.sum(jnp.where(named, (code % LEVELS), 0).astype(jnp.float32), axis=1) / LEVELS
        rank = jnp.dot(mask.astype(jnp.bfloat16), before, preferred_element_type=jnp.float32)
        picks, weights = [], None
        for s in range(sources):
            place = jnp.where(mask[s : s + 1] > 0, rank[s : s + 1].astype(jnp.int32) + s * capacity, -1)
            hit = row_iota == place
            scaled = jnp.sum(jnp.where(hit, level[s : s + 1], 0.0), axis=1, keepdims=True)
            weights = scaled if weights is None else weights + scaled
            picks.append(hit.astype(jnp.float32).astype(jnp.bfloat16))
        return jnp.concatenate(picks, axis=1), weights

    picks, weights, spare_weights = [], [], []
    for j in range(subs):
        code = codes[j * sources : (j + 1) * sources]
        pick, weight = picker(code, my_id, serves)
        spare_pick, spare_weight = picker(code, failed_id, holds > 0)
        both = jnp.concatenate([pick, spare_pick], axis=0)
        picks.append(both)
        weights.append(weight)
        spare_weights.append(spare_weight)
        for n in range(0, width, tile):
            got = jnp.dot(
                both, tokens[j * part : (j + 1) * part, n : n + tile], preferred_element_type=jnp.float32
            ).astype(jnp.bfloat16)
            rows_in[j * rows : (j + 1) * rows, n : n + tile] = got[:rows]
            spare_in[j * rows : (j + 1) * rows, n : n + tile] = got[rows:]

    for n in range(0, hidden.shape[1], tile):
        hidden[:, n : n + tile] = gated_unit(
            jnp.dot(rows_in[...], w_gate[0, :, n : n + tile], preferred_element_type=jnp.float32)
        ).astype(jnp.bfloat16)
    for n in range(0, width, tile):
        result = jnp.dot(hidden[...], w_down[0, :, n : n + tile], preferred_element_type=jnp.float32)
        result = result.astype(jnp.bfloat16).astype(jnp.float32)
        for j in range(subs):
            rows_out[j, :rows, n : n + tile] = (result[j * rows : (j + 1) * rows] * weights[j]).astype(
                jnp.bfloat16
            )

    @pl.when(holds > 0)
    def _():
        spare_hidden[...] = gated_unit(
            jnp.dot(spare_in[...], spare_gate[0], preferred_element_type=jnp.float32)
        ).astype(jnp.bfloat16)
        for n in range(0, width, tile):
            result = jnp.dot(
                spare_hidden[...], spare_down[0, :, n : n + tile], preferred_element_type=jnp.float32
            )
            for j in range(subs):
                rows_out[j, rows:, n : n + tile] = (
                    result[j * rows : (j + 1) * rows] * spare_weights[j]
                ).astype(jnp.bfloat16)

    @pl.when(holds <= 0)
    def _():
        rows_out[:, rows:, :] = jnp.zeros((subs, rows, width), jnp.bfloat16)

    for j in range(subs):
        for n in range(0, width, tile):
            out[j * part : (j + 1) * part, n : n + tile] = lax.dot_general(
                picks[j],
                rows_out[j, :, n : n + tile],
                (((0,), (0,)), ((), ())),
                preferred_element_type=jnp.float32,
            ).astype(jnp.bfloat16)


def run_experts(scalars, codes, tokens, w_gate, w_down, spare_gate, spare_down, capacity):
    owners, top, tok = codes.shape
    width, inner, spare = w_gate.shape[1], w_gate.shape[2], spare_gate.shape[2]
    sources = max(1, 128 // capacity)
    subs = 2 if sources * tok <= 512 else 1
    step = subs * sources
    rows = sources * capacity
    whole = lambda a: pl.BlockSpec(a.shape, lambda i: (0, 0, 0), pipeline_mode=pl.Buffered(1))
    return pl.pallas_call(
        functools.partial(expert_kernel, subs=subs, sources=sources, capacity=capacity),
        grid=(owners // step,),
        out_shape=jax.ShapeDtypeStruct((owners * tok, width), jnp.bfloat16),
        in_specs=[
            pl.BlockSpec(memory_space=pltpu.SMEM),
            pl.BlockSpec((step, top, tok), lambda i: (i, 0, 0)),
            pl.BlockSpec((step * tok, width), lambda i: (i, 0)),
            whole(w_gate),
            whole(w_down),
            whole(spare_gate),
            whole(spare_down),
        ],
        out_specs=pl.BlockSpec((step * tok, width), lambda i: (i, 0)),
        scratch_shapes=[
            pltpu.VMEM((subs * rows, width), jnp.bfloat16),
            pltpu.VMEM((subs * rows, width), jnp.bfloat16),
            pltpu.VMEM((subs * rows, inner), jnp.bfloat16),
            pltpu.VMEM((subs * rows, spare), jnp.bfloat16),
            pltpu.VMEM((subs, 2 * rows, width), jnp.bfloat16),
        ],
        compiler_params=pltpu.CompilerParams(vmem_limit_bytes=56 * 1024 * 1024),
        cost_estimate=pl.CostEstimate(
            flops=owners * capacity * 4 * width * (inner + spare),
            bytes_accessed=4 * width * (inner + spare) + 4 * owners * tok * width,
            transcendentals=owners * capacity * inner,
        ),
        name="experts",
    )(scalars, codes, tokens, w_gate, w_down, spare_gate, spare_down)


def group_kernel(failed, holders, *refs, others, tok, top, capacity):
    blocks, weights_hbm, refs = refs[:4], refs[4:8], refs[8 + others :]
    keep0, keep1, send, held, w_gate, w_down, spare_gate, spare_down = refs[:8]
    rows_in, spare_in, hidden, spare_hidden, rows_out, dense, fetched, stored = refs[8:]
    width, inner = w_gate.shape
    tile = 512
    my_id, failed_id = lax.axis_index("expert"), failed[0]
    holds = holders[failed_id, 0] == my_id
    for j in range(1, holders.shape[1]):
        holds = holds | (holders[failed_id, j] == my_id)
    copies = []

    def fetch(source, target):
        copy = pltpu.make_async_copy(source, target, fetched.at[len(copies)])
        copy.start()
        copies.append(copy)
        return copy

    gate_hbm, down_hbm, spare_gate_hbm, spare_down_hbm = weights_hbm
    block_copies = [fetch(block, held.at[s]) for s, block in enumerate(blocks)]
    gate_copies = [
        fetch(gate_hbm.at[0, :, n : n + tile], w_gate.at[:, n : n + tile]) for n in range(0, inner, tile)
    ]
    spare_copies = [fetch(spare_gate_hbm.at[0], spare_gate), fetch(spare_down_hbm.at[0], spare_down)]
    down_copies = [
        fetch(down_hbm.at[0, :, n : n + tile], w_down.at[:, n : n + tile]) for n in range(0, width, tile)
    ]

    before = (
        lax.broadcasted_iota(jnp.int32, (tok, tok), 0)
        < lax.broadcasted_iota(jnp.int32, (tok, tok), 1)
    ).astype(jnp.float32).astype(jnp.bfloat16)
    row_iota = lax.broadcasted_iota(jnp.int32, (capacity, tok), 0)

    def picker(meta, wanted, live):
        mask = jnp.zeros((8, tok), jnp.float32)
        level = jnp.zeros((8, tok), jnp.float32)
        for k in range(top):
            named = (meta[:, k * tok : (k + 1) * tok] == wanted.astype(jnp.float32)) & live
            high = meta[:, (top + k) * tok : (top + k + 1) * tok]
            low = meta[:, (2 * top + k) * tok : (2 * top + k + 1) * tok]
            mask = mask + jnp.where(named, 1.0, 0.0)
            level = level + jnp.where(named, (high * 32.0 + low) / LEVELS, 0.0)
        rank = jnp.dot(mask.astype(jnp.bfloat16), before, preferred_element_type=jnp.float32)
        place = jnp.where(mask[:1] > 0, rank[:1].astype(jnp.int32), -1)
        hit = row_iota == place
        weight = jnp.sum(jnp.where(hit, level[:1], 0.0), axis=1, keepdims=True)
        return hit.astype(jnp.float32).astype(jnp.bfloat16), weight

    picks, weights, spare_weights = [], [], []
    for s in range(len(blocks)):
        block_copies[s].wait()
        meta = held[s, tok : tok + 8, :].astype(jnp.float32)
        pick, weight = picker(meta, my_id, my_id != failed_id)
        spare_pick, spare_weight = picker(meta, failed_id, holds)
        both = jnp.concatenate([pick, spare_pick], axis=0)
        picks.append(both)
        weights.append(weight)
        spare_weights.append(spare_weight)
        for n in range(0, width, tile):
            got = jnp.dot(both, held[s, :tok, n : n + tile], preferred_element_type=jnp.float32).astype(
                jnp.bfloat16
            )
            rows_in[s * capacity : (s + 1) * capacity, n : n + tile] = got[:capacity]
            spare_in[s * capacity : (s + 1) * capacity, n : n + tile] = got[capacity:]

    for i, n in enumerate(range(0, inner, tile)):
        gate_copies[i].wait()
        hidden[:, n : n + tile] = gated_unit(
            jnp.dot(rows_in[...], w_gate[:, n : n + tile], preferred_element_type=jnp.float32)
        ).astype(jnp.bfloat16)
    for copy in spare_copies:
        copy.wait()

    @pl.when(holds)
    def _():
        spare_hidden[...] = gated_unit(
            jnp.dot(spare_in[...], spare_gate[...], preferred_element_type=jnp.float32)
        ).astype(jnp.bfloat16)
        for n in range(0, width, tile):
            result = jnp.dot(
                spare_hidden[...], spare_down[:, n : n + tile], preferred_element_type=jnp.float32
            )
            for s in range(len(blocks)):
                rows_out[s, capacity:, n : n + tile] = (
                    result[s * capacity : (s + 1) * capacity] * spare_weights[s]
                ).astype(jnp.bfloat16)

    @pl.when(jnp.logical_not(holds))
    def _():
        rows_out[:, capacity:, :] = jnp.zeros((len(blocks), capacity, width), jnp.bfloat16)

    for i, n in enumerate(range(0, width, tile)):
        down_copies[i].wait()
        result = jnp.dot(hidden[...], w_down[:, n : n + tile], preferred_element_type=jnp.float32)
        result = result.astype(jnp.bfloat16).astype(jnp.float32)
        for s in range(len(blocks)):
            rows_out[s, :capacity, n : n + tile] = (
                result[s * capacity : (s + 1) * capacity] * weights[s]
            ).astype(jnp.bfloat16)
            dense[s, :, n : n + tile] = lax.dot_general(
                picks[s],
                rows_out[s, :, n : n + tile],
                (((0,), (0,)), ((), ())),
                preferred_element_type=jnp.float32,
            ).astype(jnp.bfloat16)
    stores = [
        pltpu.make_async_copy(dense.at[s], target, stored.at[s])
        for s, target in enumerate((keep0, keep1, send.at[0], send.at[1]))
    ]
    for copy in stores:
        copy.start()
    for copy in stores:
        copy.wait()


def run_group(failed, holders, blocks, weights, earlier, tok, top, capacity):
    width, inner, spare = weights[0].shape[1], weights[0].shape[2], weights[2].shape[2]
    count = len(blocks)
    rows = count * capacity
    hbm = pl.BlockSpec(memory_space=pl.ANY)
    smem = pl.BlockSpec(memory_space=pltpu.SMEM)
    block = pltpu.HBM((tok, width), jnp.bfloat16)
    return pl.pallas_call(
        functools.partial(
            group_kernel, others=len(earlier), tok=tok, top=top, capacity=capacity
        ),
        out_shape=(block, block, pltpu.HBM((2, tok, width), jnp.bfloat16)),
        in_specs=[smem, smem] + [hbm] * (count + 4 + len(earlier)),
        out_specs=(hbm, hbm, hbm),
        scratch_shapes=[
            pltpu.VMEM((count, *blocks[0].shape), jnp.bfloat16),
            pltpu.VMEM((width, inner), jnp.bfloat16),
            pltpu.VMEM((inner, width), jnp.bfloat16),
            pltpu.VMEM((width, spare), jnp.bfloat16),
            pltpu.VMEM((spare, width), jnp.bfloat16),
            pltpu.VMEM((rows, width), jnp.bfloat16),
            pltpu.VMEM((rows, width), jnp.bfloat16),
            pltpu.VMEM((rows, inner), jnp.bfloat16),
            pltpu.VMEM((rows, spare), jnp.bfloat16),
            pltpu.VMEM((count, 2 * capacity, width), jnp.bfloat16),
            pltpu.VMEM((count, tok, width), jnp.bfloat16),
            pltpu.SemaphoreType.DMA((count + inner // 512 + width // 512 + 2,)),
            pltpu.SemaphoreType.DMA((count,)),
        ],
        compiler_params=pltpu.CompilerParams(vmem_limit_bytes=VMEM_GRANT),
        cost_estimate=pl.CostEstimate(
            flops=rows * 4 * width * (inner + spare),
            bytes_accessed=4 * width * (inner + spare) + 4 * count * tok * width,
            transcendentals=rows * inner,
        ),
        name="group",
    )(failed, holders, *map(in_hbm, (*blocks, *weights, *earlier)))


def in_hbm(array):
    return pltpu.with_memory_space_constraint(array, pltpu.HBM)


def nothing(*refs):
    pass


def come_after(value, *others):
    return pl.pallas_call(
        nothing,
        out_shape=pltpu.HBM(value.shape, value.dtype),
        in_specs=[pl.BlockSpec(memory_space=pl.ANY)] * (1 + len(others)),
        out_specs=pl.BlockSpec(memory_space=pl.ANY),
        input_output_aliases={0: 0},
        compiler_params=pltpu.CompilerParams(vmem_limit_bytes=VMEM_GRANT),
        cost_estimate=pl.CostEstimate(flops=0, bytes_accessed=0, transcendentals=0),
        name="after",
    )(*map(in_hbm, (value, *others)))


def folded_ring(length):
    return [0] + list(range(1, length, 2)) + list(range(2, length, 2))[::-1]


def by_permutes(failed, holders, tokens, expert_ids, gate_levels, weights, owners, capacity):
    tok, top = expert_ids.shape
    width = tokens.shape[1]
    order = folded_ring(owners // 4)
    steps = len(order)
    after = {a: order[(i + 1) % steps] for i, a in enumerate(order)}
    round_ring = [(d, after[d // 4] * 4 + d % 4) for d in range(owners)]
    over_y = [(d, d ^ 2) for d in range(owners)]
    over_core = [(d, d ^ 1) for d in range(owners)]
    move = lambda a, pairs: lax.ppermute(a, "expert", pairs)

    meta = jnp.concatenate([expert_ids.T, gate_levels.T >> 5, gate_levels.T & 31], axis=0)
    meta = meta.astype(jnp.bfloat16).reshape(1, 3 * top * tok)
    meta = jnp.pad(meta, ((0, 7), (0, width - 3 * top * tok)))
    held = [jnp.concatenate([tokens, meta], axis=0)]
    across, results = [], []
    for k in range(steps):
        if k > 0:
            held.append(move(held[-1], round_ring))
            if k > 1:
                held[k] = come_after(held[k], results[k - 2][0])
        across.append(move(held[k], over_y))
        blocks = (held[k], across[k], move(held[k], over_core), move(across[k], over_core))
        earlier = [results[-1][0]] if results else []
        results.append(run_group(failed, holders, blocks, weights, earlier, tok, top, capacity))

    f32 = lambda a: a.astype(jnp.float32)
    passing = None
    for k in list(range(1, steps)) + [0]:
        keep0, keep1, send = results[k]
        if k < steps - 1:
            send = come_after(send, across[k + 1], held[min(k + 2, steps - 1)])
        got = move(send, over_core)
        far = (f32(keep1) + f32(got[1])).astype(jnp.bfloat16)
        total = f32(keep0) + f32(got[0]) + f32(move(far, over_y))
        if passing is not None:
            total = total + f32(move(passing, round_ring))
        passing = total.astype(jnp.bfloat16)
    return passing


def shards(
    tokens,
    expert_ids,
    gate_levels,
    failed_device,
    replica_holders,
    w_gate,
    w_down,
    spare_gate,
    spare_down,
):
    owners = lax.axis_size("expert")
    tok_count, top_count = expert_ids.shape
    capacity = 2 * tok_count * top_count // owners
    my_index = lax.axis_index("expert").astype(jnp.int32)
    failed_id = failed_device[0]
    holder_row = lax.dynamic_index_in_dim(replica_holders, failed_id, 0, keepdims=False)
    holds = jnp.any(holder_row == my_index).astype(jnp.int32)
    scalars = jnp.stack([my_index, failed_id, holds])
    weights = (w_gate, w_down, spare_gate, spare_down)
    if owners % 4 == 0 and owners <= 32 and 3 * top_count * tok_count <= tokens.shape[1]:
        return by_permutes(
            failed_device, replica_holders, tokens, expert_ids, gate_levels, weights, owners, capacity
        )
    codes = (expert_ids * LEVELS + gate_levels).T
    all_codes = lax.all_gather(codes, "expert", axis=0)
    all_tokens = lax.all_gather(tokens, "expert", axis=0, tiled=True)
    dense = run_experts(scalars, all_codes, all_tokens, *weights, capacity)
    return lax.psum_scatter(dense, "expert", scatter_dimension=0, tiled=True)


def solution(mesh):
    in_specs = (
        P(("group", "expert"), None),
        P(("group", "expert"), None),
        P(("group", "expert"), None),
        P(),
        P(),
        P("expert", None, None),
        P("expert", None, None),
        P("expert", None, None),
        P("expert", None, None),
    )
    out_specs = P(("group", "expert"), None)
    return jax.shard_map(shards, mesh=mesh, in_specs=in_specs, out_specs=out_specs, check_vma=False)
```

```python
import functools
import jax
import jax.numpy as jnp
from jax import lax
from jax.experimental import pallas as pl
from jax.experimental.pallas import tpu as pltpu
from jax.sharding import PartitionSpec as P

LEVELS = 1024
VMEM_GRANT = 65200 * 1024


def gated_unit(values):
    return values * (0.5 + 0.5 * jnp.tanh(0.851 * values))


def expert_kernel(
    scalars,
    codes,
    tokens,
    w_gate,
    w_down,
    spare_gate,
    spare_down,
    out,
    rows_in,
    spare_in,
    hidden,
    spare_hidden,
    rows_out,
    *,
    subs,
    sources,
    capacity,
):
    tok = codes.shape[2]
    part = sources * tok
    rows = sources * capacity
    width = tokens.shape[1]
    tile = 512
    my_id, failed_id, holds = scalars[0], scalars[1], scalars[2]
    serves = my_id != failed_id

    before = (
        lax.broadcasted_iota(jnp.int32, (tok, tok), 0)
        < lax.broadcasted_iota(jnp.int32, (tok, tok), 1)
    ).astype(jnp.bfloat16)
    row_iota = lax.broadcasted_iota(jnp.int32, (rows, tok), 0)

    def picker(code, wanted, live):
        named = ((code // LEVELS) == wanted) & live
        mask = jnp.sum(named.astype(jnp.float32), axis=1)
        level = jnp.sum(jnp.where(named, (code % LEVELS), 0).astype(jnp.float32), axis=1) / LEVELS
        rank = jnp.dot(mask.astype(jnp.bfloat16), before, preferred_element_type=jnp.float32)
        picks, weights = [], None
        for s in range(sources):
            place = jnp.where(mask[s : s + 1] > 0, rank[s : s + 1].astype(jnp.int32) + s * capacity, -1)
            hit = row_iota == place
            scaled = jnp.sum(jnp.where(hit, level[s : s + 1], 0.0), axis=1, keepdims=True)
            weights = scaled if weights is None else weights + scaled
            picks.append(hit.astype(jnp.float32).astype(jnp.bfloat16))
        return jnp.concatenate(picks, axis=1), weights

    picks, weights, spare_weights = [], [], []
    for j in range(subs):
        code = codes[j * sources : (j + 1) * sources]
        pick, weight = picker(code, my_id, serves)
        spare_pick, spare_weight = picker(code, failed_id, holds > 0)
        both = jnp.concatenate([pick, spare_pick], axis=0)
        picks.append(both)
        weights.append(weight)
        spare_weights.append(spare_weight)
        for n in range(0, width, tile):
            got = jnp.dot(
                both, tokens[j * part : (j + 1) * part, n : n + tile], preferred_element_type=jnp.float32
            ).astype(jnp.bfloat16)
            rows_in[j * rows : (j + 1) * rows, n : n + tile] = got[:rows]
            spare_in[j * rows : (j + 1) * rows, n : n + tile] = got[rows:]

    for n in range(0, hidden.shape[1], tile):
        hidden[:, n : n + tile] = gated_unit(
            jnp.dot(rows_in[...], w_gate[0, :, n : n + tile], preferred_element_type=jnp.float32)
        ).astype(jnp.bfloat16)
    for n in range(0, width, tile):
        result = jnp.dot(hidden[...], w_down[0, :, n : n + tile], preferred_element_type=jnp.float32)
        result = result.astype(jnp.bfloat16).astype(jnp.float32)
        for j in range(subs):
            rows_out[j, :rows, n : n + tile] = (result[j * rows : (j + 1) * rows] * weights[j]).astype(
                jnp.bfloat16
            )

    @pl.when(holds > 0)
    def _():
        spare_hidden[...] = gated_unit(
            jnp.dot(spare_in[...], spare_gate[0], preferred_element_type=jnp.float32)
        ).astype(jnp.bfloat16)
        for n in range(0, width, tile):
            result = jnp.dot(
                spare_hidden[...], spare_down[0, :, n : n + tile], preferred_element_type=jnp.float32
            )
            for j in range(subs):
                rows_out[j, rows:, n : n + tile] = (
                    result[j * rows : (j + 1) * rows] * spare_weights[j]
                ).astype(jnp.bfloat16)

    @pl.when(holds <= 0)
    def _():
        rows_out[:, rows:, :] = jnp.zeros((subs, rows, width), jnp.bfloat16)

    for j in range(subs):
        for n in range(0, width, tile):
            out[j * part : (j + 1) * part, n : n + tile] = lax.dot_general(
                picks[j],
                rows_out[j, :, n : n + tile],
                (((0,), (0,)), ((), ())),
                preferred_element_type=jnp.float32,
            ).astype(jnp.bfloat16)


def run_experts(scalars, codes, tokens, w_gate, w_down, spare_gate, spare_down, capacity):
    owners, top, tok = codes.shape
    width, inner, spare = w_gate.shape[1], w_gate.shape[2], spare_gate.shape[2]
    sources = max(1, 128 // capacity)
    subs = 2 if sources * tok <= 512 else 1
    step = subs * sources
    rows = sources * capacity
    whole = lambda a: pl.BlockSpec(a.shape, lambda i: (0, 0, 0), pipeline_mode=pl.Buffered(1))
    return pl.pallas_call(
        functools.partial(expert_kernel, subs=subs, sources=sources, capacity=capacity),
        grid=(owners // step,),
        out_shape=jax.ShapeDtypeStruct((owners * tok, width), jnp.bfloat16),
        in_specs=[
            pl.BlockSpec(memory_space=pltpu.SMEM),
            pl.BlockSpec((step, top, tok), lambda i: (i, 0, 0)),
            pl.BlockSpec((step * tok, width), lambda i: (i, 0)),
            whole(w_gate),
            whole(w_down),
            whole(spare_gate),
            whole(spare_down),
        ],
        out_specs=pl.BlockSpec((step * tok, width), lambda i: (i, 0)),
        scratch_shapes=[
            pltpu.VMEM((subs * rows, width), jnp.bfloat16),
            pltpu.VMEM((subs * rows, width), jnp.bfloat16),
            pltpu.VMEM((subs * rows, inner), jnp.bfloat16),
            pltpu.VMEM((subs * rows, spare), jnp.bfloat16),
            pltpu.VMEM((subs, 2 * rows, width), jnp.bfloat16),
        ],
        compiler_params=pltpu.CompilerParams(vmem_limit_bytes=56 * 1024 * 1024),
        cost_estimate=pl.CostEstimate(
            flops=owners * capacity * 4 * width * (inner + spare),
            bytes_accessed=4 * width * (inner + spare) + 4 * owners * tok * width,
            transcendentals=owners * capacity * inner,
        ),
        name="experts",
    )(scalars, codes, tokens, w_gate, w_down, spare_gate, spare_down)


def group_kernel(failed, holders, *refs, others, tok, top, capacity):
    blocks, weights_hbm, refs = refs[:4], refs[4:8], refs[8 + others :]
    keep0, keep1, send, held, w_gate, w_down, spare_gate, spare_down = refs[:8]
    rows_in, spare_in, hidden, spare_hidden, rows_out, dense, fetched, stored = refs[8:]
    width, inner = w_gate.shape
    tile = 512
    my_id, failed_id = lax.axis_index("expert"), failed[0]
    holds = holders[failed_id, 0] == my_id
    for j in range(1, holders.shape[1]):
        holds = holds | (holders[failed_id, j] == my_id)
    copies = []

    def fetch(source, target, start=True):
        copy = pltpu.make_async_copy(source, target, fetched.at[len(copies)])
        if start:
            copy.start()
        copies.append(copy)
        return copy

    gate_hbm, down_hbm, spare_gate_hbm, spare_down_hbm = weights_hbm
    block_copies = [fetch(block, held.at[s]) for s, block in enumerate(blocks)]
    gate_copies = [
        fetch(gate_hbm.at[0, :, n : n + tile], w_gate.at[:, n : n + tile]) for n in range(0, inner, tile)
    ]
    spare_copies = [
        fetch(spare_gate_hbm.at[0], spare_gate, False),
        fetch(spare_down_hbm.at[0], spare_down, False),
    ]

    @pl.when(holds)
    def _():
        for copy in spare_copies:
            copy.start()

    down_copies = [
        fetch(down_hbm.at[0, :, n : n + tile], w_down.at[:, n : n + tile]) for n in range(0, width, tile)
    ]

    before = (
        lax.broadcasted_iota(jnp.int32, (tok, tok), 0)
        < lax.broadcasted_iota(jnp.int32, (tok, tok), 1)
    ).astype(jnp.float32).astype(jnp.bfloat16)
    row_iota = lax.broadcasted_iota(jnp.int32, (capacity, tok), 0)

    def picker(meta, wanted, live):
        mask = jnp.zeros((8, tok), jnp.float32)
        level = jnp.zeros((8, tok), jnp.float32)
        for k in range(top):
            named = (meta[:, k * tok : (k + 1) * tok] == wanted.astype(jnp.float32)) & live
            high = meta[:, (top + k) * tok : (top + k + 1) * tok]
            low = meta[:, (2 * top + k) * tok : (2 * top + k + 1) * tok]
            mask = mask + jnp.where(named, 1.0, 0.0)
            level = level + jnp.where(named, (high * 32.0 + low) / LEVELS, 0.0)
        rank = jnp.dot(mask.astype(jnp.bfloat16), before, preferred_element_type=jnp.float32)
        place = jnp.where(mask[:1] > 0, rank[:1].astype(jnp.int32), -1)
        hit = row_iota == place
        weight = jnp.sum(jnp.where(hit, level[:1], 0.0), axis=1, keepdims=True)
        return hit.astype(jnp.float32).astype(jnp.bfloat16), weight

    picks, weights, spare_weights = [], [], []
    for s in range(len(blocks)):
        block_copies[s].wait()
        meta = held[s, tok : tok + 8, :].astype(jnp.float32)
        pick, weight = picker(meta, my_id, my_id != failed_id)
        spare_pick, spare_weight = picker(meta, failed_id, holds)
        both = jnp.concatenate([pick, spare_pick], axis=0)
        picks.append(both)
        weights.append(weight)
        spare_weights.append(spare_weight)
        for n in range(0, width, tile):
            got = jnp.dot(both, held[s, :tok, n : n + tile], preferred_element_type=jnp.float32).astype(
                jnp.bfloat16
            )
            rows_in[s * capacity : (s + 1) * capacity, n : n + tile] = got[:capacity]
            spare_in[s * capacity : (s + 1) * capacity, n : n + tile] = got[capacity:]

    for i, n in enumerate(range(0, inner, tile)):
        gate_copies[i].wait()
        hidden[:, n : n + tile] = gated_unit(
            jnp.dot(rows_in[...], w_gate[:, n : n + tile], preferred_element_type=jnp.float32)
        ).astype(jnp.bfloat16)

    @pl.when(holds)
    def _():
        for copy in spare_copies:
            copy.wait()
        spare_hidden[...] = gated_unit(
            jnp.dot(spare_in[...], spare_gate[...], preferred_element_type=jnp.float32)
        ).astype(jnp.bfloat16)
        for n in range(0, width, tile):
            result = jnp.dot(
                spare_hidden[...], spare_down[:, n : n + tile], preferred_element_type=jnp.float32
            )
            for s in range(len(blocks)):
                rows_out[s, capacity:, n : n + tile] = (
                    result[s * capacity : (s + 1) * capacity] * spare_weights[s]
                ).astype(jnp.bfloat16)

    @pl.when(jnp.logical_not(holds))
    def _():
        rows_out[:, capacity:, :] = jnp.zeros((len(blocks), capacity, width), jnp.bfloat16)

    stores = []
    for i, n in enumerate(range(0, width, tile)):
        down_copies[i].wait()
        result = jnp.dot(hidden[...], w_down[:, n : n + tile], preferred_element_type=jnp.float32)
        result = result.astype(jnp.bfloat16).astype(jnp.float32)
        for s in range(len(blocks)):
            rows_out[s, :capacity, n : n + tile] = (
                result[s * capacity : (s + 1) * capacity] * weights[s]
            ).astype(jnp.bfloat16)
            dense[s, :, n : n + tile] = lax.dot_general(
                picks[s],
                rows_out[s, :, n : n + tile],
                (((0,), (0,)), ((), ())),
                preferred_element_type=jnp.float32,
            ).astype(jnp.bfloat16)
            target = (keep0, keep1, send.at[0], send.at[1])[s]
            stores.append(
                pltpu.make_async_copy(
                    dense.at[s, :, n : n + tile], target.at[:, n : n + tile], stored.at[len(stores)]
                )
            )
            stores[-1].start()
    for copy in stores:
        copy.wait()


def run_group(failed, holders, blocks, weights, earlier, tok, top, capacity):
    width, inner, spare = weights[0].shape[1], weights[0].shape[2], weights[2].shape[2]
    count = len(blocks)
    rows = count * capacity
    hbm = pl.BlockSpec(memory_space=pl.ANY)
    smem = pl.BlockSpec(memory_space=pltpu.SMEM)
    block = pltpu.HBM((tok, width), jnp.bfloat16)
    return pl.pallas_call(
        functools.partial(
            group_kernel, others=len(earlier), tok=tok, top=top, capacity=capacity
        ),
        out_shape=(block, block, pltpu.HBM((2, tok, width), jnp.bfloat16)),
        in_specs=[smem, smem] + [hbm] * (count + 4 + len(earlier)),
        out_specs=(hbm, hbm, hbm),
        scratch_shapes=[
            pltpu.VMEM((count, *blocks[0].shape), jnp.bfloat16),
            pltpu.VMEM((width, inner), jnp.bfloat16),
            pltpu.VMEM((inner, width), jnp.bfloat16),
            pltpu.VMEM((width, spare), jnp.bfloat16),
            pltpu.VMEM((spare, width), jnp.bfloat16),
            pltpu.VMEM((rows, width), jnp.bfloat16),
            pltpu.VMEM((rows, width), jnp.bfloat16),
            pltpu.VMEM((rows, inner), jnp.bfloat16),
            pltpu.VMEM((rows, spare), jnp.bfloat16),
            pltpu.VMEM((count, 2 * capacity, width), jnp.bfloat16),
            pltpu.VMEM((count, tok, width), jnp.bfloat16),
            pltpu.SemaphoreType.DMA((count + inner // 512 + width // 512 + 2,)),
            pltpu.SemaphoreType.DMA((count * (width // 512),)),
        ],
        compiler_params=pltpu.CompilerParams(vmem_limit_bytes=VMEM_GRANT),
        cost_estimate=pl.CostEstimate(
            flops=rows * 4 * width * (inner + spare),
            bytes_accessed=4 * width * (inner + spare) + 4 * count * tok * width,
            transcendentals=rows * inner,
        ),
        name="group",
    )(failed, holders, *map(in_hbm, (*blocks, *weights, *earlier)))


def in_hbm(array):
    return pltpu.with_memory_space_constraint(array, pltpu.HBM)


def nothing(*refs):
    pass


def come_after(value, *others):
    return pl.pallas_call(
        nothing,
        out_shape=pltpu.HBM(value.shape, value.dtype),
        in_specs=[pl.BlockSpec(memory_space=pl.ANY)] * (1 + len(others)),
        out_specs=pl.BlockSpec(memory_space=pl.ANY),
        input_output_aliases={0: 0},
        compiler_params=pltpu.CompilerParams(vmem_limit_bytes=VMEM_GRANT),
        cost_estimate=pl.CostEstimate(flops=0, bytes_accessed=0, transcendentals=0),
        name="after",
    )(*map(in_hbm, (value, *others)))


def folded_ring(length):
    return [0] + list(range(1, length, 2)) + list(range(2, length, 2))[::-1]


def by_permutes(failed, holders, tokens, expert_ids, gate_levels, weights, owners, capacity):
    tok, top = expert_ids.shape
    width = tokens.shape[1]
    order = folded_ring(owners // 4)
    steps = len(order)
    after = {a: order[(i + 1) % steps] for i, a in enumerate(order)}
    round_ring = [(d, after[d // 4] * 4 + d % 4) for d in range(owners)]
    over_y = [(d, d ^ 2) for d in range(owners)]
    over_core = [(d, d ^ 1) for d in range(owners)]
    move = lambda a, pairs: lax.ppermute(a, "expert", pairs)

    meta = jnp.concatenate([expert_ids.T, gate_levels.T >> 5, gate_levels.T & 31], axis=0)
    meta = meta.astype(jnp.bfloat16).reshape(1, 3 * top * tok)
    meta = jnp.pad(meta, ((0, 7), (0, width - 3 * top * tok)))
    held = [jnp.concatenate([tokens, meta], axis=0)]
    across, results = [], []
    for k in range(steps):
        if k > 0:
            held.append(move(held[-1], round_ring))
            if k > 1:
                held[k] = come_after(held[k], results[k - 2][0])
        if 1 < k == steps - 1:
            across.append(move(across[-1], round_ring))
        else:
            across.append(move(held[k], over_y))
        if k == 1:
            across[1] = come_after(across[1], results[0][0])
        blocks = (held[k], across[k], move(held[k], over_core), move(across[k], over_core))
        earlier = [results[-1][0]] if results else []
        results.append(run_group(failed, holders, blocks, weights, earlier, tok, top, capacity))

    f32 = lambda a: a.astype(jnp.float32)
    passing = None
    for k in list(range(1, steps)) + [0]:
        keep0, keep1, send = results[k]
        if k < steps - 1:
            send = come_after(send, across[k + 1], held[min(k + 2, steps - 1)])
        got = move(send, over_core)
        far = (f32(keep1) + f32(got[1])).astype(jnp.bfloat16)
        if k == 0 and steps > 1:
            far = come_after(far, from_y)
        from_y = move(far, over_y)
        total = f32(keep0) + f32(got[0]) + f32(from_y)
        if passing is not None:
            total = total + f32(move(passing, round_ring))
        passing = total.astype(jnp.bfloat16)
    return passing


def shards(
    tokens,
    expert_ids,
    gate_levels,
    failed_device,
    replica_holders,
    w_gate,
    w_down,
    spare_gate,
    spare_down,
):
    owners = lax.axis_size("expert")
    tok_count, top_count = expert_ids.shape
    capacity = 2 * tok_count * top_count // owners
    my_index = lax.axis_index("expert").astype(jnp.int32)
    failed_id = failed_device[0]
    holder_row = lax.dynamic_index_in_dim(replica_holders, failed_id, 0, keepdims=False)
    holds = jnp.any(holder_row == my_index).astype(jnp.int32)
    scalars = jnp.stack([my_index, failed_id, holds])
    weights = (w_gate, w_down, spare_gate, spare_down)
    if owners % 4 == 0 and owners <= 32 and 3 * top_count * tok_count <= tokens.shape[1]:
        return by_permutes(
            failed_device, replica_holders, tokens, expert_ids, gate_levels, weights, owners, capacity
        )
    codes = (expert_ids * LEVELS + gate_levels).T
    all_codes = lax.all_gather(codes, "expert", axis=0)
    all_tokens = lax.all_gather(tokens, "expert", axis=0, tiled=True)
    dense = run_experts(scalars, all_codes, all_tokens, *weights, capacity)
    return lax.psum_scatter(dense, "expert", scatter_dimension=0, tiled=True)


def solution(mesh):
    in_specs = (
        P(("group", "expert"), None),
        P(("group", "expert"), None),
        P(("group", "expert"), None),
        P(),
        P(),
        P("expert", None, None),
        P("expert", None, None),
        P("expert", None, None),
        P("expert", None, None),
    )
    out_specs = P(("group", "expert"), None)
    return jax.shard_map(shards, mesh=mesh, in_specs=in_specs, out_specs=out_specs, check_vma=False)
```

```python
import functools
import jax
import jax.numpy as jnp
from jax import lax
from jax.experimental import pallas as pl
from jax.experimental.pallas import tpu as pltpu
from jax.sharding import PartitionSpec as P

LEVELS = 1024
VMEM_GRANT = 65200 * 1024


def gated_unit(values):
    return values * (0.5 + 0.5 * jnp.tanh(0.851 * values))


def expert_kernel(
    scalars,
    codes,
    tokens,
    w_gate,
    w_down,
    spare_gate,
    spare_down,
    out,
    rows_in,
    spare_in,
    hidden,
    spare_hidden,
    rows_out,
    *,
    subs,
    sources,
    capacity,
):
    tok = codes.shape[2]
    part = sources * tok
    rows = sources * capacity
    width = tokens.shape[1]
    tile = 512
    my_id, failed_id, holds = scalars[0], scalars[1], scalars[2]
    serves = my_id != failed_id

    before = (
        lax.broadcasted_iota(jnp.int32, (tok, tok), 0)
        < lax.broadcasted_iota(jnp.int32, (tok, tok), 1)
    ).astype(jnp.bfloat16)
    row_iota = lax.broadcasted_iota(jnp.int32, (rows, tok), 0)

    def picker(code, wanted, live):
        named = ((code // LEVELS) == wanted) & live
        mask = jnp.sum(named.astype(jnp.float32), axis=1)
        level = jnp.sum(jnp.where(named, (code % LEVELS), 0).astype(jnp.float32), axis=1) / LEVELS
        rank = jnp.dot(mask.astype(jnp.bfloat16), before, preferred_element_type=jnp.float32)
        picks, weights = [], None
        for s in range(sources):
            place = jnp.where(mask[s : s + 1] > 0, rank[s : s + 1].astype(jnp.int32) + s * capacity, -1)
            hit = row_iota == place
            scaled = jnp.sum(jnp.where(hit, level[s : s + 1], 0.0), axis=1, keepdims=True)
            weights = scaled if weights is None else weights + scaled
            picks.append(hit.astype(jnp.float32).astype(jnp.bfloat16))
        return jnp.concatenate(picks, axis=1), weights

    picks, weights, spare_weights = [], [], []
    for j in range(subs):
        code = codes[j * sources : (j + 1) * sources]
        pick, weight = picker(code, my_id, serves)
        spare_pick, spare_weight = picker(code, failed_id, holds > 0)
        both = jnp.concatenate([pick, spare_pick], axis=0)
        picks.append(both)
        weights.append(weight)
        spare_weights.append(spare_weight)
        for n in range(0, width, tile):
            got = jnp.dot(
                both, tokens[j * part : (j + 1) * part, n : n + tile], preferred_element_type=jnp.float32
            ).astype(jnp.bfloat16)
            rows_in[j * rows : (j + 1) * rows, n : n + tile] = got[:rows]
            spare_in[j * rows : (j + 1) * rows, n : n + tile] = got[rows:]

    for n in range(0, hidden.shape[1], tile):
        hidden[:, n : n + tile] = gated_unit(
            jnp.dot(rows_in[...], w_gate[0, :, n : n + tile], preferred_element_type=jnp.float32)
        ).astype(jnp.bfloat16)
    for n in range(0, width, tile):
        result = jnp.dot(hidden[...], w_down[0, :, n : n + tile], preferred_element_type=jnp.float32)
        result = result.astype(jnp.bfloat16).astype(jnp.float32)
        for j in range(subs):
            rows_out[j, :rows, n : n + tile] = (result[j * rows : (j + 1) * rows] * weights[j]).astype(
                jnp.bfloat16
            )

    @pl.when(holds > 0)
    def _():
        spare_hidden[...] = gated_unit(
            jnp.dot(spare_in[...], spare_gate[0], preferred_element_type=jnp.float32)
        ).astype(jnp.bfloat16)
        for n in range(0, width, tile):
            result = jnp.dot(
                spare_hidden[...], spare_down[0, :, n : n + tile], preferred_element_type=jnp.float32
            )
            for j in range(subs):
                rows_out[j, rows:, n : n + tile] = (
                    result[j * rows : (j + 1) * rows] * spare_weights[j]
                ).astype(jnp.bfloat16)

    @pl.when(holds <= 0)
    def _():
        rows_out[:, rows:, :] = jnp.zeros((subs, rows, width), jnp.bfloat16)

    for j in range(subs):
        for n in range(0, width, tile):
            out[j * part : (j + 1) * part, n : n + tile] = lax.dot_general(
                picks[j],
                rows_out[j, :, n : n + tile],
                (((0,), (0,)), ((), ())),
                preferred_element_type=jnp.float32,
            ).astype(jnp.bfloat16)


def run_experts(scalars, codes, tokens, w_gate, w_down, spare_gate, spare_down, capacity):
    owners, top, tok = codes.shape
    width, inner, spare = w_gate.shape[1], w_gate.shape[2], spare_gate.shape[2]
    sources = max(1, 128 // capacity)
    subs = 2 if sources * tok <= 512 else 1
    step = subs * sources
    rows = sources * capacity
    whole = lambda a: pl.BlockSpec(a.shape, lambda i: (0, 0, 0), pipeline_mode=pl.Buffered(1))
    return pl.pallas_call(
        functools.partial(expert_kernel, subs=subs, sources=sources, capacity=capacity),
        grid=(owners // step,),
        out_shape=jax.ShapeDtypeStruct((owners * tok, width), jnp.bfloat16),
        in_specs=[
            pl.BlockSpec(memory_space=pltpu.SMEM),
            pl.BlockSpec((step, top, tok), lambda i: (i, 0, 0)),
            pl.BlockSpec((step * tok, width), lambda i: (i, 0)),
            whole(w_gate),
            whole(w_down),
            whole(spare_gate),
            whole(spare_down),
        ],
        out_specs=pl.BlockSpec((step * tok, width), lambda i: (i, 0)),
        scratch_shapes=[
            pltpu.VMEM((subs * rows, width), jnp.bfloat16),
            pltpu.VMEM((subs * rows, width), jnp.bfloat16),
            pltpu.VMEM((subs * rows, inner), jnp.bfloat16),
            pltpu.VMEM((subs * rows, spare), jnp.bfloat16),
            pltpu.VMEM((subs, 2 * rows, width), jnp.bfloat16),
        ],
        compiler_params=pltpu.CompilerParams(vmem_limit_bytes=56 * 1024 * 1024),
        cost_estimate=pl.CostEstimate(
            flops=owners * capacity * 4 * width * (inner + spare),
            bytes_accessed=4 * width * (inner + spare) + 4 * owners * tok * width,
            transcendentals=owners * capacity * inner,
        ),
        name="experts",
    )(scalars, codes, tokens, w_gate, w_down, spare_gate, spare_down)


def group_kernel(failed, holders, *refs, others, tok, top, capacity):
    blocks, weights_hbm, refs = refs[:4], refs[4:8], refs[8 + others :]
    keep0, keep1, send, held, w_gate, w_down, spare_gate, spare_down = refs[:8]
    rows_in, spare_in, hidden, spare_hidden, rows_out, dense, fetched, stored = refs[8:]
    width, inner = w_gate.shape
    tile = 512
    my_id, failed_id = lax.axis_index("expert"), failed[0]
    holds = holders[0, failed_id] == my_id
    for j in range(1, holders.shape[0]):
        holds = holds | (holders[j, failed_id] == my_id)
    copies = []

    def fetch(source, target, start=True):
        copy = pltpu.make_async_copy(source, target, fetched.at[len(copies)])
        if start:
            copy.start()
        copies.append(copy)
        return copy

    gate_hbm, down_hbm, spare_gate_hbm, spare_down_hbm = weights_hbm
    block_copies = [fetch(block, held.at[s]) for s, block in enumerate(blocks)]
    gate_copies = [
        fetch(gate_hbm.at[0, :, n : n + tile], w_gate.at[:, n : n + tile]) for n in range(0, inner, tile)
    ]
    spare_copies = [
        fetch(spare_gate_hbm.at[0], spare_gate, False),
        fetch(spare_down_hbm.at[0], spare_down, False),
    ]

    @pl.when(holds)
    def _():
        for copy in spare_copies:
            copy.start()

    down_copies = [
        fetch(down_hbm.at[0, :, n : n + tile], w_down.at[:, n : n + tile]) for n in range(0, width, tile)
    ]

    count = len(blocks)
    before = (
        lax.broadcasted_iota(jnp.int32, (tok, tok), 0)
        < lax.broadcasted_iota(jnp.int32, (tok, tok), 1)
    ).astype(jnp.float32).astype(jnp.bfloat16)
    own = lax.broadcasted_iota(jnp.int32, (2 * count, tok), 0) < count
    wanted = jnp.where(own, my_id, failed_id).astype(jnp.float32)
    serves = jnp.where(my_id != failed_id, 1.0, 0.0)
    live = jnp.where(own, serves, jnp.where(holds, 1.0, 0.0))
    slots = 2 * capacity
    row_iota = lax.broadcasted_iota(jnp.int32, (slots, tok), 0)
    lane_iota = lax.broadcasted_iota(jnp.int32, (tok, slots), 1)

    for copy in block_copies:
        copy.wait()
    meta = jnp.concatenate([held[s, tok : tok + 8, :].astype(jnp.float32)[:1] for s in range(count)] * 2, axis=0)
    mask = jnp.zeros((2 * count, tok), jnp.float32)
    level = jnp.zeros((2 * count, tok), jnp.float32)
    for k in range(top):
        named = jnp.where(meta[:, k * tok : (k + 1) * tok] == wanted, live, 0.0)
        high = meta[:, (top + k) * tok : (top + k + 1) * tok]
        low = meta[:, (2 * top + k) * tok : (2 * top + k + 1) * tok]
        mask = mask + named
        level = level + named * ((high * 32.0 + low) / LEVELS)
    rank = jnp.dot(mask.astype(jnp.bfloat16), before, preferred_element_type=jnp.float32)
    place = jnp.where(mask > 0, rank + jnp.where(own, 0.0, float(capacity)), -1.0)
    place_rows = place.astype(jnp.int32)
    place_columns = place.T.astype(jnp.int32)

    spreads, weights = [], []
    for s in range(count):
        here, there = place_rows[s : s + 1], place_rows[count + s : count + s + 1]
        hit_here, hit_there = row_iota == here, row_iota == there
        pick = jnp.where(hit_here | hit_there, 1.0, 0.0).astype(jnp.bfloat16)
        weights.append(
            jnp.sum(
                jnp.where(hit_here, level[s : s + 1], 0.0)
                + jnp.where(hit_there, level[count + s : count + s + 1], 0.0),
                axis=1,
                keepdims=True,
            )
        )
        here, there = place_columns[:, s : s + 1], place_columns[:, count + s : count + s + 1]
        spreads.append(jnp.where((lane_iota == here) | (lane_iota == there), 1.0, 0.0).astype(jnp.bfloat16))
        for n in range(0, width, tile):
            got = jnp.dot(pick, held[s, :tok, n : n + tile], preferred_element_type=jnp.float32).astype(
                jnp.bfloat16
            )
            rows_in[s * capacity : (s + 1) * capacity, n : n + tile] = got[:capacity]
            spare_in[s * capacity : (s + 1) * capacity, n : n + tile] = got[capacity:]

    for i, n in enumerate(range(0, inner, tile)):
        gate_copies[i].wait()
        hidden[:, n : n + tile] = gated_unit(
            jnp.dot(rows_in[...], w_gate[:, n : n + tile], preferred_element_type=jnp.float32)
        ).astype(jnp.bfloat16)

    @pl.when(holds)
    def _():
        for copy in spare_copies:
            copy.wait()
        spare_hidden[...] = gated_unit(
            jnp.dot(spare_in[...], spare_gate[...], preferred_element_type=jnp.float32)
        ).astype(jnp.bfloat16)
        for n in range(0, width, tile):
            result = jnp.dot(
                spare_hidden[...], spare_down[:, n : n + tile], preferred_element_type=jnp.float32
            )
            for s in range(count):
                rows_out[s, capacity:, n : n + tile] = (
                    result[s * capacity : (s + 1) * capacity] * weights[s][capacity:]
                ).astype(jnp.bfloat16)

    @pl.when(jnp.logical_not(holds))
    def _():
        rows_out[:, capacity:, :] = jnp.zeros((count, capacity, width), jnp.bfloat16)

    stores = []
    for i, n in enumerate(range(0, width, tile)):
        down_copies[i].wait()
        result = jnp.dot(hidden[...], w_down[:, n : n + tile], preferred_element_type=jnp.float32)
        result = result.astype(jnp.bfloat16).astype(jnp.float32)
        for s in range(count):
            rows_out[s, :capacity, n : n + tile] = (
                result[s * capacity : (s + 1) * capacity] * weights[s][:capacity]
            ).astype(jnp.bfloat16)
            dense[s, :, n : n + tile] = jnp.dot(
                spreads[s], rows_out[s, :, n : n + tile], preferred_element_type=jnp.float32
            ).astype(jnp.bfloat16)
            target = (keep0, keep1, send.at[0], send.at[1])[s]
            stores.append(
                pltpu.make_async_copy(
                    dense.at[s, :, n : n + tile], target.at[:, n : n + tile], stored.at[len(stores)]
                )
            )
            stores[-1].start()
    for copy in stores:
        copy.wait()


def run_group(failed, holders, blocks, weights, earlier, tok, top, capacity):
    width, inner, spare = weights[0].shape[1], weights[0].shape[2], weights[2].shape[2]
    count = len(blocks)
    rows = count * capacity
    hbm = pl.BlockSpec(memory_space=pl.ANY)
    smem = pl.BlockSpec(memory_space=pltpu.SMEM)
    block = pltpu.HBM((tok, width), jnp.bfloat16)
    return pl.pallas_call(
        functools.partial(
            group_kernel, others=len(earlier), tok=tok, top=top, capacity=capacity
        ),
        out_shape=(block, block, pltpu.HBM((2, tok, width), jnp.bfloat16)),
        in_specs=[smem, smem] + [hbm] * (count + 4 + len(earlier)),
        out_specs=(hbm, hbm, hbm),
        scratch_shapes=[
            pltpu.VMEM((count, *blocks[0].shape), jnp.bfloat16),
            pltpu.VMEM((width, inner), jnp.bfloat16),
            pltpu.VMEM((inner, width), jnp.bfloat16),
            pltpu.VMEM((width, spare), jnp.bfloat16),
            pltpu.VMEM((spare, width), jnp.bfloat16),
            pltpu.VMEM((rows, width), jnp.bfloat16),
            pltpu.VMEM((rows, width), jnp.bfloat16),
            pltpu.VMEM((rows, inner), jnp.bfloat16),
            pltpu.VMEM((rows, spare), jnp.bfloat16),
            pltpu.VMEM((count, 2 * capacity, width), jnp.bfloat16),
            pltpu.VMEM((count, tok, width), jnp.bfloat16),
            pltpu.SemaphoreType.DMA((count + inner // 512 + width // 512 + 2,)),
            pltpu.SemaphoreType.DMA((count * (width // 512),)),
        ],
        compiler_params=pltpu.CompilerParams(vmem_limit_bytes=VMEM_GRANT),
        cost_estimate=pl.CostEstimate(
            flops=rows * 4 * width * (inner + spare),
            bytes_accessed=4 * width * (inner + spare) + 4 * count * tok * width,
            transcendentals=rows * inner,
        ),
        name="group",
    )(failed, holders, *map(in_hbm, (*blocks, *weights, *earlier)))


def in_hbm(array):
    return pltpu.with_memory_space_constraint(array, pltpu.HBM)


def nothing(*refs):
    pass


def come_after(value, *others):
    return pl.pallas_call(
        nothing,
        out_shape=pltpu.HBM(value.shape, value.dtype),
        in_specs=[pl.BlockSpec(memory_space=pl.ANY)] * (1 + len(others)),
        out_specs=pl.BlockSpec(memory_space=pl.ANY),
        input_output_aliases={0: 0},
        compiler_params=pltpu.CompilerParams(vmem_limit_bytes=VMEM_GRANT),
        cost_estimate=pl.CostEstimate(flops=0, bytes_accessed=0, transcendentals=0),
        name="after",
    )(*map(in_hbm, (value, *others)))


def folded_ring(length):
    return [0] + list(range(1, length, 2)) + list(range(2, length, 2))[::-1]


def by_permutes(failed, holders, tokens, expert_ids, gate_levels, weights, owners, capacity):
    tok, top = expert_ids.shape
    width = tokens.shape[1]
    order = folded_ring(owners // 4)
    steps = len(order)
    after = {a: order[(i + 1) % steps] for i, a in enumerate(order)}
    round_ring = [(d, after[d // 4] * 4 + d % 4) for d in range(owners)]
    over_y = [(d, d ^ 2) for d in range(owners)]
    over_core = [(d, d ^ 1) for d in range(owners)]
    move = lambda a, pairs: lax.ppermute(a, "expert", pairs)

    meta = jnp.concatenate([expert_ids.T, gate_levels.T >> 5, gate_levels.T & 31], axis=0)
    meta = meta.astype(jnp.bfloat16).reshape(1, 3 * top * tok)
    meta = jnp.pad(meta, ((0, 7), (0, width - 3 * top * tok)))
    held = [jnp.concatenate([tokens, meta], axis=0)]
    across, results = [], []
    for k in range(steps):
        if k > 0:
            held.append(move(held[-1], round_ring))
            if k > 1:
                held[k] = come_after(held[k], results[k - 2][0])
        if 1 < k == steps - 1:
            across.append(move(across[-1], round_ring))
        else:
            across.append(move(held[k], over_y))
        if k == 1:
            across[1] = come_after(across[1], results[0][0])
        blocks = (held[k], across[k], move(held[k], over_core), move(across[k], over_core))
        earlier = [results[-1][0]] if results else []
        results.append(run_group(failed, holders, blocks, weights, earlier, tok, top, capacity))

    f32 = lambda a: a.astype(jnp.float32)
    passing = None
    for k in list(range(1, steps)) + [0]:
        keep0, keep1, send = results[k]
        if k < steps - 1:
            send = come_after(send, across[k + 1], held[min(k + 2, steps - 1)])
        got = move(send, over_core)
        far = (f32(keep1) + f32(got[1])).astype(jnp.bfloat16)
        if k == 0 and steps > 1:
            far = come_after(far, from_y)
        from_y = move(far, over_y)
        total = f32(keep0) + f32(got[0]) + f32(from_y)
        if passing is not None:
            total = total + f32(move(passing, round_ring))
        passing = total.astype(jnp.bfloat16)
    return passing


def shards(
    tokens,
    expert_ids,
    gate_levels,
    failed_device,
    replica_holders,
    w_gate,
    w_down,
    spare_gate,
    spare_down,
):
    owners = lax.axis_size("expert")
    tok_count, top_count = expert_ids.shape
    capacity = 2 * tok_count * top_count // owners
    my_index = lax.axis_index("expert").astype(jnp.int32)
    failed_id = failed_device[0]
    holder_row = lax.dynamic_index_in_dim(replica_holders, failed_id, 0, keepdims=False)
    holds = jnp.any(holder_row == my_index).astype(jnp.int32)
    scalars = jnp.stack([my_index, failed_id, holds])
    weights = (w_gate, w_down, spare_gate, spare_down)
    if owners % 4 == 0 and owners <= 32 and 3 * top_count * tok_count <= tokens.shape[1]:
        return by_permutes(
            failed_device, replica_holders.T, tokens, expert_ids, gate_levels, weights, owners, capacity
        )
    codes = (expert_ids * LEVELS + gate_levels).T
    all_codes = lax.all_gather(codes, "expert", axis=0)
    all_tokens = lax.all_gather(tokens, "expert", axis=0, tiled=True)
    dense = run_experts(scalars, all_codes, all_tokens, *weights, capacity)
    return lax.psum_scatter(dense, "expert", scatter_dimension=0, tiled=True)


def solution(mesh):
    in_specs = (
        P(("group", "expert"), None),
        P(("group", "expert"), None),
        P(("group", "expert"), None),
        P(),
        P(),
        P("expert", None, None),
        P("expert", None, None),
        P("expert", None, None),
        P("expert", None, None),
    )
    out_specs = P(("group", "expert"), None)
    return jax.shard_map(shards, mesh=mesh, in_specs=in_specs, out_specs=out_specs, check_vma=False)
```

```python
import functools
import jax
import jax.numpy as jnp
from jax import lax
from jax.experimental import pallas as pl
from jax.experimental.pallas import tpu as pltpu
from jax.sharding import PartitionSpec as P

LEVELS = 1024
VMEM_GRANT = 65200 * 1024


def gated_unit(values):
    return values * (0.5 + 0.5 * jnp.tanh(0.851 * values))


def expert_kernel(
    scalars,
    codes,
    tokens,
    w_gate,
    w_down,
    spare_gate,
    spare_down,
    out,
    rows_in,
    spare_in,
    hidden,
    spare_hidden,
    rows_out,
    *,
    subs,
    sources,
    capacity,
):
    tok = codes.shape[2]
    part = sources * tok
    rows = sources * capacity
    width = tokens.shape[1]
    tile = 512
    my_id, failed_id, holds = scalars[0], scalars[1], scalars[2]
    serves = my_id != failed_id

    before = (
        lax.broadcasted_iota(jnp.int32, (tok, tok), 0)
        < lax.broadcasted_iota(jnp.int32, (tok, tok), 1)
    ).astype(jnp.bfloat16)
    row_iota = lax.broadcasted_iota(jnp.int32, (rows, tok), 0)

    def picker(code, wanted, live):
        named = ((code // LEVELS) == wanted) & live
        mask = jnp.sum(named.astype(jnp.float32), axis=1)
        level = jnp.sum(jnp.where(named, (code % LEVELS), 0).astype(jnp.float32), axis=1) / LEVELS
        rank = jnp.dot(mask.astype(jnp.bfloat16), before, preferred_element_type=jnp.float32)
        picks, weights = [], None
        for s in range(sources):
            place = jnp.where(mask[s : s + 1] > 0, rank[s : s + 1].astype(jnp.int32) + s * capacity, -1)
            hit = row_iota == place
            scaled = jnp.sum(jnp.where(hit, level[s : s + 1], 0.0), axis=1, keepdims=True)
            weights = scaled if weights is None else weights + scaled
            picks.append(hit.astype(jnp.float32).astype(jnp.bfloat16))
        return jnp.concatenate(picks, axis=1), weights

    picks, weights, spare_weights = [], [], []
    for j in range(subs):
        code = codes[j * sources : (j + 1) * sources]
        pick, weight = picker(code, my_id, serves)
        spare_pick, spare_weight = picker(code, failed_id, holds > 0)
        both = jnp.concatenate([pick, spare_pick], axis=0)
        picks.append(both)
        weights.append(weight)
        spare_weights.append(spare_weight)
        for n in range(0, width, tile):
            got = jnp.dot(
                both, tokens[j * part : (j + 1) * part, n : n + tile], preferred_element_type=jnp.float32
            ).astype(jnp.bfloat16)
            rows_in[j * rows : (j + 1) * rows, n : n + tile] = got[:rows]
            spare_in[j * rows : (j + 1) * rows, n : n + tile] = got[rows:]

    for n in range(0, hidden.shape[1], tile):
        hidden[:, n : n + tile] = gated_unit(
            jnp.dot(rows_in[...], w_gate[0, :, n : n + tile], preferred_element_type=jnp.float32)
        ).astype(jnp.bfloat16)
    for n in range(0, width, tile):
        result = jnp.dot(hidden[...], w_down[0, :, n : n + tile], preferred_element_type=jnp.float32)
        result = result.astype(jnp.bfloat16).astype(jnp.float32)
        for j in range(subs):
            rows_out[j, :rows, n : n + tile] = (result[j * rows : (j + 1) * rows] * weights[j]).astype(
                jnp.bfloat16
            )

    @pl.when(holds > 0)
    def _():
        spare_hidden[...] = gated_unit(
            jnp.dot(spare_in[...], spare_gate[0], preferred_element_type=jnp.float32)
        ).astype(jnp.bfloat16)
        for n in range(0, width, tile):
            result = jnp.dot(
                spare_hidden[...], spare_down[0, :, n : n + tile], preferred_element_type=jnp.float32
            )
            for j in range(subs):
                rows_out[j, rows:, n : n + tile] = (
                    result[j * rows : (j + 1) * rows] * spare_weights[j]
                ).astype(jnp.bfloat16)

    @pl.when(holds <= 0)
    def _():
        rows_out[:, rows:, :] = jnp.zeros((subs, rows, width), jnp.bfloat16)

    for j in range(subs):
        for n in range(0, width, tile):
            out[j * part : (j + 1) * part, n : n + tile] = lax.dot_general(
                picks[j],
                rows_out[j, :, n : n + tile],
                (((0,), (0,)), ((), ())),
                preferred_element_type=jnp.float32,
            ).astype(jnp.bfloat16)


def run_experts(scalars, codes, tokens, w_gate, w_down, spare_gate, spare_down, capacity):
    owners, top, tok = codes.shape
    width, inner, spare = w_gate.shape[1], w_gate.shape[2], spare_gate.shape[2]
    sources = max(1, 128 // capacity)
    subs = 2 if sources * tok <= 512 else 1
    step = subs * sources
    rows = sources * capacity
    whole = lambda a: pl.BlockSpec(a.shape, lambda i: (0, 0, 0), pipeline_mode=pl.Buffered(1))
    return pl.pallas_call(
        functools.partial(expert_kernel, subs=subs, sources=sources, capacity=capacity),
        grid=(owners // step,),
        out_shape=jax.ShapeDtypeStruct((owners * tok, width), jnp.bfloat16),
        in_specs=[
            pl.BlockSpec(memory_space=pltpu.SMEM),
            pl.BlockSpec((step, top, tok), lambda i: (i, 0, 0)),
            pl.BlockSpec((step * tok, width), lambda i: (i, 0)),
            whole(w_gate),
            whole(w_down),
            whole(spare_gate),
            whole(spare_down),
        ],
        out_specs=pl.BlockSpec((step * tok, width), lambda i: (i, 0)),
        scratch_shapes=[
            pltpu.VMEM((subs * rows, width), jnp.bfloat16),
            pltpu.VMEM((subs * rows, width), jnp.bfloat16),
            pltpu.VMEM((subs * rows, inner), jnp.bfloat16),
            pltpu.VMEM((subs * rows, spare), jnp.bfloat16),
            pltpu.VMEM((subs, 2 * rows, width), jnp.bfloat16),
        ],
        compiler_params=pltpu.CompilerParams(vmem_limit_bytes=56 * 1024 * 1024),
        cost_estimate=pl.CostEstimate(
            flops=owners * capacity * 4 * width * (inner + spare),
            bytes_accessed=4 * width * (inner + spare) + 4 * owners * tok * width,
            transcendentals=owners * capacity * inner,
        ),
        name="experts",
    )(scalars, codes, tokens, w_gate, w_down, spare_gate, spare_down)


def group_kernel(failed, holders, *refs, others, adds, tok, top, capacity):
    blocks, weights_hbm, shares, refs = refs[:4], refs[4:8], refs[8 : 8 + 2 * adds], refs[8 + 2 * adds + others :]
    keep0, keep1, send = refs[:3]
    far, refs = refs[3 : 3 + adds], refs[3 + adds :]
    held, w_gate, w_down, spare_gate, spare_down = refs[:5]
    rows_in, spare_in, hidden, spare_hidden, rows_out, dense, summed, fetched, stored = refs[5:]
    width, inner = w_gate.shape
    tile = 512
    my_id, failed_id = lax.axis_index("expert"), failed[0]
    holds = holders[0, failed_id] == my_id
    for j in range(1, holders.shape[0]):
        holds = holds | (holders[j, failed_id] == my_id)
    copies = []

    def fetch(source, target, start=True):
        copy = pltpu.make_async_copy(source, target, fetched.at[len(copies)])
        if start:
            copy.start()
        copies.append(copy)
        return copy

    gate_hbm, down_hbm, spare_gate_hbm, spare_down_hbm = weights_hbm
    block_copies = [fetch(block, held.at[s]) for s, block in enumerate(blocks)]
    gate_copies = [
        fetch(gate_hbm.at[0, :, n : n + tile], w_gate.at[:, n : n + tile]) for n in range(0, inner, tile)
    ]
    share_copies = []
    if adds:
        share_copies = [fetch(shares[0], summed.at[0]), fetch(shares[1].at[1], summed.at[1])]
    spare_copies = [
        fetch(spare_gate_hbm.at[0], spare_gate, False),
        fetch(spare_down_hbm.at[0], spare_down, False),
    ]
    down_copies = [
        fetch(down_hbm.at[0, :, n : n + tile], w_down.at[:, n : n + tile], False)
        for n in range(0, width, tile)
    ]

    count = len(blocks)
    before = (
        lax.broadcasted_iota(jnp.int32, (tok, tok), 0)
        < lax.broadcasted_iota(jnp.int32, (tok, tok), 1)
    ).astype(jnp.float32).astype(jnp.bfloat16)
    own = lax.broadcasted_iota(jnp.int32, (2 * count, tok), 0) < count
    wanted = jnp.where(own, my_id, failed_id).astype(jnp.float32)
    serves = jnp.where(my_id != failed_id, 1.0, 0.0)
    live = jnp.where(own, serves, jnp.where(holds, 1.0, 0.0))
    slots = 2 * capacity
    row_iota = lax.broadcasted_iota(jnp.int32, (slots, tok), 0)
    lane_iota = lax.broadcasted_iota(jnp.int32, (tok, slots), 1)

    for copy in block_copies:
        copy.wait()
    meta = jnp.concatenate([held[s, tok : tok + 8, :].astype(jnp.float32)[:1] for s in range(count)] * 2, axis=0)
    mask = jnp.zeros((2 * count, tok), jnp.float32)
    level = jnp.zeros((2 * count, tok), jnp.float32)
    for k in range(top):
        named = jnp.where(meta[:, k * tok : (k + 1) * tok] == wanted, live, 0.0)
        high = meta[:, (top + k) * tok : (top + k + 1) * tok]
        low = meta[:, (2 * top + k) * tok : (2 * top + k + 1) * tok]
        mask = mask + named
        level = level + named * ((high * 32.0 + low) / LEVELS)
    rank = jnp.dot(mask.astype(jnp.bfloat16), before, preferred_element_type=jnp.float32)
    place = jnp.where(mask > 0, rank + jnp.where(own, 0.0, float(capacity)), -1.0)
    place_rows = place.astype(jnp.int32)
    place_columns = place.T.astype(jnp.int32)

    spreads, weights = [], []
    for s in range(count):
        here, there = place_rows[s : s + 1], place_rows[count + s : count + s + 1]
        hit_here, hit_there = row_iota == here, row_iota == there
        pick = jnp.where(hit_here | hit_there, 1.0, 0.0).astype(jnp.bfloat16)
        weights.append(
            jnp.sum(
                jnp.where(hit_here, level[s : s + 1], 0.0)
                + jnp.where(hit_there, level[count + s : count + s + 1], 0.0),
                axis=1,
                keepdims=True,
            )
        )
        here, there = place_columns[:, s : s + 1], place_columns[:, count + s : count + s + 1]
        spreads.append(jnp.where((lane_iota == here) | (lane_iota == there), 1.0, 0.0).astype(jnp.bfloat16))
        for n in range(0, width, tile):
            got = jnp.dot(pick, held[s, :tok, n : n + tile], preferred_element_type=jnp.float32).astype(
                jnp.bfloat16
            )
            rows_in[s * capacity : (s + 1) * capacity, n : n + tile] = got[:capacity]
            spare_in[s * capacity : (s + 1) * capacity, n : n + tile] = got[capacity:]

    for i, n in enumerate(range(0, inner, tile)):
        gate_copies[i].wait()
        if i == 0:

            @pl.when(holds)
            def _():
                for copy in spare_copies:
                    copy.start()

        for copy in down_copies[i:] if n + tile >= inner else down_copies[i : i + 1]:
            copy.start()
        hidden[:, n : n + tile] = gated_unit(
            jnp.dot(rows_in[...], w_gate[:, n : n + tile], preferred_element_type=jnp.float32)
        ).astype(jnp.bfloat16)
    stores = []
    if adds:
        for copy in share_copies:
            copy.wait()
        total = summed[0].astype(jnp.float32) + summed[1].astype(jnp.float32)
        summed[0] = total.astype(jnp.bfloat16)
        stores.append(pltpu.make_async_copy(summed.at[0], far[0], stored.at[0]))
        stores[0].start()

    @pl.when(holds)
    def _():
        for copy in spare_copies:
            copy.wait()
        spare_hidden[...] = gated_unit(
            jnp.dot(spare_in[...], spare_gate[...], preferred_element_type=jnp.float32)
        ).astype(jnp.bfloat16)
        for n in range(0, width, tile):
            result = jnp.dot(
                spare_hidden[...], spare_down[:, n : n + tile], preferred_element_type=jnp.float32
            )
            for s in range(count):
                rows_out[s, capacity:, n : n + tile] = (
                    result[s * capacity : (s + 1) * capacity] * weights[s][capacity:]
                ).astype(jnp.bfloat16)

    @pl.when(jnp.logical_not(holds))
    def _():
        rows_out[:, capacity:, :] = jnp.zeros((count, capacity, width), jnp.bfloat16)

    for i, n in enumerate(range(0, width, tile)):
        down_copies[i].wait()
        result = jnp.dot(hidden[...], w_down[:, n : n + tile], preferred_element_type=jnp.float32)
        result = result.astype(jnp.bfloat16).astype(jnp.float32)
        for s in range(count):
            rows_out[s, :capacity, n : n + tile] = (
                result[s * capacity : (s + 1) * capacity] * weights[s][:capacity]
            ).astype(jnp.bfloat16)
            dense[s, :, n : n + tile] = jnp.dot(
                spreads[s], rows_out[s, :, n : n + tile], preferred_element_type=jnp.float32
            ).astype(jnp.bfloat16)
            target = (keep0, keep1, send.at[0], send.at[1])[s]
            stores.append(
                pltpu.make_async_copy(
                    dense.at[s, :, n : n + tile], target.at[:, n : n + tile], stored.at[len(stores)]
                )
            )
            stores[-1].start()
    for copy in stores:
        copy.wait()


def run_group(failed, holders, blocks, weights, shares, earlier, tok, top, capacity):
    width, inner, spare = weights[0].shape[1], weights[0].shape[2], weights[2].shape[2]
    count, adds = len(blocks), len(shares) // 2
    rows = count * capacity
    hbm = pl.BlockSpec(memory_space=pl.ANY)
    smem = pl.BlockSpec(memory_space=pltpu.SMEM)
    block = pltpu.HBM((tok, width), jnp.bfloat16)
    return pl.pallas_call(
        functools.partial(
            group_kernel, others=len(earlier), adds=adds, tok=tok, top=top, capacity=capacity
        ),
        out_shape=(block, block, pltpu.HBM((2, tok, width), jnp.bfloat16)) + (block,) * adds,
        in_specs=[smem, smem] + [hbm] * (count + 4 + len(shares) + len(earlier)),
        out_specs=(hbm,) * (3 + adds),
        scratch_shapes=[
            pltpu.VMEM((count, *blocks[0].shape), jnp.bfloat16),
            pltpu.VMEM((width, inner), jnp.bfloat16),
            pltpu.VMEM((inner, width), jnp.bfloat16),
            pltpu.VMEM((width, spare), jnp.bfloat16),
            pltpu.VMEM((spare, width), jnp.bfloat16),
            pltpu.VMEM((rows, width), jnp.bfloat16),
            pltpu.VMEM((rows, width), jnp.bfloat16),
            pltpu.VMEM((rows, inner), jnp.bfloat16),
            pltpu.VMEM((rows, spare), jnp.bfloat16),
            pltpu.VMEM((count, 2 * capacity, width), jnp.bfloat16),
            pltpu.VMEM((count, tok, width), jnp.bfloat16),
            pltpu.VMEM((2, tok, width), jnp.bfloat16),
            pltpu.SemaphoreType.DMA((count + inner // 512 + width // 512 + 4,)),
            pltpu.SemaphoreType.DMA((1 + count * (width // 512),)),
        ],
        compiler_params=pltpu.CompilerParams(vmem_limit_bytes=VMEM_GRANT),
        cost_estimate=pl.CostEstimate(
            flops=rows * 4 * width * (inner + spare),
            bytes_accessed=4 * width * (inner + spare) + 4 * count * tok * width,
            transcendentals=rows * inner,
        ),
        name="group",
    )(failed, holders, *map(in_hbm, (*blocks, *weights, *shares, *earlier)))


def in_hbm(array):
    return pltpu.with_memory_space_constraint(array, pltpu.HBM)


def nothing(*refs):
    pass


def come_after(value, *others):
    return pl.pallas_call(
        nothing,
        out_shape=pltpu.HBM(value.shape, value.dtype),
        in_specs=[pl.BlockSpec(memory_space=pl.ANY)] * (1 + len(others)),
        out_specs=pl.BlockSpec(memory_space=pl.ANY),
        input_output_aliases={0: 0},
        compiler_params=pltpu.CompilerParams(vmem_limit_bytes=VMEM_GRANT),
        cost_estimate=pl.CostEstimate(flops=0, bytes_accessed=0, transcendentals=0),
        name="after",
    )(*map(in_hbm, (value, *others)))


def folded_ring(length):
    return [0] + list(range(1, length, 2)) + list(range(2, length, 2))[::-1]


def by_permutes(failed, holders, tokens, expert_ids, gate_levels, weights, owners, capacity):
    tok, top = expert_ids.shape
    width = tokens.shape[1]
    order = folded_ring(owners // 4)
    steps = len(order)
    after = {a: order[(i + 1) % steps] for i, a in enumerate(order)}
    round_ring = [(d, after[d // 4] * 4 + d % 4) for d in range(owners)]
    over_y = [(d, d ^ 2) for d in range(owners)]
    over_core = [(d, d ^ 1) for d in range(owners)]
    move = lambda a, pairs: lax.ppermute(a, "expert", pairs)

    meta = jnp.concatenate([expert_ids.T, gate_levels.T >> 5, gate_levels.T & 31], axis=0)
    meta = meta.astype(jnp.bfloat16).reshape(1, 3 * top * tok)
    meta = jnp.pad(meta, ((0, 7), (0, width - 3 * top * tok)))
    held = [jnp.concatenate([tokens, meta], axis=0)]
    held.append(move(held[0], round_ring))
    across, kept, got, from_y = [], [], [], []

    def add_group(k, shares):
        blocks = (held[k], across[k], move(held[k], over_core), move(across[k], over_core))
        keep0, keep1, send, *summed = run_group(
            failed, holders, blocks, weights, shares, (), tok, top, capacity
        )
        kept.append((keep0, keep1))
        from_y.extend(move(a, over_y) for a in summed)
        return send

    across.append(move(held[0], over_y))
    send = add_group(0, ())
    for k in range(1, steps):
        last = k == steps - 1
        across.append(move(across[-1], round_ring) if last else move(held[k], over_y))
        if k == 1:
            across[1] = come_after(across[1], kept[0][0])
        if not last:
            held.append(come_after(move(held[k], round_ring), kept[k - 1][0]))
        send = come_after(send, across[k], held[min(k + 1, steps - 1)], *from_y[-2:-1])
        got.append(move(send, over_core))
        send = add_group(k, (kept[-1][1], got[-1]))
    got.append(move(come_after(send, *from_y[-2:-1]), over_core))

    f32 = lambda a: a.astype(jnp.float32)
    last = steps - 1
    summed = (f32(kept[last][1]) + f32(got[last][1])).astype(jnp.bfloat16)
    from_y.append(move(summed, over_y))
    total = lambda k: f32(kept[k][0]) + f32(got[k][0]) + f32(from_y[k])
    result = total(0)
    place = {a: i for i, a in enumerate(order)}
    for k in range(1, steps):
        home = [(d, order[(place[d // 4] - k) % steps] * 4 + d % 4) for d in range(owners)]
        result = result + f32(move(total(k).astype(jnp.bfloat16), home))
    return result.astype(jnp.bfloat16)


def shards(
    tokens,
    expert_ids,
    gate_levels,
    failed_device,
    replica_holders,
    w_gate,
    w_down,
    spare_gate,
    spare_down,
):
    owners = lax.axis_size("expert")
    tok_count, top_count = expert_ids.shape
    capacity = 2 * tok_count * top_count // owners
    my_index = lax.axis_index("expert").astype(jnp.int32)
    failed_id = failed_device[0]
    holder_row = lax.dynamic_index_in_dim(replica_holders, failed_id, 0, keepdims=False)
    holds = jnp.any(holder_row == my_index).astype(jnp.int32)
    scalars = jnp.stack([my_index, failed_id, holds])
    weights = (w_gate, w_down, spare_gate, spare_down)
    if 12 <= owners <= 32 and owners % 4 == 0 and 3 * top_count * tok_count <= tokens.shape[1]:
        return by_permutes(
            failed_device, replica_holders.T, tokens, expert_ids, gate_levels, weights, owners, capacity
        )
    codes = (expert_ids * LEVELS + gate_levels).T
    all_codes = lax.all_gather(codes, "expert", axis=0)
    all_tokens = lax.all_gather(tokens, "expert", axis=0, tiled=True)
    dense = run_experts(scalars, all_codes, all_tokens, *weights, capacity)
    return lax.psum_scatter(dense, "expert", scatter_dimension=0, tiled=True)


def solution(mesh):
    in_specs = (
        P(("group", "expert"), None),
        P(("group", "expert"), None),
        P(("group", "expert"), None),
        P(),
        P(),
        P("expert", None, None),
        P("expert", None, None),
        P("expert", None, None),
        P("expert", None, None),
    )
    out_specs = P(("group", "expert"), None)
    return jax.shard_map(shards, mesh=mesh, in_specs=in_specs, out_specs=out_specs, check_vma=False)
```

```python
import functools
import jax
import jax.numpy as jnp
from jax import lax
from jax.experimental import pallas as pl
from jax.experimental.pallas import tpu as pltpu
from jax.sharding import PartitionSpec as P

LEVELS = 1024
VMEM_GRANT = 65200 * 1024


def gated_unit(values):
    return values * (0.5 + 0.5 * jnp.tanh(0.851 * values))


def expert_kernel(
    scalars,
    codes,
    tokens,
    w_gate,
    w_down,
    spare_gate,
    spare_down,
    out,
    rows_in,
    spare_in,
    hidden,
    spare_hidden,
    rows_out,
    *,
    subs,
    sources,
    capacity,
):
    tok = codes.shape[2]
    part = sources * tok
    rows = sources * capacity
    width = tokens.shape[1]
    tile = 512
    my_id, failed_id, holds = scalars[0], scalars[1], scalars[2]
    serves = my_id != failed_id

    before = (
        lax.broadcasted_iota(jnp.int32, (tok, tok), 0)
        < lax.broadcasted_iota(jnp.int32, (tok, tok), 1)
    ).astype(jnp.bfloat16)
    row_iota = lax.broadcasted_iota(jnp.int32, (rows, tok), 0)

    def picker(code, wanted, live):
        named = ((code // LEVELS) == wanted) & live
        mask = jnp.sum(named.astype(jnp.float32), axis=1)
        level = jnp.sum(jnp.where(named, (code % LEVELS), 0).astype(jnp.float32), axis=1) / LEVELS
        rank = jnp.dot(mask.astype(jnp.bfloat16), before, preferred_element_type=jnp.float32)
        picks, weights = [], None
        for s in range(sources):
            place = jnp.where(mask[s : s + 1] > 0, rank[s : s + 1].astype(jnp.int32) + s * capacity, -1)
            hit = row_iota == place
            scaled = jnp.sum(jnp.where(hit, level[s : s + 1], 0.0), axis=1, keepdims=True)
            weights = scaled if weights is None else weights + scaled
            picks.append(hit.astype(jnp.float32).astype(jnp.bfloat16))
        return jnp.concatenate(picks, axis=1), weights

    picks, weights, spare_weights = [], [], []
    for j in range(subs):
        code = codes[j * sources : (j + 1) * sources]
        pick, weight = picker(code, my_id, serves)
        spare_pick, spare_weight = picker(code, failed_id, holds > 0)
        both = jnp.concatenate([pick, spare_pick], axis=0)
        picks.append(both)
        weights.append(weight)
        spare_weights.append(spare_weight)
        for n in range(0, width, tile):
            got = jnp.dot(
                both, tokens[j * part : (j + 1) * part, n : n + tile], preferred_element_type=jnp.float32
            ).astype(jnp.bfloat16)
            rows_in[j * rows : (j + 1) * rows, n : n + tile] = got[:rows]
            spare_in[j * rows : (j + 1) * rows, n : n + tile] = got[rows:]

    for n in range(0, hidden.shape[1], tile):
        hidden[:, n : n + tile] = gated_unit(
            jnp.dot(rows_in[...], w_gate[0, :, n : n + tile], preferred_element_type=jnp.float32)
        ).astype(jnp.bfloat16)
    for n in range(0, width, tile):
        result = jnp.dot(hidden[...], w_down[0, :, n : n + tile], preferred_element_type=jnp.float32)
        result = result.astype(jnp.bfloat16).astype(jnp.float32)
        for j in range(subs):
            rows_out[j, :rows, n : n + tile] = (result[j * rows : (j + 1) * rows] * weights[j]).astype(
                jnp.bfloat16
            )

    @pl.when(holds > 0)
    def _():
        spare_hidden[...] = gated_unit(
            jnp.dot(spare_in[...], spare_gate[0], preferred_element_type=jnp.float32)
        ).astype(jnp.bfloat16)
        for n in range(0, width, tile):
            result = jnp.dot(
                spare_hidden[...], spare_down[0, :, n : n + tile], preferred_element_type=jnp.float32
            )
            for j in range(subs):
                rows_out[j, rows:, n : n + tile] = (
                    result[j * rows : (j + 1) * rows] * spare_weights[j]
                ).astype(jnp.bfloat16)

    @pl.when(holds <= 0)
    def _():
        rows_out[:, rows:, :] = jnp.zeros((subs, rows, width), jnp.bfloat16)

    for j in range(subs):
        for n in range(0, width, tile):
            out[j * part : (j + 1) * part, n : n + tile] = lax.dot_general(
                picks[j],
                rows_out[j, :, n : n + tile],
                (((0,), (0,)), ((), ())),
                preferred_element_type=jnp.float32,
            ).astype(jnp.bfloat16)


def run_experts(scalars, codes, tokens, w_gate, w_down, spare_gate, spare_down, capacity):
    owners, top, tok = codes.shape
    width, inner, spare = w_gate.shape[1], w_gate.shape[2], spare_gate.shape[2]
    sources = max(1, 128 // capacity)
    subs = 2 if sources * tok <= 512 else 1
    step = subs * sources
    rows = sources * capacity
    whole = lambda a: pl.BlockSpec(a.shape, lambda i: (0, 0, 0), pipeline_mode=pl.Buffered(1))
    return pl.pallas_call(
        functools.partial(expert_kernel, subs=subs, sources=sources, capacity=capacity),
        grid=(owners // step,),
        out_shape=jax.ShapeDtypeStruct((owners * tok, width), jnp.bfloat16),
        in_specs=[
            pl.BlockSpec(memory_space=pltpu.SMEM),
            pl.BlockSpec((step, top, tok), lambda i: (i, 0, 0)),
            pl.BlockSpec((step * tok, width), lambda i: (i, 0)),
            whole(w_gate),
            whole(w_down),
            whole(spare_gate),
            whole(spare_down),
        ],
        out_specs=pl.BlockSpec((step * tok, width), lambda i: (i, 0)),
        scratch_shapes=[
            pltpu.VMEM((subs * rows, width), jnp.bfloat16),
            pltpu.VMEM((subs * rows, width), jnp.bfloat16),
            pltpu.VMEM((subs * rows, inner), jnp.bfloat16),
            pltpu.VMEM((subs * rows, spare), jnp.bfloat16),
            pltpu.VMEM((subs, 2 * rows, width), jnp.bfloat16),
        ],
        compiler_params=pltpu.CompilerParams(vmem_limit_bytes=56 * 1024 * 1024),
        cost_estimate=pl.CostEstimate(
            flops=owners * capacity * 4 * width * (inner + spare),
            bytes_accessed=4 * width * (inner + spare) + 4 * owners * tok * width,
            transcendentals=owners * capacity * inner,
        ),
        name="experts",
    )(scalars, codes, tokens, w_gate, w_down, spare_gate, spare_down)


def group_kernel(failed, holders, *refs, others, adds, tok, top, capacity):
    blocks, weights_hbm, shares, refs = refs[:4], refs[4:8], refs[8 : 8 + 2 * adds], refs[8 + 2 * adds + others :]
    keep0, keep1, send = refs[:3]
    far, refs = refs[3 : 3 + adds], refs[3 + adds :]
    held, w_gate, w_down, spare_gate, spare_down = refs[:5]
    rows_in, spare_in, hidden, spare_hidden, rows_out, dense, summed, fetched, stored = refs[5:]
    width, inner = w_gate.shape
    tile = 512
    my_id, failed_id = lax.axis_index("expert"), failed[0]
    holds = holders[0, failed_id] == my_id
    for j in range(1, holders.shape[0]):
        holds = holds | (holders[j, failed_id] == my_id)
    copies = []

    def fetch(source, target, start=True):
        copy = pltpu.make_async_copy(source, target, fetched.at[len(copies)])
        if start:
            copy.start()
        copies.append(copy)
        return copy

    gate_hbm, down_hbm, spare_gate_hbm, spare_down_hbm = weights_hbm
    block_copies = [fetch(block, held.at[s]) for s, block in enumerate(blocks)]
    gate_copies = [
        fetch(gate_hbm.at[0, :, n : n + tile], w_gate.at[:, n : n + tile]) for n in range(0, inner, tile)
    ]
    share_copies = []
    if adds:
        share_copies = [fetch(shares[0], summed.at[0]), fetch(shares[1].at[1], summed.at[1])]
    spare_copies = [
        fetch(spare_gate_hbm.at[0], spare_gate, False),
        fetch(spare_down_hbm.at[0], spare_down, False),
    ]

    @pl.when(holds)
    def _():
        for copy in spare_copies:
            copy.start()

    down_copies = [
        fetch(down_hbm.at[0, :, n : n + tile], w_down.at[:, n : n + tile]) for n in range(0, width, tile)
    ]

    count = len(blocks)
    before = (
        lax.broadcasted_iota(jnp.int32, (tok, tok), 0)
        < lax.broadcasted_iota(jnp.int32, (tok, tok), 1)
    ).astype(jnp.float32).astype(jnp.bfloat16)
    own = lax.broadcasted_iota(jnp.int32, (2 * count, tok), 0) < count
    wanted = jnp.where(own, my_id, failed_id).astype(jnp.float32)
    serves = jnp.where(my_id != failed_id, 1.0, 0.0)
    live = jnp.where(own, serves, jnp.where(holds, 1.0, 0.0))
    slots = 2 * capacity
    row_iota = lax.broadcasted_iota(jnp.int32, (slots, tok), 0)
    lane_iota = lax.broadcasted_iota(jnp.int32, (tok, slots), 1)

    for copy in block_copies:
        copy.wait()
    meta = jnp.concatenate([held[s, tok : tok + 8, :].astype(jnp.float32)[:1] for s in range(count)] * 2, axis=0)
    mask = jnp.zeros((2 * count, tok), jnp.float32)
    level = jnp.zeros((2 * count, tok), jnp.float32)
    for k in range(top):
        named = jnp.where(meta[:, k * tok : (k + 1) * tok] == wanted, live, 0.0)
        high = meta[:, (top + k) * tok : (top + k + 1) * tok]
        low = meta[:, (2 * top + k) * tok : (2 * top + k + 1) * tok]
        mask = mask + named
        level = level + named * ((high * 32.0 + low) / LEVELS)
    rank = jnp.dot(mask.astype(jnp.bfloat16), before, preferred_element_type=jnp.float32)
    place = jnp.where(mask > 0, rank + jnp.where(own, 0.0, float(capacity)), -1.0)
    place_rows = place.astype(jnp.int32)
    place_columns = place.T.astype(jnp.int32)

    spreads, weights = [], []
    for s in range(count):
        here, there = place_rows[s : s + 1], place_rows[count + s : count + s + 1]
        hit_here, hit_there = row_iota == here, row_iota == there
        pick = jnp.where(hit_here | hit_there, 1.0, 0.0).astype(jnp.bfloat16)
        weights.append(
            jnp.sum(
                jnp.where(hit_here, level[s : s + 1], 0.0)
                + jnp.where(hit_there, level[count + s : count + s + 1], 0.0),
                axis=1,
                keepdims=True,
            )
        )
        here, there = place_columns[:, s : s + 1], place_columns[:, count + s : count + s + 1]
        spreads.append(jnp.where((lane_iota == here) | (lane_iota == there), 1.0, 0.0).astype(jnp.bfloat16))
        for n in range(0, width, tile):
            got = jnp.dot(pick, held[s, :tok, n : n + tile], preferred_element_type=jnp.float32).astype(
                jnp.bfloat16
            )
            rows_in[s * capacity : (s + 1) * capacity, n : n + tile] = got[:capacity]
            spare_in[s * capacity : (s + 1) * capacity, n : n + tile] = got[capacity:]

    for i, n in enumerate(range(0, inner, tile)):
        gate_copies[i].wait()
        hidden[:, n : n + tile] = gated_unit(
            jnp.dot(rows_in[...], w_gate[:, n : n + tile], preferred_element_type=jnp.float32)
        ).astype(jnp.bfloat16)
    stores = []
    if adds:
        for copy in share_copies:
            copy.wait()
        total = summed[0].astype(jnp.float32) + summed[1].astype(jnp.float32)
        summed[0] = total.astype(jnp.bfloat16)
        stores.append(pltpu.make_async_copy(summed.at[0], far[0], stored.at[0]))
        stores[0].start()

    @pl.when(holds)
    def _():
        for copy in spare_copies:
            copy.wait()
        spare_hidden[...] = gated_unit(
            jnp.dot(spare_in[...], spare_gate[...], preferred_element_type=jnp.float32)
        ).astype(jnp.bfloat16)
        for n in range(0, width, tile):
            result = jnp.dot(
                spare_hidden[...], spare_down[:, n : n + tile], preferred_element_type=jnp.float32
            )
            for s in range(count):
                rows_out[s, capacity:, n : n + tile] = (
                    result[s * capacity : (s + 1) * capacity] * weights[s][capacity:]
                ).astype(jnp.bfloat16)

    @pl.when(jnp.logical_not(holds))
    def _():
        rows_out[:, capacity:, :] = jnp.zeros((count, capacity, width), jnp.bfloat16)

    for i, n in enumerate(range(0, width, tile)):
        down_copies[i].wait()
        result = jnp.dot(hidden[...], w_down[:, n : n + tile], preferred_element_type=jnp.float32)
        result = result.astype(jnp.bfloat16).astype(jnp.float32)
        for s in range(count):
            rows_out[s, :capacity, n : n + tile] = (
                result[s * capacity : (s + 1) * capacity] * weights[s][:capacity]
            ).astype(jnp.bfloat16)
            dense[s, :, n : n + tile] = jnp.dot(
                spreads[s], rows_out[s, :, n : n + tile], preferred_element_type=jnp.float32
            ).astype(jnp.bfloat16)
            target = (keep0, keep1, send.at[0], send.at[1])[s]
            stores.append(
                pltpu.make_async_copy(
                    dense.at[s, :, n : n + tile], target.at[:, n : n + tile], stored.at[len(stores)]
                )
            )
            stores[-1].start()
    for copy in stores:
        copy.wait()


def run_group(failed, holders, blocks, weights, shares, earlier, tok, top, capacity):
    width, inner, spare = weights[0].shape[1], weights[0].shape[2], weights[2].shape[2]
    count, adds = len(blocks), len(shares) // 2
    rows = count * capacity
    hbm = pl.BlockSpec(memory_space=pl.ANY)
    smem = pl.BlockSpec(memory_space=pltpu.SMEM)
    block = pltpu.HBM((tok, width), jnp.bfloat16)
    return pl.pallas_call(
        functools.partial(
            group_kernel, others=len(earlier), adds=adds, tok=tok, top=top, capacity=capacity
        ),
        out_shape=(block, block, pltpu.HBM((2, tok, width), jnp.bfloat16)) + (block,) * adds,
        in_specs=[smem, smem] + [hbm] * (count + 4 + len(shares) + len(earlier)),
        out_specs=(hbm,) * (3 + adds),
        scratch_shapes=[
            pltpu.VMEM((count, *blocks[0].shape), jnp.bfloat16),
            pltpu.VMEM((width, inner), jnp.bfloat16),
            pltpu.VMEM((inner, width), jnp.bfloat16),
            pltpu.VMEM((width, spare), jnp.bfloat16),
            pltpu.VMEM((spare, width), jnp.bfloat16),
            pltpu.VMEM((rows, width), jnp.bfloat16),
            pltpu.VMEM((rows, width), jnp.bfloat16),
            pltpu.VMEM((rows, inner), jnp.bfloat16),
            pltpu.VMEM((rows, spare), jnp.bfloat16),
            pltpu.VMEM((count, 2 * capacity, width), jnp.bfloat16),
            pltpu.VMEM((count, tok, width), jnp.bfloat16),
            pltpu.VMEM((2, tok, width), jnp.bfloat16),
            pltpu.SemaphoreType.DMA((count + inner // 512 + width // 512 + 4,)),
            pltpu.SemaphoreType.DMA((1 + count * (width // 512),)),
        ],
        compiler_params=pltpu.CompilerParams(vmem_limit_bytes=VMEM_GRANT),
        cost_estimate=pl.CostEstimate(
            flops=rows * 4 * width * (inner + spare),
            bytes_accessed=4 * width * (inner + spare) + 4 * count * tok * width,
            transcendentals=rows * inner,
        ),
        name="group",
    )(failed, holders, *map(in_hbm, (*blocks, *weights, *shares, *earlier)))


def in_hbm(array):
    return pltpu.with_memory_space_constraint(array, pltpu.HBM)


def nothing(*refs):
    pass


def come_after(value, *others):
    return pl.pallas_call(
        nothing,
        out_shape=pltpu.HBM(value.shape, value.dtype),
        in_specs=[pl.BlockSpec(memory_space=pl.ANY)] * (1 + len(others)),
        out_specs=pl.BlockSpec(memory_space=pl.ANY),
        input_output_aliases={0: 0},
        compiler_params=pltpu.CompilerParams(vmem_limit_bytes=VMEM_GRANT),
        cost_estimate=pl.CostEstimate(flops=0, bytes_accessed=0, transcendentals=0),
        name="after",
    )(*map(in_hbm, (value, *others)))


def folded_ring(length):
    return [0] + list(range(1, length, 2)) + list(range(2, length, 2))[::-1]


def by_permutes(failed, holders, tokens, expert_ids, gate_levels, weights, owners, capacity):
    tok, top = expert_ids.shape
    width = tokens.shape[1]
    order = folded_ring(owners // 4)
    steps = len(order)
    after = {a: order[(i + 1) % steps] for i, a in enumerate(order)}
    round_ring = [(d, after[d // 4] * 4 + d % 4) for d in range(owners)]
    back = [(b, a) for a, b in round_ring]
    over_y = [(d, d ^ 2) for d in range(owners)]
    over_core = [(d, d ^ 1) for d in range(owners)]
    move = lambda a, pairs: lax.ppermute(a, "expert", pairs)
    f32 = lambda a: a.astype(jnp.float32)
    add = lambda a, b: (f32(a) + f32(b)).astype(jnp.bfloat16)

    meta = jnp.concatenate([expert_ids.T, gate_levels.T >> 5, gate_levels.T & 31], axis=0)
    meta = meta.astype(jnp.bfloat16).reshape(1, 3 * top * tok)
    meta = jnp.pad(meta, ((0, 7), (0, width - 3 * top * tok)))
    held = [jnp.concatenate([tokens, meta], axis=0)]
    held.append(move(held[0], round_ring))
    across, kept, got, from_y = [], [], [], []

    def add_group(k, shares, *earlier):
        blocks = (held[k], across[k], move(held[k], over_core), move(across[k], over_core))
        keep0, keep1, send, *summed = run_group(
            failed, holders, blocks, weights, shares, earlier, tok, top, capacity
        )
        kept.append((keep0, keep1))
        from_y.extend(move(a, over_y) for a in summed)
        return send

    across.append(move(held[0], over_y))
    send = add_group(0, ())
    for k in range(1, steps):
        last = k == steps - 1
        across.append(move(across[-1], round_ring) if last else move(held[k], over_y))
        if k == 1:
            across[1] = come_after(across[1], kept[0][0])
        if not last:
            held.append(come_after(move(held[k], round_ring), kept[k - 1][0]))
        send = come_after(send, across[k], held[min(k + 1, steps - 1)], *from_y[-2:-1])
        got.append(move(send, over_core))
        if last:
            share = add(kept[-1][1], got[-1][1])
            from_y.append(move(share, over_y))
            send = add_group(k, (), share)
        else:
            send = add_group(k, (kept[-1][1], got[-1]))
    got.append(move(come_after(send, *from_y[-2:-1]), over_core))
    from_y.append(move(add(kept[-1][1], got[-1][1]), over_y))

    total = lambda k: f32(kept[k][0]) + f32(got[k][0]) + f32(from_y[k])
    result = total(0) + f32(move(total(1).astype(jnp.bfloat16), back))
    passing = total(2)
    for k in range(3, steps):
        passing = total(k) + f32(move(passing.astype(jnp.bfloat16), round_ring))
    return (result + f32(move(passing.astype(jnp.bfloat16), round_ring))).astype(jnp.bfloat16)


def shards(
    tokens,
    expert_ids,
    gate_levels,
    failed_device,
    replica_holders,
    w_gate,
    w_down,
    spare_gate,
    spare_down,
):
    owners = lax.axis_size("expert")
    tok_count, top_count = expert_ids.shape
    capacity = 2 * tok_count * top_count // owners
    my_index = lax.axis_index("expert").astype(jnp.int32)
    failed_id = failed_device[0]
    holder_row = lax.dynamic_index_in_dim(replica_holders, failed_id, 0, keepdims=False)
    holds = jnp.any(holder_row == my_index).astype(jnp.int32)
    scalars = jnp.stack([my_index, failed_id, holds])
    weights = (w_gate, w_down, spare_gate, spare_down)
    if 12 <= owners <= 32 and owners % 4 == 0 and 3 * top_count * tok_count <= tokens.shape[1]:
        return by_permutes(
            failed_device, replica_holders.T, tokens, expert_ids, gate_levels, weights, owners, capacity
        )
    codes = (expert_ids * LEVELS + gate_levels).T
    all_codes = lax.all_gather(codes, "expert", axis=0)
    all_tokens = lax.all_gather(tokens, "expert", axis=0, tiled=True)
    dense = run_experts(scalars, all_codes, all_tokens, *weights, capacity)
    return lax.psum_scatter(dense, "expert", scatter_dimension=0, tiled=True)


def solution(mesh):
    in_specs = (
        P(("group", "expert"), None),
        P(("group", "expert"), None),
        P(("group", "expert"), None),
        P(),
        P(),
        P("expert", None, None),
        P("expert", None, None),
        P("expert", None, None),
        P("expert", None, None),
    )
    out_specs = P(("group", "expert"), None)
    return jax.shard_map(shards, mesh=mesh, in_specs=in_specs, out_specs=out_specs, check_vma=False)
```

```python
import functools
import jax
import jax.numpy as jnp
from jax import lax
from jax.experimental import pallas as pl
from jax.experimental.pallas import tpu as pltpu
from jax.sharding import PartitionSpec as P

LEVELS = 1024
VMEM_GRANT = 65200 * 1024


def gated_unit(values):
    return values * (0.5 + 0.5 * jnp.tanh(0.851 * values))


def expert_kernel(
    scalars,
    codes,
    tokens,
    w_gate,
    w_down,
    spare_gate,
    spare_down,
    out,
    rows_in,
    spare_in,
    hidden,
    spare_hidden,
    rows_out,
    *,
    subs,
    sources,
    capacity,
):
    tok = codes.shape[2]
    part = sources * tok
    rows = sources * capacity
    width = tokens.shape[1]
    tile = 512
    my_id, failed_id, holds = scalars[0], scalars[1], scalars[2]
    serves = my_id != failed_id

    before = (
        lax.broadcasted_iota(jnp.int32, (tok, tok), 0)
        < lax.broadcasted_iota(jnp.int32, (tok, tok), 1)
    ).astype(jnp.bfloat16)
    row_iota = lax.broadcasted_iota(jnp.int32, (rows, tok), 0)

    def picker(code, wanted, live):
        named = ((code // LEVELS) == wanted) & live
        mask = jnp.sum(named.astype(jnp.float32), axis=1)
        level = jnp.sum(jnp.where(named, (code % LEVELS), 0).astype(jnp.float32), axis=1) / LEVELS
        rank = jnp.dot(mask.astype(jnp.bfloat16), before, preferred_element_type=jnp.float32)
        picks, weights = [], None
        for s in range(sources):
            place = jnp.where(mask[s : s + 1] > 0, rank[s : s + 1].astype(jnp.int32) + s * capacity, -1)
            hit = row_iota == place
            scaled = jnp.sum(jnp.where(hit, level[s : s + 1], 0.0), axis=1, keepdims=True)
            weights = scaled if weights is None else weights + scaled
            picks.append(hit.astype(jnp.float32).astype(jnp.bfloat16))
        return jnp.concatenate(picks, axis=1), weights

    picks, weights, spare_weights = [], [], []
    for j in range(subs):
        code = codes[j * sources : (j + 1) * sources]
        pick, weight = picker(code, my_id, serves)
        spare_pick, spare_weight = picker(code, failed_id, holds > 0)
        both = jnp.concatenate([pick, spare_pick], axis=0)
        picks.append(both)
        weights.append(weight)
        spare_weights.append(spare_weight)
        for n in range(0, width, tile):
            got = jnp.dot(
                both, tokens[j * part : (j + 1) * part, n : n + tile], preferred_element_type=jnp.float32
            ).astype(jnp.bfloat16)
            rows_in[j * rows : (j + 1) * rows, n : n + tile] = got[:rows]
            spare_in[j * rows : (j + 1) * rows, n : n + tile] = got[rows:]

    for n in range(0, hidden.shape[1], tile):
        hidden[:, n : n + tile] = gated_unit(
            jnp.dot(rows_in[...], w_gate[0, :, n : n + tile], preferred_element_type=jnp.float32)
        ).astype(jnp.bfloat16)
    for n in range(0, width, tile):
        result = jnp.dot(hidden[...], w_down[0, :, n : n + tile], preferred_element_type=jnp.float32)
        result = result.astype(jnp.bfloat16).astype(jnp.float32)
        for j in range(subs):
            rows_out[j, :rows, n : n + tile] = (result[j * rows : (j + 1) * rows] * weights[j]).astype(
                jnp.bfloat16
            )

    @pl.when(holds > 0)
    def _():
        spare_hidden[...] = gated_unit(
            jnp.dot(spare_in[...], spare_gate[0], preferred_element_type=jnp.float32)
        ).astype(jnp.bfloat16)
        for n in range(0, width, tile):
            result = jnp.dot(
                spare_hidden[...], spare_down[0, :, n : n + tile], preferred_element_type=jnp.float32
            )
            for j in range(subs):
                rows_out[j, rows:, n : n + tile] = (
                    result[j * rows : (j + 1) * rows] * spare_weights[j]
                ).astype(jnp.bfloat16)

    @pl.when(holds <= 0)
    def _():
        rows_out[:, rows:, :] = jnp.zeros((subs, rows, width), jnp.bfloat16)

    for j in range(subs):
        for n in range(0, width, tile):
            out[j * part : (j + 1) * part, n : n + tile] = lax.dot_general(
                picks[j],
                rows_out[j, :, n : n + tile],
                (((0,), (0,)), ((), ())),
                preferred_element_type=jnp.float32,
            ).astype(jnp.bfloat16)


def run_experts(scalars, codes, tokens, w_gate, w_down, spare_gate, spare_down, capacity):
    owners, top, tok = codes.shape
    width, inner, spare = w_gate.shape[1], w_gate.shape[2], spare_gate.shape[2]
    sources = max(1, 128 // capacity)
    subs = 2 if sources * tok <= 512 else 1
    step = subs * sources
    rows = sources * capacity
    whole = lambda a: pl.BlockSpec(a.shape, lambda i: (0, 0, 0), pipeline_mode=pl.Buffered(1))
    return pl.pallas_call(
        functools.partial(expert_kernel, subs=subs, sources=sources, capacity=capacity),
        grid=(owners // step,),
        out_shape=jax.ShapeDtypeStruct((owners * tok, width), jnp.bfloat16),
        in_specs=[
            pl.BlockSpec(memory_space=pltpu.SMEM),
            pl.BlockSpec((step, top, tok), lambda i: (i, 0, 0)),
            pl.BlockSpec((step * tok, width), lambda i: (i, 0)),
            whole(w_gate),
            whole(w_down),
            whole(spare_gate),
            whole(spare_down),
        ],
        out_specs=pl.BlockSpec((step * tok, width), lambda i: (i, 0)),
        scratch_shapes=[
            pltpu.VMEM((subs * rows, width), jnp.bfloat16),
            pltpu.VMEM((subs * rows, width), jnp.bfloat16),
            pltpu.VMEM((subs * rows, inner), jnp.bfloat16),
            pltpu.VMEM((subs * rows, spare), jnp.bfloat16),
            pltpu.VMEM((subs, 2 * rows, width), jnp.bfloat16),
        ],
        compiler_params=pltpu.CompilerParams(vmem_limit_bytes=56 * 1024 * 1024),
        cost_estimate=pl.CostEstimate(
            flops=owners * capacity * 4 * width * (inner + spare),
            bytes_accessed=4 * width * (inner + spare) + 4 * owners * tok * width,
            transcendentals=owners * capacity * inner,
        ),
        name="experts",
    )(scalars, codes, tokens, w_gate, w_down, spare_gate, spare_down)


def group_kernel(failed, holders, *refs, others, tok, top, capacity):
    blocks, weights_hbm, refs = refs[:4], refs[4:8], refs[8 + others :]
    keep0, keep1, send, held, w_gate, w_down, spare_gate, spare_down = refs[:8]
    rows_in, spare_in, hidden, spare_hidden, rows_out, dense, fetched, stored = refs[8:]
    width, inner = w_gate.shape
    tile = 512
    my_id, failed_id = lax.axis_index("expert"), failed[0]
    holds = holders[0, failed_id] == my_id
    for j in range(1, holders.shape[0]):
        holds = holds | (holders[j, failed_id] == my_id)
    copies = []

    def fetch(source, target, start=True):
        copy = pltpu.make_async_copy(source, target, fetched.at[len(copies)])
        if start:
            copy.start()
        copies.append(copy)
        return copy

    gate_hbm, down_hbm, spare_gate_hbm, spare_down_hbm = weights_hbm
    block_copies = [fetch(block, held.at[s]) for s, block in enumerate(blocks)]
    gate_copies = [
        fetch(gate_hbm.at[0, :, n : n + tile], w_gate.at[:, n : n + tile]) for n in range(0, inner, tile)
    ]
    spare_copies = [
        fetch(spare_gate_hbm.at[0], spare_gate, False),
        fetch(spare_down_hbm.at[0], spare_down, False),
    ]

    @pl.when(holds)
    def _():
        for copy in spare_copies:
            copy.start()

    down_copies = [
        fetch(down_hbm.at[0, :, n : n + tile], w_down.at[:, n : n + tile]) for n in range(0, width, tile)
    ]

    count = len(blocks)
    before = (
        lax.broadcasted_iota(jnp.int32, (tok, tok), 0)
        < lax.broadcasted_iota(jnp.int32, (tok, tok), 1)
    ).astype(jnp.float32).astype(jnp.bfloat16)
    own = lax.broadcasted_iota(jnp.int32, (2 * count, tok), 0) < count
    wanted = jnp.where(own, my_id, failed_id).astype(jnp.float32)
    serves = jnp.where(my_id != failed_id, 1.0, 0.0)
    live = jnp.where(own, serves, jnp.where(holds, 1.0, 0.0))
    slots = 2 * capacity
    row_iota = lax.broadcasted_iota(jnp.int32, (slots, tok), 0)
    lane_iota = lax.broadcasted_iota(jnp.int32, (tok, slots), 1)

    for copy in block_copies:
        copy.wait()
    meta = jnp.concatenate([held[s, tok : tok + 8, :].astype(jnp.float32)[:1] for s in range(count)] * 2, axis=0)
    mask = jnp.zeros((2 * count, tok), jnp.float32)
    level = jnp.zeros((2 * count, tok), jnp.float32)
    for k in range(top):
        named = jnp.where(meta[:, k * tok : (k + 1) * tok] == wanted, live, 0.0)
        high = meta[:, (top + k) * tok : (top + k + 1) * tok]
        low = meta[:, (2 * top + k) * tok : (2 * top + k + 1) * tok]
        mask = mask + named
        level = level + named * ((high * 32.0 + low) / LEVELS)
    rank = jnp.dot(mask.astype(jnp.bfloat16), before, preferred_element_type=jnp.float32)
    place = jnp.where(mask > 0, rank + jnp.where(own, 0.0, float(capacity)), -1.0)
    place_rows = place.astype(jnp.int32)
    place_columns = place.T.astype(jnp.int32)

    spreads, weights = [], []
    for s in range(count):
        here, there = place_rows[s : s + 1], place_rows[count + s : count + s + 1]
        hit_here, hit_there = row_iota == here, row_iota == there
        pick = jnp.where(hit_here | hit_there, 1.0, 0.0).astype(jnp.bfloat16)
        weights.append(
            jnp.sum(
                jnp.where(hit_here, level[s : s + 1], 0.0)
                + jnp.where(hit_there, level[count + s : count + s + 1], 0.0),
                axis=1,
                keepdims=True,
            )
        )
        here, there = place_columns[:, s : s + 1], place_columns[:, count + s : count + s + 1]
        spreads.append(jnp.where((lane_iota == here) | (lane_iota == there), 1.0, 0.0).astype(jnp.bfloat16))
        for n in range(0, width, tile):
            got = jnp.dot(pick, held[s, :tok, n : n + tile], preferred_element_type=jnp.float32).astype(
                jnp.bfloat16
            )
            rows_in[s * capacity : (s + 1) * capacity, n : n + tile] = got[:capacity]
            spare_in[s * capacity : (s + 1) * capacity, n : n + tile] = got[capacity:]

    for i, n in enumerate(range(0, inner, tile)):
        gate_copies[i].wait()
        hidden[:, n : n + tile] = gated_unit(
            jnp.dot(rows_in[...], w_gate[:, n : n + tile], preferred_element_type=jnp.float32)
        ).astype(jnp.bfloat16)

    @pl.when(holds)
    def _():
        for copy in spare_copies:
            copy.wait()
        spare_hidden[...] = gated_unit(
            jnp.dot(spare_in[...], spare_gate[...], preferred_element_type=jnp.float32)
        ).astype(jnp.bfloat16)
        for n in range(0, width, tile):
            result = jnp.dot(
                spare_hidden[...], spare_down[:, n : n + tile], preferred_element_type=jnp.float32
            )
            for s in range(count):
                rows_out[s, capacity:, n : n + tile] = (
                    result[s * capacity : (s + 1) * capacity] * weights[s][capacity:]
                ).astype(jnp.bfloat16)

    @pl.when(jnp.logical_not(holds))
    def _():
        rows_out[:, capacity:, :] = jnp.zeros((count, capacity, width), jnp.bfloat16)

    stores = []
    for i, n in enumerate(range(0, width, tile)):
        down_copies[i].wait()
        result = jnp.dot(hidden[...], w_down[:, n : n + tile], preferred_element_type=jnp.float32)
        result = result.astype(jnp.bfloat16).astype(jnp.float32)
        for s in range(count):
            rows_out[s, :capacity, n : n + tile] = (
                result[s * capacity : (s + 1) * capacity] * weights[s][:capacity]
            ).astype(jnp.bfloat16)
            dense[s, :, n : n + tile] = jnp.dot(
                spreads[s], rows_out[s, :, n : n + tile], preferred_element_type=jnp.float32
            ).astype(jnp.bfloat16)
            target = (keep0, keep1, send.at[0], send.at[1])[s]
            stores.append(
                pltpu.make_async_copy(
                    dense.at[s, :, n : n + tile], target.at[:, n : n + tile], stored.at[len(stores)]
                )
            )
            stores[-1].start()
    for copy in stores:
        copy.wait()


def run_group(failed, holders, blocks, weights, earlier, tok, top, capacity):
    width, inner, spare = weights[0].shape[1], weights[0].shape[2], weights[2].shape[2]
    count = len(blocks)
    rows = count * capacity
    hbm = pl.BlockSpec(memory_space=pl.ANY)
    smem = pl.BlockSpec(memory_space=pltpu.SMEM)
    block = pltpu.HBM((tok, width), jnp.bfloat16)
    return pl.pallas_call(
        functools.partial(
            group_kernel, others=len(earlier), tok=tok, top=top, capacity=capacity
        ),
        out_shape=(block, block, pltpu.HBM((2, tok, width), jnp.bfloat16)),
        in_specs=[smem, smem] + [hbm] * (count + 4 + len(earlier)),
        out_specs=(hbm, hbm, hbm),
        scratch_shapes=[
            pltpu.VMEM((count, *blocks[0].shape), jnp.bfloat16),
            pltpu.VMEM((width, inner), jnp.bfloat16),
            pltpu.VMEM((inner, width), jnp.bfloat16),
            pltpu.VMEM((width, spare), jnp.bfloat16),
            pltpu.VMEM((spare, width), jnp.bfloat16),
            pltpu.VMEM((rows, width), jnp.bfloat16),
            pltpu.VMEM((rows, width), jnp.bfloat16),
            pltpu.VMEM((rows, inner), jnp.bfloat16),
            pltpu.VMEM((rows, spare), jnp.bfloat16),
            pltpu.VMEM((count, 2 * capacity, width), jnp.bfloat16),
            pltpu.VMEM((count, tok, width), jnp.bfloat16),
            pltpu.SemaphoreType.DMA((count + inner // 512 + width // 512 + 2,)),
            pltpu.SemaphoreType.DMA((count * (width // 512),)),
        ],
        compiler_params=pltpu.CompilerParams(vmem_limit_bytes=VMEM_GRANT),
        cost_estimate=pl.CostEstimate(
            flops=rows * 4 * width * (inner + spare),
            bytes_accessed=4 * width * (inner + spare) + 4 * count * tok * width,
            transcendentals=rows * inner,
        ),
        name="group",
    )(failed, holders, *map(in_hbm, (*blocks, *weights, *earlier)))


def in_hbm(array):
    return pltpu.with_memory_space_constraint(array, pltpu.HBM)


def nothing(*refs):
    pass


def come_after(value, *others):
    return pl.pallas_call(
        nothing,
        out_shape=pltpu.HBM(value.shape, value.dtype),
        in_specs=[pl.BlockSpec(memory_space=pl.ANY)] * (1 + len(others)),
        out_specs=pl.BlockSpec(memory_space=pl.ANY),
        input_output_aliases={0: 0},
        compiler_params=pltpu.CompilerParams(vmem_limit_bytes=VMEM_GRANT),
        cost_estimate=pl.CostEstimate(flops=0, bytes_accessed=0, transcendentals=0),
        name="after",
    )(*map(in_hbm, (value, *others)))


def sum_kernel(*refs, plan):
    terms = [term for sum_of in plan for term in sum_of]
    inputs = 1 + max(i for i, _ in terms)
    sources, outs, (parts, done, fetched, stored) = refs[:inputs], refs[inputs:-4], refs[-4:]
    half = done.shape[1] // 2
    halves = (slice(0, half), slice(half, 2 * half))
    copies = [
        [
            pltpu.make_async_copy(
                (sources[i] if lead is None else sources[i].at[lead]).at[rows],
                parts.at[t, rows],
                fetched.at[2 * t + h],
            )
            for h, rows in enumerate(halves)
        ]
        for t, (i, lead) in enumerate(terms)
    ]
    for pair in copies:
        for copy in pair:
            copy.start()
    stores = []
    at = 0
    for o, sum_of in enumerate(plan):
        for h, rows in enumerate(halves):
            for t in range(at, at + len(sum_of)):
                copies[t][h].wait()
            total = parts[at, rows].astype(jnp.float32)
            for t in range(at + 1, at + len(sum_of)):
                total = total + parts[t, rows].astype(jnp.float32)
            done[o, rows] = total.astype(jnp.bfloat16)
            stores.append(
                pltpu.make_async_copy(done.at[o, rows], outs[o].at[rows], stored.at[2 * o + h])
            )
            stores[-1].start()
        at += len(sum_of)
    for copy in stores:
        copy.wait()


def add_up(*sums):
    arrays = [array for sum_of in sums for array, _ in sum_of]
    numbers = iter(range(len(arrays)))
    plan = tuple(tuple((next(numbers), lead) for _, lead in sum_of) for sum_of in sums)
    tok, width = arrays[0].shape[-2:]
    hbm = pl.BlockSpec(memory_space=pl.ANY)
    return pl.pallas_call(
        functools.partial(sum_kernel, plan=plan),
        out_shape=(pltpu.HBM((tok, width), jnp.bfloat16),) * len(sums),
        in_specs=[hbm] * len(arrays),
        out_specs=(hbm,) * len(sums),
        scratch_shapes=[
            pltpu.VMEM((len(arrays), tok, width), jnp.bfloat16),
            pltpu.VMEM((len(sums), tok, width), jnp.bfloat16),
            pltpu.SemaphoreType.DMA((2 * len(arrays),)),
            pltpu.SemaphoreType.DMA((2 * len(sums),)),
        ],
        compiler_params=pltpu.CompilerParams(vmem_limit_bytes=VMEM_GRANT),
        cost_estimate=pl.CostEstimate(
            flops=len(arrays) * tok * width,
            bytes_accessed=2 * (len(arrays) + len(sums)) * tok * width,
            transcendentals=0,
        ),
        name="sums",
    )(*map(in_hbm, arrays))


def folded_ring(length):
    return [0] + list(range(1, length, 2)) + list(range(2, length, 2))[::-1]


def by_permutes(failed, holders, tokens, expert_ids, gate_levels, weights, owners, capacity):
    tok, top = expert_ids.shape
    width = tokens.shape[1]
    order = folded_ring(owners // 4)
    steps = len(order)
    after = {a: order[(i + 1) % steps] for i, a in enumerate(order)}
    round_ring = [(d, after[d // 4] * 4 + d % 4) for d in range(owners)]
    over_y = [(d, d ^ 2) for d in range(owners)]
    over_core = [(d, d ^ 1) for d in range(owners)]
    move = lambda a, pairs: lax.ppermute(a, "expert", pairs)

    meta = jnp.concatenate([expert_ids.T, gate_levels.T >> 5, gate_levels.T & 31], axis=0)
    meta = meta.astype(jnp.bfloat16).reshape(1, 3 * top * tok)
    meta = jnp.pad(meta, ((0, 7), (0, width - 3 * top * tok)))
    held = [jnp.concatenate([tokens, meta], axis=0)]
    held.append(move(held[0], round_ring))
    across, kept, got = [], [], []
    last = steps - 1

    def add_group(k, *earlier):
        blocks = (held[k], across[k], move(held[k], over_core), move(across[k], over_core))
        keep0, keep1, send = run_group(failed, holders, blocks, weights, earlier, tok, top, capacity)
        kept.append((keep0, keep1))
        return send

    def share(k):
        return [(kept[k][1], None), (got[k], 1)]

    def total(k, *more):
        return [(kept[k][0], None), (got[k], 0)] + [(a, None) for a in more]

    across.append(move(held[0], over_y))
    send = add_group(0)
    far, from_y, arrived = kept[0][0], None, ()
    for k in range(1, steps):
        across.append(move(across[-1], round_ring) if k == last else move(held[k], over_y))
        if k == 1:
            across[1] = come_after(across[1], kept[0][0])
        if k < last:
            held.append(come_after(move(held[k], round_ring), kept[k - 1][0]))
        before = () if from_y is None else (from_y,)
        got.append(move(come_after(send, across[k], held[min(k + 1, last)], *before), over_core))
        if k == 2:
            (far,) = add_up(share(1))
        elif k > 2:
            far, passing = add_up(share(k - 1), total(k - 2, from_y, *arrived))
            arrived = (move(passing, round_ring),)
        if k > 1:
            from_y = move(far, over_y)
        send = add_group(k, far)
    got.append(move(come_after(send, from_y, *arrived), over_core))
    (passing,) = add_up(total(last - 1, from_y, *arrived))
    arrived = move(passing, round_ring)
    (far,) = add_up(share(last))
    (passing,) = add_up(total(last, move(far, over_y), arrived))
    arrived = move(passing, round_ring)
    (far,) = add_up(share(0))
    from_y = move(come_after(far, passing), over_y)
    return add_up(total(0, from_y, arrived))[0]


def shards(
    tokens,
    expert_ids,
    gate_levels,
    failed_device,
    replica_holders,
    w_gate,
    w_down,
    spare_gate,
    spare_down,
):
    owners = lax.axis_size("expert")
    tok_count, top_count = expert_ids.shape
    capacity = 2 * tok_count * top_count // owners
    my_index = lax.axis_index("expert").astype(jnp.int32)
    failed_id = failed_device[0]
    holder_row = lax.dynamic_index_in_dim(replica_holders, failed_id, 0, keepdims=False)
    holds = jnp.any(holder_row == my_index).astype(jnp.int32)
    scalars = jnp.stack([my_index, failed_id, holds])
    weights = (w_gate, w_down, spare_gate, spare_down)
    if 12 <= owners <= 32 and owners % 4 == 0 and 3 * top_count * tok_count <= tokens.shape[1]:
        return by_permutes(
            failed_device, replica_holders.T, tokens, expert_ids, gate_levels, weights, owners, capacity
        )
    codes = (expert_ids * LEVELS + gate_levels).T
    all_codes = lax.all_gather(codes, "expert", axis=0)
    all_tokens = lax.all_gather(tokens, "expert", axis=0, tiled=True)
    dense = run_experts(scalars, all_codes, all_tokens, *weights, capacity)
    return lax.psum_scatter(dense, "expert", scatter_dimension=0, tiled=True)


def solution(mesh):
    in_specs = (
        P(("group", "expert"), None),
        P(("group", "expert"), None),
        P(("group", "expert"), None),
        P(),
        P(),
        P("expert", None, None),
        P("expert", None, None),
        P("expert", None, None),
        P("expert", None, None),
    )
    out_specs = P(("group", "expert"), None)
    return jax.shard_map(shards, mesh=mesh, in_specs=in_specs, out_specs=out_specs, check_vma=False)
```

```python
import functools
import jax
import jax.numpy as jnp
from jax import lax
from jax.experimental import pallas as pl
from jax.experimental.pallas import tpu as pltpu
from jax.sharding import PartitionSpec as P

LEVELS = 1024
VMEM_GRANT = 65200 * 1024


def gated_unit(values):
    return values * (0.5 + 0.5 * jnp.tanh(0.851 * values))


def expert_kernel(
    scalars,
    codes,
    tokens,
    w_gate,
    w_down,
    spare_gate,
    spare_down,
    out,
    rows_in,
    spare_in,
    hidden,
    spare_hidden,
    rows_out,
    *,
    subs,
    sources,
    capacity,
):
    tok = codes.shape[2]
    part = sources * tok
    rows = sources * capacity
    width = tokens.shape[1]
    tile = 512
    my_id, failed_id, holds = scalars[0], scalars[1], scalars[2]
    serves = my_id != failed_id

    before = (
        lax.broadcasted_iota(jnp.int32, (tok, tok), 0)
        < lax.broadcasted_iota(jnp.int32, (tok, tok), 1)
    ).astype(jnp.bfloat16)
    row_iota = lax.broadcasted_iota(jnp.int32, (rows, tok), 0)

    def picker(code, wanted, live):
        named = ((code // LEVELS) == wanted) & live
        mask = jnp.sum(named.astype(jnp.float32), axis=1)
        level = jnp.sum(jnp.where(named, (code % LEVELS), 0).astype(jnp.float32), axis=1) / LEVELS
        rank = jnp.dot(mask.astype(jnp.bfloat16), before, preferred_element_type=jnp.float32)
        picks, weights = [], None
        for s in range(sources):
            place = jnp.where(mask[s : s + 1] > 0, rank[s : s + 1].astype(jnp.int32) + s * capacity, -1)
            hit = row_iota == place
            scaled = jnp.sum(jnp.where(hit, level[s : s + 1], 0.0), axis=1, keepdims=True)
            weights = scaled if weights is None else weights + scaled
            picks.append(hit.astype(jnp.float32).astype(jnp.bfloat16))
        return jnp.concatenate(picks, axis=1), weights

    picks, weights, spare_weights = [], [], []
    for j in range(subs):
        code = codes[j * sources : (j + 1) * sources]
        pick, weight = picker(code, my_id, serves)
        spare_pick, spare_weight = picker(code, failed_id, holds > 0)
        both = jnp.concatenate([pick, spare_pick], axis=0)
        picks.append(both)
        weights.append(weight)
        spare_weights.append(spare_weight)
        for n in range(0, width, tile):
            got = jnp.dot(
                both, tokens[j * part : (j + 1) * part, n : n + tile], preferred_element_type=jnp.float32
            ).astype(jnp.bfloat16)
            rows_in[j * rows : (j + 1) * rows, n : n + tile] = got[:rows]
            spare_in[j * rows : (j + 1) * rows, n : n + tile] = got[rows:]

    for n in range(0, hidden.shape[1], tile):
        hidden[:, n : n + tile] = gated_unit(
            jnp.dot(rows_in[...], w_gate[0, :, n : n + tile], preferred_element_type=jnp.float32)
        ).astype(jnp.bfloat16)
    for n in range(0, width, tile):
        result = jnp.dot(hidden[...], w_down[0, :, n : n + tile], preferred_element_type=jnp.float32)
        result = result.astype(jnp.bfloat16).astype(jnp.float32)
        for j in range(subs):
            rows_out[j, :rows, n : n + tile] = (result[j * rows : (j + 1) * rows] * weights[j]).astype(
                jnp.bfloat16
            )

    @pl.when(holds > 0)
    def _():
        spare_hidden[...] = gated_unit(
            jnp.dot(spare_in[...], spare_gate[0], preferred_element_type=jnp.float32)
        ).astype(jnp.bfloat16)
        for n in range(0, width, tile):
            result = jnp.dot(
                spare_hidden[...], spare_down[0, :, n : n + tile], preferred_element_type=jnp.float32
            )
            for j in range(subs):
                rows_out[j, rows:, n : n + tile] = (
                    result[j * rows : (j + 1) * rows] * spare_weights[j]
                ).astype(jnp.bfloat16)

    @pl.when(holds <= 0)
    def _():
        rows_out[:, rows:, :] = jnp.zeros((subs, rows, width), jnp.bfloat16)

    for j in range(subs):
        for n in range(0, width, tile):
            out[j * part : (j + 1) * part, n : n + tile] = lax.dot_general(
                picks[j],
                rows_out[j, :, n : n + tile],
                (((0,), (0,)), ((), ())),
                preferred_element_type=jnp.float32,
            ).astype(jnp.bfloat16)


def run_experts(scalars, codes, tokens, w_gate, w_down, spare_gate, spare_down, capacity):
    owners, top, tok = codes.shape
    width, inner, spare = w_gate.shape[1], w_gate.shape[2], spare_gate.shape[2]
    sources = max(1, 128 // capacity)
    subs = 2 if sources * tok <= 512 else 1
    step = subs * sources
    rows = sources * capacity
    whole = lambda a: pl.BlockSpec(a.shape, lambda i: (0, 0, 0), pipeline_mode=pl.Buffered(1))
    return pl.pallas_call(
        functools.partial(expert_kernel, subs=subs, sources=sources, capacity=capacity),
        grid=(owners // step,),
        out_shape=jax.ShapeDtypeStruct((owners * tok, width), jnp.bfloat16),
        in_specs=[
            pl.BlockSpec(memory_space=pltpu.SMEM),
            pl.BlockSpec((step, top, tok), lambda i: (i, 0, 0)),
            pl.BlockSpec((step * tok, width), lambda i: (i, 0)),
            whole(w_gate),
            whole(w_down),
            whole(spare_gate),
            whole(spare_down),
        ],
        out_specs=pl.BlockSpec((step * tok, width), lambda i: (i, 0)),
        scratch_shapes=[
            pltpu.VMEM((subs * rows, width), jnp.bfloat16),
            pltpu.VMEM((subs * rows, width), jnp.bfloat16),
            pltpu.VMEM((subs * rows, inner), jnp.bfloat16),
            pltpu.VMEM((subs * rows, spare), jnp.bfloat16),
            pltpu.VMEM((subs, 2 * rows, width), jnp.bfloat16),
        ],
        compiler_params=pltpu.CompilerParams(vmem_limit_bytes=56 * 1024 * 1024),
        cost_estimate=pl.CostEstimate(
            flops=owners * capacity * 4 * width * (inner + spare),
            bytes_accessed=4 * width * (inner + spare) + 4 * owners * tok * width,
            transcendentals=owners * capacity * inner,
        ),
        name="experts",
    )(scalars, codes, tokens, w_gate, w_down, spare_gate, spare_down)


def group_kernel(failed, holders, *refs, others, adds, tok, top, capacity):
    blocks, weights_hbm, shares, refs = refs[:4], refs[4:8], refs[8 : 8 + 2 * adds], refs[8 + 2 * adds + others :]
    keep0, keep1, send = refs[:3]
    far, refs = refs[3 : 3 + adds], refs[3 + adds :]
    held, w_gate, w_down, spare_gate, spare_down = refs[:5]
    rows_in, spare_in, hidden, spare_hidden, rows_out, dense, summed, fetched, stored = refs[5:]
    width, inner = w_gate.shape
    tile = 512
    my_id, failed_id = lax.axis_index("expert"), failed[0]
    holds = holders[0, failed_id] == my_id
    for j in range(1, holders.shape[0]):
        holds = holds | (holders[j, failed_id] == my_id)
    copies = []

    def fetch(source, target, start=True):
        copy = pltpu.make_async_copy(source, target, fetched.at[len(copies)])
        if start:
            copy.start()
        copies.append(copy)
        return copy

    gate_hbm, down_hbm, spare_gate_hbm, spare_down_hbm = weights_hbm
    block_copies = [fetch(block, held.at[s]) for s, block in enumerate(blocks)]
    gate_copies = [
        fetch(gate_hbm.at[0, :, n : n + tile], w_gate.at[:, n : n + tile]) for n in range(0, inner, tile)
    ]
    share_copies = []
    if adds:
        share_copies = [fetch(shares[0], summed.at[0]), fetch(shares[1].at[1], summed.at[1])]
    spare_copies = [
        fetch(spare_gate_hbm.at[0], spare_gate, False),
        fetch(spare_down_hbm.at[0], spare_down, False),
    ]

    @pl.when(holds)
    def _():
        for copy in spare_copies:
            copy.start()

    down_copies = [
        fetch(down_hbm.at[0, :, n : n + tile], w_down.at[:, n : n + tile]) for n in range(0, width, tile)
    ]

    count = len(blocks)
    before = (
        lax.broadcasted_iota(jnp.int32, (tok, tok), 0)
        < lax.broadcasted_iota(jnp.int32, (tok, tok), 1)
    ).astype(jnp.float32).astype(jnp.bfloat16)
    own = lax.broadcasted_iota(jnp.int32, (2 * count, tok), 0) < count
    wanted = jnp.where(own, my_id, failed_id).astype(jnp.float32)
    serves = jnp.where(my_id != failed_id, 1.0, 0.0)
    live = jnp.where(own, serves, jnp.where(holds, 1.0, 0.0))
    slots = 2 * capacity
    row_iota = lax.broadcasted_iota(jnp.int32, (slots, tok), 0)
    lane_iota = lax.broadcasted_iota(jnp.int32, (tok, slots), 1)

    for copy in block_copies:
        copy.wait()
    meta = jnp.concatenate([held[s, tok : tok + 8, :].astype(jnp.float32)[:1] for s in range(count)] * 2, axis=0)
    mask = jnp.zeros((2 * count, tok), jnp.float32)
    level = jnp.zeros((2 * count, tok), jnp.float32)
    for k in range(top):
        named = jnp.where(meta[:, k * tok : (k + 1) * tok] == wanted, live, 0.0)
        high = meta[:, (top + k) * tok : (top + k + 1) * tok]
        low = meta[:, (2 * top + k) * tok : (2 * top + k + 1) * tok]
        mask = mask + named
        level = level + named * ((high * 32.0 + low) / LEVELS)
    rank = jnp.dot(mask.astype(jnp.bfloat16), before, preferred_element_type=jnp.float32)
    place = jnp.where(mask > 0, rank + jnp.where(own, 0.0, float(capacity)), -1.0)
    place_rows = place.astype(jnp.int32)
    place_columns = place.T.astype(jnp.int32)

    spreads, weights = [], []
    for s in range(count):
        here, there = place_rows[s : s + 1], place_rows[count + s : count + s + 1]
        hit_here, hit_there = row_iota == here, row_iota == there
        pick = jnp.where(hit_here | hit_there, 1.0, 0.0).astype(jnp.bfloat16)
        weights.append(
            jnp.sum(
                jnp.where(hit_here, level[s : s + 1], 0.0)
                + jnp.where(hit_there, level[count + s : count + s + 1], 0.0),
                axis=1,
                keepdims=True,
            )
        )
        here, there = place_columns[:, s : s + 1], place_columns[:, count + s : count + s + 1]
        spreads.append(jnp.where((lane_iota == here) | (lane_iota == there), 1.0, 0.0).astype(jnp.bfloat16))
        for n in range(0, width, tile):
            got = jnp.dot(pick, held[s, :tok, n : n + tile], preferred_element_type=jnp.float32).astype(
                jnp.bfloat16
            )
            rows_in[s * capacity : (s + 1) * capacity, n : n + tile] = got[:capacity]
            spare_in[s * capacity : (s + 1) * capacity, n : n + tile] = got[capacity:]

    for i, n in enumerate(range(0, inner, tile)):
        gate_copies[i].wait()
        hidden[:, n : n + tile] = gated_unit(
            jnp.dot(rows_in[...], w_gate[:, n : n + tile], preferred_element_type=jnp.float32)
        ).astype(jnp.bfloat16)
    stores = []
    if adds:
        for copy in share_copies:
            copy.wait()
        total = summed[0].astype(jnp.float32) + summed[1].astype(jnp.float32)
        summed[0] = total.astype(jnp.bfloat16)
        stores.append(pltpu.make_async_copy(summed.at[0], far[0], stored.at[0]))
        stores[0].start()

    @pl.when(holds)
    def _():
        for copy in spare_copies:
            copy.wait()
        spare_hidden[...] = gated_unit(
            jnp.dot(spare_in[...], spare_gate[...], preferred_element_type=jnp.float32)
        ).astype(jnp.bfloat16)
        for n in range(0, width, tile):
            result = jnp.dot(
                spare_hidden[...], spare_down[:, n : n + tile], preferred_element_type=jnp.float32
            )
            for s in range(count):
                rows_out[s, capacity:, n : n + tile] = (
                    result[s * capacity : (s + 1) * capacity] * weights[s][capacity:]
                ).astype(jnp.bfloat16)

    @pl.when(jnp.logical_not(holds))
    def _():
        rows_out[:, capacity:, :] = jnp.zeros((count, capacity, width), jnp.bfloat16)

    for i, n in enumerate(range(0, width, tile)):
        down_copies[i].wait()
        result = jnp.dot(hidden[...], w_down[:, n : n + tile], preferred_element_type=jnp.float32)
        result = result.astype(jnp.bfloat16).astype(jnp.float32)
        for s in range(count):
            rows_out[s, :capacity, n : n + tile] = (
                result[s * capacity : (s + 1) * capacity] * weights[s][:capacity]
            ).astype(jnp.bfloat16)
            dense[s, :, n : n + tile] = jnp.dot(
                spreads[s], rows_out[s, :, n : n + tile], preferred_element_type=jnp.float32
            ).astype(jnp.bfloat16)
            target = (keep0, keep1, send.at[0], send.at[1])[s]
            stores.append(
                pltpu.make_async_copy(
                    dense.at[s, :, n : n + tile], target.at[:, n : n + tile], stored.at[len(stores)]
                )
            )
            stores[-1].start()
    for copy in stores:
        copy.wait()


def run_group(failed, holders, blocks, weights, shares, earlier, tok, top, capacity):
    width, inner, spare = weights[0].shape[1], weights[0].shape[2], weights[2].shape[2]
    count, adds = len(blocks), len(shares) // 2
    rows = count * capacity
    hbm = pl.BlockSpec(memory_space=pl.ANY)
    smem = pl.BlockSpec(memory_space=pltpu.SMEM)
    block = pltpu.HBM((tok, width), jnp.bfloat16)
    return pl.pallas_call(
        functools.partial(
            group_kernel, others=len(earlier), adds=adds, tok=tok, top=top, capacity=capacity
        ),
        out_shape=(block, block, pltpu.HBM((2, tok, width), jnp.bfloat16)) + (block,) * adds,
        in_specs=[smem, smem] + [hbm] * (count + 4 + len(shares) + len(earlier)),
        out_specs=(hbm,) * (3 + adds),
        scratch_shapes=[
            pltpu.VMEM((count, *blocks[0].shape), jnp.bfloat16),
            pltpu.VMEM((width, inner), jnp.bfloat16),
            pltpu.VMEM((inner, width), jnp.bfloat16),
            pltpu.VMEM((width, spare), jnp.bfloat16),
            pltpu.VMEM((spare, width), jnp.bfloat16),
            pltpu.VMEM((rows, width), jnp.bfloat16),
            pltpu.VMEM((rows, width), jnp.bfloat16),
            pltpu.VMEM((rows, inner), jnp.bfloat16),
            pltpu.VMEM((rows, spare), jnp.bfloat16),
            pltpu.VMEM((count, 2 * capacity, width), jnp.bfloat16),
            pltpu.VMEM((count, tok, width), jnp.bfloat16),
            pltpu.VMEM((2, tok, width), jnp.bfloat16),
            pltpu.SemaphoreType.DMA((count + inner // 512 + width // 512 + 4,)),
            pltpu.SemaphoreType.DMA((1 + count * (width // 512),)),
        ],
        compiler_params=pltpu.CompilerParams(vmem_limit_bytes=VMEM_GRANT),
        cost_estimate=pl.CostEstimate(
            flops=rows * 4 * width * (inner + spare),
            bytes_accessed=4 * width * (inner + spare) + 4 * count * tok * width,
            transcendentals=rows * inner,
        ),
        name="group",
    )(failed, holders, *map(in_hbm, (*blocks, *weights, *shares, *earlier)))


def in_hbm(array):
    return pltpu.with_memory_space_constraint(array, pltpu.HBM)


def nothing(*refs):
    pass


def come_after(value, *others):
    return pl.pallas_call(
        nothing,
        out_shape=pltpu.HBM(value.shape, value.dtype),
        in_specs=[pl.BlockSpec(memory_space=pl.ANY)] * (1 + len(others)),
        out_specs=pl.BlockSpec(memory_space=pl.ANY),
        input_output_aliases={0: 0},
        compiler_params=pltpu.CompilerParams(vmem_limit_bytes=VMEM_GRANT),
        cost_estimate=pl.CostEstimate(flops=0, bytes_accessed=0, transcendentals=0),
        name="after",
    )(*map(in_hbm, (value, *others)))


def folded_ring(length):
    return [0] + list(range(1, length, 2)) + list(range(2, length, 2))[::-1]


def by_permutes(failed, holders, tokens, expert_ids, gate_levels, weights, owners, capacity):
    tok, top = expert_ids.shape
    width = tokens.shape[1]
    order = folded_ring(owners // 4)
    steps = len(order)
    after = {a: order[(i + 1) % steps] for i, a in enumerate(order)}
    round_ring = [(d, after[d // 4] * 4 + d % 4) for d in range(owners)]
    over_y = [(d, d ^ 2) for d in range(owners)]
    over_core = [(d, d ^ 1) for d in range(owners)]
    move = lambda a, pairs: lax.ppermute(a, "expert", pairs)
    f32 = lambda a: a.astype(jnp.float32)
    add = lambda a, b: (f32(a) + f32(b)).astype(jnp.bfloat16)

    meta = jnp.concatenate([expert_ids.T, gate_levels.T >> 5, gate_levels.T & 31], axis=0)
    meta = meta.astype(jnp.bfloat16).reshape(1, 3 * top * tok)
    meta = jnp.pad(meta, ((0, 7), (0, width - 3 * top * tok)))
    held = [jnp.concatenate([tokens, meta], axis=0)]
    held.append(move(held[0], round_ring))
    across, kept, got = [], [], []
    last = steps - 1

    def add_group(k, shares, *earlier):
        blocks = (held[k], across[k], move(held[k], over_core), move(across[k], over_core))
        keep0, keep1, send, *summed = run_group(
            failed, holders, blocks, weights, shares, earlier, tok, top, capacity
        )
        kept.append((keep0, keep1))
        return send, *summed

    def total(k, rows, *more):
        result = f32(kept[k][0][rows]) + f32(got[k][0, rows])
        for a in more:
            result = result + f32(a)
        return result.astype(jnp.bfloat16)

    across.append(move(held[0], over_y))
    (send,) = add_group(0, ())
    from_y, arrived, own = None, (), None
    every = slice(0, tok)
    for k in range(1, steps):
        across.append(move(across[-1], round_ring) if k == last else move(held[k], over_y))
        if k == 1:
            across[1] = come_after(across[1], kept[0][0])
        if k < last:
            held.append(come_after(move(held[k], round_ring), kept[k - 1][0]))
        got.append(move(come_after(send, across[k], held[min(k + 1, last)]), over_core))
        if k > 2:
            arrived = (move(total(k - 2, every, from_y, *arrived), round_ring),)
        if k > 1:
            from_y = move(add(kept[k - 1][1], got[k - 1][1]), over_y)
        if k == 2:
            send, own = add_group(k, (kept[0][1], got[0]), kept[k - 1][0])
            own = move(own, over_y)
        else:
            (send,) = add_group(k, (), kept[k - 1][0])
    got.append(move(come_after(send, own), over_core))

    halves = (slice(0, tok // 2), slice(tok // 2, tok))
    passing = [
        move(total(last - 1, rows, from_y[rows], *(a[rows] for a in arrived)), round_ring) for rows in halves
    ]
    shares = [move(add(kept[last][1][rows], got[last][1, rows]), over_y) for rows in halves]
    first, second = halves
    passed = total(last, first, shares[0], passing[0])
    follows = total(last, second, shares[1], come_after(passing[1], passed))
    passed = total(0, first, own[first], move(passed, round_ring))
    follows = come_after(move(follows, round_ring), passed)
    return jnp.concatenate([passed, total(0, second, own[second], follows)], axis=0)


def shards(
    tokens,
    expert_ids,
    gate_levels,
    failed_device,
    replica_holders,
    w_gate,
    w_down,
    spare_gate,
    spare_down,
):
    owners = lax.axis_size("expert")
    tok_count, top_count = expert_ids.shape
    capacity = 2 * tok_count * top_count // owners
    my_index = lax.axis_index("expert").astype(jnp.int32)
    failed_id = failed_device[0]
    holder_row = lax.dynamic_index_in_dim(replica_holders, failed_id, 0, keepdims=False)
    holds = jnp.any(holder_row == my_index).astype(jnp.int32)
    scalars = jnp.stack([my_index, failed_id, holds])
    weights = (w_gate, w_down, spare_gate, spare_down)
    if 12 <= owners <= 32 and owners % 4 == 0 and 3 * top_count * tok_count <= tokens.shape[1]:
        return by_permutes(
            failed_device, replica_holders.T, tokens, expert_ids, gate_levels, weights, owners, capacity
        )
    codes = (expert_ids * LEVELS + gate_levels).T
    all_codes = lax.all_gather(codes, "expert", axis=0)
    all_tokens = lax.all_gather(tokens, "expert", axis=0, tiled=True)
    dense = run_experts(scalars, all_codes, all_tokens, *weights, capacity)
    return lax.psum_scatter(dense, "expert", scatter_dimension=0, tiled=True)


def solution(mesh):
    in_specs = (
        P(("group", "expert"), None),
        P(("group", "expert"), None),
        P(("group", "expert"), None),
        P(),
        P(),
        P("expert", None, None),
        P("expert", None, None),
        P("expert", None, None),
        P("expert", None, None),
    )
    out_specs = P(("group", "expert"), None)
    return jax.shard_map(shards, mesh=mesh, in_specs=in_specs, out_specs=out_specs, check_vma=False)
```

```python
import functools
import jax
import jax.numpy as jnp
from jax import lax
from jax.experimental import pallas as pl
from jax.experimental.pallas import tpu as pltpu
from jax.sharding import PartitionSpec as P

LEVELS = 1024
VMEM_GRANT = 65200 * 1024


def gated_unit(values):
    return values * (0.5 + 0.5 * jnp.tanh(0.851 * values))


def expert_kernel(
    scalars,
    codes,
    tokens,
    w_gate,
    w_down,
    spare_gate,
    spare_down,
    out,
    rows_in,
    spare_in,
    hidden,
    spare_hidden,
    rows_out,
    *,
    subs,
    sources,
    capacity,
):
    tok = codes.shape[2]
    part = sources * tok
    rows = sources * capacity
    width = tokens.shape[1]
    tile = 512
    my_id, failed_id, holds = scalars[0], scalars[1], scalars[2]
    serves = my_id != failed_id

    before = (
        lax.broadcasted_iota(jnp.int32, (tok, tok), 0)
        < lax.broadcasted_iota(jnp.int32, (tok, tok), 1)
    ).astype(jnp.bfloat16)
    row_iota = lax.broadcasted_iota(jnp.int32, (rows, tok), 0)

    def picker(code, wanted, live):
        named = ((code // LEVELS) == wanted) & live
        mask = jnp.sum(named.astype(jnp.float32), axis=1)
        level = jnp.sum(jnp.where(named, (code % LEVELS), 0).astype(jnp.float32), axis=1) / LEVELS
        rank = jnp.dot(mask.astype(jnp.bfloat16), before, preferred_element_type=jnp.float32)
        picks, weights = [], None
        for s in range(sources):
            place = jnp.where(mask[s : s + 1] > 0, rank[s : s + 1].astype(jnp.int32) + s * capacity, -1)
            hit = row_iota == place
            scaled = jnp.sum(jnp.where(hit, level[s : s + 1], 0.0), axis=1, keepdims=True)
            weights = scaled if weights is None else weights + scaled
            picks.append(hit.astype(jnp.float32).astype(jnp.bfloat16))
        return jnp.concatenate(picks, axis=1), weights

    picks, weights, spare_weights = [], [], []
    for j in range(subs):
        code = codes[j * sources : (j + 1) * sources]
        pick, weight = picker(code, my_id, serves)
        spare_pick, spare_weight = picker(code, failed_id, holds > 0)
        both = jnp.concatenate([pick, spare_pick], axis=0)
        picks.append(both)
        weights.append(weight)
        spare_weights.append(spare_weight)
        for n in range(0, width, tile):
            got = jnp.dot(
                both, tokens[j * part : (j + 1) * part, n : n + tile], preferred_element_type=jnp.float32
            ).astype(jnp.bfloat16)
            rows_in[j * rows : (j + 1) * rows, n : n + tile] = got[:rows]
            spare_in[j * rows : (j + 1) * rows, n : n + tile] = got[rows:]

    for n in range(0, hidden.shape[1], tile):
        hidden[:, n : n + tile] = gated_unit(
            jnp.dot(rows_in[...], w_gate[0, :, n : n + tile], preferred_element_type=jnp.float32)
        ).astype(jnp.bfloat16)
    for n in range(0, width, tile):
        result = jnp.dot(hidden[...], w_down[0, :, n : n + tile], preferred_element_type=jnp.float32)
        result = result.astype(jnp.bfloat16).astype(jnp.float32)
        for j in range(subs):
            rows_out[j, :rows, n : n + tile] = (result[j * rows : (j + 1) * rows] * weights[j]).astype(
                jnp.bfloat16
            )

    @pl.when(holds > 0)
    def _():
        spare_hidden[...] = gated_unit(
            jnp.dot(spare_in[...], spare_gate[0], preferred_element_type=jnp.float32)
        ).astype(jnp.bfloat16)
        for n in range(0, width, tile):
            result = jnp.dot(
                spare_hidden[...], spare_down[0, :, n : n + tile], preferred_element_type=jnp.float32
            )
            for j in range(subs):
                rows_out[j, rows:, n : n + tile] = (
                    result[j * rows : (j + 1) * rows] * spare_weights[j]
                ).astype(jnp.bfloat16)

    @pl.when(holds <= 0)
    def _():
        rows_out[:, rows:, :] = jnp.zeros((subs, rows, width), jnp.bfloat16)

    for j in range(subs):
        for n in range(0, width, tile):
            out[j * part : (j + 1) * part, n : n + tile] = lax.dot_general(
                picks[j],
                rows_out[j, :, n : n + tile],
                (((0,), (0,)), ((), ())),
                preferred_element_type=jnp.float32,
            ).astype(jnp.bfloat16)


def run_experts(scalars, codes, tokens, w_gate, w_down, spare_gate, spare_down, capacity):
    owners, top, tok = codes.shape
    width, inner, spare = w_gate.shape[1], w_gate.shape[2], spare_gate.shape[2]
    sources = max(1, 128 // capacity)
    subs = 2 if sources * tok <= 512 else 1
    step = subs * sources
    rows = sources * capacity
    whole = lambda a: pl.BlockSpec(a.shape, lambda i: (0, 0, 0), pipeline_mode=pl.Buffered(1))
    return pl.pallas_call(
        functools.partial(expert_kernel, subs=subs, sources=sources, capacity=capacity),
        grid=(owners // step,),
        out_shape=jax.ShapeDtypeStruct((owners * tok, width), jnp.bfloat16),
        in_specs=[
            pl.BlockSpec(memory_space=pltpu.SMEM),
            pl.BlockSpec((step, top, tok), lambda i: (i, 0, 0)),
            pl.BlockSpec((step * tok, width), lambda i: (i, 0)),
            whole(w_gate),
            whole(w_down),
            whole(spare_gate),
            whole(spare_down),
        ],
        out_specs=pl.BlockSpec((step * tok, width), lambda i: (i, 0)),
        scratch_shapes=[
            pltpu.VMEM((subs * rows, width), jnp.bfloat16),
            pltpu.VMEM((subs * rows, width), jnp.bfloat16),
            pltpu.VMEM((subs * rows, inner), jnp.bfloat16),
            pltpu.VMEM((subs * rows, spare), jnp.bfloat16),
            pltpu.VMEM((subs, 2 * rows, width), jnp.bfloat16),
        ],
        compiler_params=pltpu.CompilerParams(vmem_limit_bytes=56 * 1024 * 1024),
        cost_estimate=pl.CostEstimate(
            flops=owners * capacity * 4 * width * (inner + spare),
            bytes_accessed=4 * width * (inner + spare) + 4 * owners * tok * width,
            transcendentals=owners * capacity * inner,
        ),
        name="experts",
    )(scalars, codes, tokens, w_gate, w_down, spare_gate, spare_down)


def group_kernel(failed, holders, *refs, others, adds, tok, top, capacity):
    blocks, weights_hbm, shares, refs = refs[:4], refs[4:8], refs[8 : 8 + 2 * adds], refs[8 + 2 * adds + others :]
    keep0, keep1, send = refs[:3]
    far, refs = refs[3 : 3 + adds], refs[3 + adds :]
    held, w_gate, w_down, spare_gate, spare_down = refs[:5]
    rows_in, spare_in, hidden, spare_hidden, rows_out, dense, summed, fetched, stored = refs[5:]
    width, inner = w_gate.shape
    tile = 512
    my_id, failed_id = lax.axis_index("expert"), failed[0]
    holds = holders[0, failed_id] == my_id
    for j in range(1, holders.shape[0]):
        holds = holds | (holders[j, failed_id] == my_id)
    copies = []

    def fetch(source, target, start=True):
        copy = pltpu.make_async_copy(source, target, fetched.at[len(copies)])
        if start:
            copy.start()
        copies.append(copy)
        return copy

    gate_hbm, down_hbm, spare_gate_hbm, spare_down_hbm = weights_hbm
    block_copies = [fetch(block, held.at[s]) for s, block in enumerate(blocks)]
    gate_copies = [
        fetch(gate_hbm.at[0, :, n : n + tile], w_gate.at[:, n : n + tile]) for n in range(0, inner, tile)
    ]
    share_copies = []
    if adds:
        share_copies = [fetch(shares[0], summed.at[0]), fetch(shares[1].at[1], summed.at[1])]
    spare_copies = [
        fetch(spare_gate_hbm.at[0], spare_gate, False),
        fetch(spare_down_hbm.at[0], spare_down, False),
    ]

    @pl.when(holds)
    def _():
        for copy in spare_copies:
            copy.start()

    down_copies = [
        fetch(down_hbm.at[0, :, n : n + tile], w_down.at[:, n : n + tile]) for n in range(0, width, tile)
    ]

    count = len(blocks)
    before = (
        lax.broadcasted_iota(jnp.int32, (tok, tok), 0)
        < lax.broadcasted_iota(jnp.int32, (tok, tok), 1)
    ).astype(jnp.float32).astype(jnp.bfloat16)
    own = lax.broadcasted_iota(jnp.int32, (2 * count, tok), 0) < count
    wanted = jnp.where(own, my_id, failed_id).astype(jnp.float32)
    serves = jnp.where(my_id != failed_id, 1.0, 0.0)
    live = jnp.where(own, serves, jnp.where(holds, 1.0, 0.0))
    slots = 2 * capacity
    row_iota = lax.broadcasted_iota(jnp.int32, (slots, tok), 0)
    lane_iota = lax.broadcasted_iota(jnp.int32, (tok, slots), 1)

    for copy in block_copies:
        copy.wait()
    meta = jnp.concatenate([held[s, tok : tok + 8, :].astype(jnp.float32)[:1] for s in range(count)] * 2, axis=0)
    mask = jnp.zeros((2 * count, tok), jnp.float32)
    level = jnp.zeros((2 * count, tok), jnp.float32)
    for k in range(top):
        named = jnp.where(meta[:, k * tok : (k + 1) * tok] == wanted, live, 0.0)
        high = meta[:, (top + k) * tok : (top + k + 1) * tok]
        low = meta[:, (2 * top + k) * tok : (2 * top + k + 1) * tok]
        mask = mask + named
        level = level + named * ((high * 32.0 + low) / LEVELS)
    rank = jnp.dot(mask.astype(jnp.bfloat16), before, preferred_element_type=jnp.float32)
    place = jnp.where(mask > 0, rank + jnp.where(own, 0.0, float(capacity)), -1.0)
    place_rows = place.astype(jnp.int32)
    place_columns = place.T.astype(jnp.int32)

    spreads, weights = [], []
    for s in range(count):
        here, there = place_rows[s : s + 1], place_rows[count + s : count + s + 1]
        hit_here, hit_there = row_iota == here, row_iota == there
        pick = jnp.where(hit_here | hit_there, 1.0, 0.0).astype(jnp.bfloat16)
        weights.append(
            jnp.sum(
                jnp.where(hit_here, level[s : s + 1], 0.0)
                + jnp.where(hit_there, level[count + s : count + s + 1], 0.0),
                axis=1,
                keepdims=True,
            )
        )
        here, there = place_columns[:, s : s + 1], place_columns[:, count + s : count + s + 1]
        spreads.append(jnp.where((lane_iota == here) | (lane_iota == there), 1.0, 0.0).astype(jnp.bfloat16))
        for n in range(0, width, tile):
            got = jnp.dot(pick, held[s, :tok, n : n + tile], preferred_element_type=jnp.float32).astype(
                jnp.bfloat16
            )
            rows_in[s * capacity : (s + 1) * capacity, n : n + tile] = got[:capacity]
            spare_in[s * capacity : (s + 1) * capacity, n : n + tile] = got[capacity:]

    for i, n in enumerate(range(0, inner, tile)):
        gate_copies[i].wait()
        hidden[:, n : n + tile] = gated_unit(
            jnp.dot(rows_in[...], w_gate[:, n : n + tile], preferred_element_type=jnp.float32)
        ).astype(jnp.bfloat16)
    stores = []
    if adds:
        for copy in share_copies:
            copy.wait()
        total = summed[0].astype(jnp.float32) + summed[1].astype(jnp.float32)
        summed[0] = total.astype(jnp.bfloat16)
        stores.append(pltpu.make_async_copy(summed.at[0], far[0], stored.at[0]))
        stores[0].start()

    @pl.when(holds)
    def _():
        for copy in spare_copies:
            copy.wait()
        spare_hidden[...] = gated_unit(
            jnp.dot(spare_in[...], spare_gate[...], preferred_element_type=jnp.float32)
        ).astype(jnp.bfloat16)
        for n in range(0, width, tile):
            result = jnp.dot(
                spare_hidden[...], spare_down[:, n : n + tile], preferred_element_type=jnp.float32
            )
            for s in range(count):
                rows_out[s, capacity:, n : n + tile] = (
                    result[s * capacity : (s + 1) * capacity] * weights[s][capacity:]
                ).astype(jnp.bfloat16)

    @pl.when(jnp.logical_not(holds))
    def _():
        rows_out[:, capacity:, :] = jnp.zeros((count, capacity, width), jnp.bfloat16)

    for i, n in enumerate(range(0, width, tile)):
        down_copies[i].wait()
        result = jnp.dot(hidden[...], w_down[:, n : n + tile], preferred_element_type=jnp.float32)
        result = result.astype(jnp.bfloat16).astype(jnp.float32)
        for s in range(count):
            rows_out[s, :capacity, n : n + tile] = (
                result[s * capacity : (s + 1) * capacity] * weights[s][:capacity]
            ).astype(jnp.bfloat16)
            dense[s, :, n : n + tile] = jnp.dot(
                spreads[s], rows_out[s, :, n : n + tile], preferred_element_type=jnp.float32
            ).astype(jnp.bfloat16)
            target = (keep0, keep1, send.at[0], send.at[1])[s]
            stores.append(
                pltpu.make_async_copy(
                    dense.at[s, :, n : n + tile], target.at[:, n : n + tile], stored.at[len(stores)]
                )
            )
            stores[-1].start()
    for copy in stores:
        copy.wait()


def run_group(failed, holders, blocks, weights, shares, earlier, tok, top, capacity):
    width, inner, spare = weights[0].shape[1], weights[0].shape[2], weights[2].shape[2]
    count, adds = len(blocks), len(shares) // 2
    rows = count * capacity
    hbm = pl.BlockSpec(memory_space=pl.ANY)
    smem = pl.BlockSpec(memory_space=pltpu.SMEM)
    block = pltpu.HBM((tok, width), jnp.bfloat16)
    return pl.pallas_call(
        functools.partial(
            group_kernel, others=len(earlier), adds=adds, tok=tok, top=top, capacity=capacity
        ),
        out_shape=(block, block, pltpu.HBM((2, tok, width), jnp.bfloat16)) + (block,) * adds,
        in_specs=[smem, smem] + [hbm] * (count + 4 + len(shares) + len(earlier)),
        out_specs=(hbm,) * (3 + adds),
        scratch_shapes=[
            pltpu.VMEM((count, *blocks[0].shape), jnp.bfloat16),
            pltpu.VMEM((width, inner), jnp.bfloat16),
            pltpu.VMEM((inner, width), jnp.bfloat16),
            pltpu.VMEM((width, spare), jnp.bfloat16),
            pltpu.VMEM((spare, width), jnp.bfloat16),
            pltpu.VMEM((rows, width), jnp.bfloat16),
            pltpu.VMEM((rows, width), jnp.bfloat16),
            pltpu.VMEM((rows, inner), jnp.bfloat16),
            pltpu.VMEM((rows, spare), jnp.bfloat16),
            pltpu.VMEM((count, 2 * capacity, width), jnp.bfloat16),
            pltpu.VMEM((count, tok, width), jnp.bfloat16),
            pltpu.VMEM((2, tok, width), jnp.bfloat16),
            pltpu.SemaphoreType.DMA((count + inner // 512 + width // 512 + 4,)),
            pltpu.SemaphoreType.DMA((1 + count * (width // 512),)),
        ],
        compiler_params=pltpu.CompilerParams(vmem_limit_bytes=VMEM_GRANT),
        cost_estimate=pl.CostEstimate(
            flops=rows * 4 * width * (inner + spare),
            bytes_accessed=4 * width * (inner + spare) + 4 * count * tok * width,
            transcendentals=rows * inner,
        ),
        name="group",
    )(failed, holders, *map(in_hbm, (*blocks, *weights, *shares, *earlier)))


def in_hbm(array):
    return pltpu.with_memory_space_constraint(array, pltpu.HBM)


def nothing(*refs):
    pass


def come_after(value, *others, flops=0):
    return pl.pallas_call(
        nothing,
        out_shape=pltpu.HBM(value.shape, value.dtype),
        in_specs=[pl.BlockSpec(memory_space=pl.ANY)] * (1 + len(others)),
        out_specs=pl.BlockSpec(memory_space=pl.ANY),
        input_output_aliases={0: 0},
        compiler_params=pltpu.CompilerParams(vmem_limit_bytes=VMEM_GRANT),
        cost_estimate=pl.CostEstimate(flops=flops, bytes_accessed=0, transcendentals=0),
        name="after",
    )(*map(in_hbm, (value, *others)))


def folded_ring(length):
    return [0] + list(range(1, length, 2)) + list(range(2, length, 2))[::-1]


def by_permutes(failed, holders, tokens, expert_ids, gate_levels, weights, owners, capacity):
    tok, top = expert_ids.shape
    width = tokens.shape[1]
    order = folded_ring(owners // 4)
    steps = len(order)
    after = {a: order[(i + 1) % steps] for i, a in enumerate(order)}
    round_ring = [(d, after[d // 4] * 4 + d % 4) for d in range(owners)]
    over_y = [(d, d ^ 2) for d in range(owners)]
    over_core = [(d, d ^ 1) for d in range(owners)]
    move = lambda a, pairs: lax.ppermute(a, "expert", pairs)
    f32 = lambda a: a.astype(jnp.float32)
    add = lambda a, b: (f32(a) + f32(b)).astype(jnp.bfloat16)

    meta = jnp.concatenate([expert_ids.T, gate_levels.T >> 5, gate_levels.T & 31], axis=0)
    meta = meta.astype(jnp.bfloat16).reshape(1, 3 * top * tok)
    meta = jnp.pad(meta, ((0, 7), (0, width - 3 * top * tok)))
    held = [jnp.concatenate([tokens, meta], axis=0)]
    held.append(move(held[0], round_ring))
    across, kept, got = [], [], []
    last = steps - 1

    def add_group(k, shares, *earlier):
        blocks = (held[k], across[k], move(held[k], over_core), move(across[k], over_core))
        keep0, keep1, send, *summed = run_group(
            failed, holders, blocks, weights, shares, earlier, tok, top, capacity
        )
        kept.append((keep0, keep1))
        return send, *summed

    def total(k, rows, *more):
        result = f32(kept[k][0][rows]) + f32(got[k][0, rows])
        for a in more:
            result = result + f32(a)
        return result.astype(jnp.bfloat16)

    across.append(move(held[0], over_y))
    (send,) = add_group(0, ())
    from_y, arrived, own = None, (), None
    every = slice(0, tok)
    for k in range(1, steps):
        across.append(move(across[-1], round_ring) if k == last else move(held[k], over_y))
        if k == 1:
            across[1] = come_after(across[1], kept[0][0])
        if k < last:
            held.append(come_after(move(held[k], round_ring), kept[k - 1][0]))
        got.append(move(come_after(send, across[k], held[min(k + 1, last)]), over_core))
        if k > 2:
            arrived = (move(total(k - 2, every, from_y, *arrived), round_ring),)
        if k > 1:
            from_y = move(add(kept[k - 1][1], got[k - 1][1]), over_y)
        if k == 2:
            send, own = add_group(k, (kept[0][1], got[0]), kept[k - 1][0])
        else:
            (send,) = add_group(k, (), kept[k - 1][0])
    got.append(move(send, over_core))

    halves = (slice(0, tok // 2), slice(tok // 2, tok))
    passing = [
        move(total(last - 1, rows, from_y[rows], *(a[rows] for a in arrived)), round_ring) for rows in halves
    ]
    shares = [move(add(kept[last][1][rows], got[last][1, rows]), over_y) for rows in halves]
    first, second = halves
    passed = total(last, first, shares[0], passing[0])
    follows = total(last, second, shares[1], come_after(passing[1], passed))
    own = move(come_after(own, passed), over_y)
    passed = come_after(move(passed, round_ring), flops=4 * 10**9)
    return total(0, every, own, jnp.concatenate([passed, move(follows, round_ring)], axis=0))


def shards(
    tokens,
    expert_ids,
    gate_levels,
    failed_device,
    replica_holders,
    w_gate,
    w_down,
    spare_gate,
    spare_down,
):
    owners = lax.axis_size("expert")
    tok_count, top_count = expert_ids.shape
    capacity = 2 * tok_count * top_count // owners
    my_index = lax.axis_index("expert").astype(jnp.int32)
    failed_id = failed_device[0]
    holder_row = lax.dynamic_index_in_dim(replica_holders, failed_id, 0, keepdims=False)
    holds = jnp.any(holder_row == my_index).astype(jnp.int32)
    scalars = jnp.stack([my_index, failed_id, holds])
    weights = (w_gate, w_down, spare_gate, spare_down)
    if 12 <= owners <= 32 and owners % 4 == 0 and 3 * top_count * tok_count <= tokens.shape[1]:
        return by_permutes(
            failed_device, replica_holders.T, tokens, expert_ids, gate_levels, weights, owners, capacity
        )
    codes = (expert_ids * LEVELS + gate_levels).T
    all_codes = lax.all_gather(codes, "expert", axis=0)
    all_tokens = lax.all_gather(tokens, "expert", axis=0, tiled=True)
    dense = run_experts(scalars, all_codes, all_tokens, *weights, capacity)
    return lax.psum_scatter(dense, "expert", scatter_dimension=0, tiled=True)


def solution(mesh):
    in_specs = (
        P(("group", "expert"), None),
        P(("group", "expert"), None),
        P(("group", "expert"), None),
        P(),
        P(),
        P("expert", None, None),
        P("expert", None, None),
        P("expert", None, None),
        P("expert", None, None),
    )
    out_specs = P(("group", "expert"), None)
    return jax.shard_map(shards, mesh=mesh, in_specs=in_specs, out_specs=out_specs, check_vma=False)
```

```python
import functools
import jax
import jax.numpy as jnp
from jax import lax
from jax.experimental import pallas as pl
from jax.experimental.pallas import tpu as pltpu
from jax.sharding import PartitionSpec as P

LEVELS = 1024
VMEM_GRANT = 65200 * 1024


def gated_unit(values):
    return values * (0.5 + 0.5 * jnp.tanh(0.851 * values))


def expert_kernel(
    scalars,
    codes,
    tokens,
    w_gate,
    w_down,
    spare_gate,
    spare_down,
    out,
    rows_in,
    spare_in,
    hidden,
    spare_hidden,
    rows_out,
    *,
    subs,
    sources,
    capacity,
):
    tok = codes.shape[2]
    part = sources * tok
    rows = sources * capacity
    width = tokens.shape[1]
    tile = 512
    my_id, failed_id, holds = scalars[0], scalars[1], scalars[2]
    serves = my_id != failed_id

    before = (
        lax.broadcasted_iota(jnp.int32, (tok, tok), 0)
        < lax.broadcasted_iota(jnp.int32, (tok, tok), 1)
    ).astype(jnp.bfloat16)
    row_iota = lax.broadcasted_iota(jnp.int32, (rows, tok), 0)

    def picker(code, wanted, live):
        named = ((code // LEVELS) == wanted) & live
        mask = jnp.sum(named.astype(jnp.float32), axis=1)
        level = jnp.sum(jnp.where(named, (code % LEVELS), 0).astype(jnp.float32), axis=1) / LEVELS
        rank = jnp.dot(mask.astype(jnp.bfloat16), before, preferred_element_type=jnp.float32)
        picks, weights = [], None
        for s in range(sources):
            place = jnp.where(mask[s : s + 1] > 0, rank[s : s + 1].astype(jnp.int32) + s * capacity, -1)
            hit = row_iota == place
            scaled = jnp.sum(jnp.where(hit, level[s : s + 1], 0.0), axis=1, keepdims=True)
            weights = scaled if weights is None else weights + scaled
            picks.append(hit.astype(jnp.float32).astype(jnp.bfloat16))
        return jnp.concatenate(picks, axis=1), weights

    picks, weights, spare_weights = [], [], []
    for j in range(subs):
        code = codes[j * sources : (j + 1) * sources]
        pick, weight = picker(code, my_id, serves)
        spare_pick, spare_weight = picker(code, failed_id, holds > 0)
        both = jnp.concatenate([pick, spare_pick], axis=0)
        picks.append(both)
        weights.append(weight)
        spare_weights.append(spare_weight)
        for n in range(0, width, tile):
            got = jnp.dot(
                both, tokens[j * part : (j + 1) * part, n : n + tile], preferred_element_type=jnp.float32
            ).astype(jnp.bfloat16)
            rows_in[j * rows : (j + 1) * rows, n : n + tile] = got[:rows]
            spare_in[j * rows : (j + 1) * rows, n : n + tile] = got[rows:]

    for n in range(0, hidden.shape[1], tile):
        hidden[:, n : n + tile] = gated_unit(
            jnp.dot(rows_in[...], w_gate[0, :, n : n + tile], preferred_element_type=jnp.float32)
        ).astype(jnp.bfloat16)
    for n in range(0, width, tile):
        result = jnp.dot(hidden[...], w_down[0, :, n : n + tile], preferred_element_type=jnp.float32)
        result = result.astype(jnp.bfloat16).astype(jnp.float32)
        for j in range(subs):
            rows_out[j, :rows, n : n + tile] = (result[j * rows : (j + 1) * rows] * weights[j]).astype(
                jnp.bfloat16
            )

    @pl.when(holds > 0)
    def _():
        spare_hidden[...] = gated_unit(
            jnp.dot(spare_in[...], spare_gate[0], preferred_element_type=jnp.float32)
        ).astype(jnp.bfloat16)
        for n in range(0, width, tile):
            result = jnp.dot(
                spare_hidden[...], spare_down[0, :, n : n + tile], preferred_element_type=jnp.float32
            )
            for j in range(subs):
                rows_out[j, rows:, n : n + tile] = (
                    result[j * rows : (j + 1) * rows] * spare_weights[j]
                ).astype(jnp.bfloat16)

    @pl.when(holds <= 0)
    def _():
        rows_out[:, rows:, :] = jnp.zeros((subs, rows, width), jnp.bfloat16)

    for j in range(subs):
        for n in range(0, width, tile):
            out[j * part : (j + 1) * part, n : n + tile] = lax.dot_general(
                picks[j],
                rows_out[j, :, n : n + tile],
                (((0,), (0,)), ((), ())),
                preferred_element_type=jnp.float32,
            ).astype(jnp.bfloat16)


def run_experts(scalars, codes, tokens, w_gate, w_down, spare_gate, spare_down, capacity):
    owners, top, tok = codes.shape
    width, inner, spare = w_gate.shape[1], w_gate.shape[2], spare_gate.shape[2]
    sources = max(1, 128 // capacity)
    subs = 2 if sources * tok <= 512 else 1
    step = subs * sources
    rows = sources * capacity
    whole = lambda a: pl.BlockSpec(a.shape, lambda i: (0, 0, 0), pipeline_mode=pl.Buffered(1))
    return pl.pallas_call(
        functools.partial(expert_kernel, subs=subs, sources=sources, capacity=capacity),
        grid=(owners // step,),
        out_shape=jax.ShapeDtypeStruct((owners * tok, width), jnp.bfloat16),
        in_specs=[
            pl.BlockSpec(memory_space=pltpu.SMEM),
            pl.BlockSpec((step, top, tok), lambda i: (i, 0, 0)),
            pl.BlockSpec((step * tok, width), lambda i: (i, 0)),
            whole(w_gate),
            whole(w_down),
            whole(spare_gate),
            whole(spare_down),
        ],
        out_specs=pl.BlockSpec((step * tok, width), lambda i: (i, 0)),
        scratch_shapes=[
            pltpu.VMEM((subs * rows, width), jnp.bfloat16),
            pltpu.VMEM((subs * rows, width), jnp.bfloat16),
            pltpu.VMEM((subs * rows, inner), jnp.bfloat16),
            pltpu.VMEM((subs * rows, spare), jnp.bfloat16),
            pltpu.VMEM((subs, 2 * rows, width), jnp.bfloat16),
        ],
        compiler_params=pltpu.CompilerParams(vmem_limit_bytes=56 * 1024 * 1024),
        cost_estimate=pl.CostEstimate(
            flops=owners * capacity * 4 * width * (inner + spare),
            bytes_accessed=4 * width * (inner + spare) + 4 * owners * tok * width,
            transcendentals=owners * capacity * inner,
        ),
        name="experts",
    )(scalars, codes, tokens, w_gate, w_down, spare_gate, spare_down)


def group_kernel(failed, holders, *refs, others, adds, tok, top, capacity):
    blocks, weights_hbm, shares, refs = refs[:4], refs[4:8], refs[8 : 8 + 2 * adds], refs[8 + 2 * adds + others :]
    keep0, keep1, send = refs[:3]
    far, refs = refs[3 : 3 + adds], refs[3 + adds :]
    held, w_gate, w_down, spare_gate, spare_down = refs[:5]
    rows_in, spare_in, hidden, spare_hidden, rows_out, dense, summed, fetched, stored = refs[5:]
    width, inner = w_gate.shape
    tile = 768
    my_id, failed_id = lax.axis_index("expert"), failed[0]
    holds = holders[0, failed_id] == my_id
    for j in range(1, holders.shape[0]):
        holds = holds | (holders[j, failed_id] == my_id)
    copies = []

    def fetch(source, target, start=True):
        copy = pltpu.make_async_copy(source, target, fetched.at[len(copies)])
        if start:
            copy.start()
        copies.append(copy)
        return copy

    gate_hbm, down_hbm, spare_gate_hbm, spare_down_hbm = weights_hbm
    block_copies = [fetch(block, held.at[s]) for s, block in enumerate(blocks)]
    gate_copies = [
        fetch(gate_hbm.at[0, :, n : n + tile], w_gate.at[:, n : n + tile]) for n in range(0, inner, tile)
    ]
    share_copies = []
    if adds:
        share_copies = [fetch(shares[0], summed.at[0]), fetch(shares[1].at[1], summed.at[1])]
    spare_copies = [
        fetch(spare_gate_hbm.at[0], spare_gate, False),
        fetch(spare_down_hbm.at[0], spare_down, False),
    ]

    @pl.when(holds)
    def _():
        for copy in spare_copies:
            copy.start()

    down_copies = [
        fetch(down_hbm.at[0, :, n : n + tile], w_down.at[:, n : n + tile]) for n in range(0, width, tile)
    ]

    count = len(blocks)
    before = (
        lax.broadcasted_iota(jnp.int32, (tok, tok), 0)
        < lax.broadcasted_iota(jnp.int32, (tok, tok), 1)
    ).astype(jnp.float32).astype(jnp.bfloat16)
    own = lax.broadcasted_iota(jnp.int32, (2 * count, tok), 0) < count
    wanted = jnp.where(own, my_id, failed_id).astype(jnp.float32)
    serves = jnp.where(my_id != failed_id, 1.0, 0.0)
    live = jnp.where(own, serves, jnp.where(holds, 1.0, 0.0))
    slots = 2 * capacity
    row_iota = lax.broadcasted_iota(jnp.int32, (slots, tok), 0)
    lane_iota = lax.broadcasted_iota(jnp.int32, (tok, slots), 1)

    for copy in block_copies:
        copy.wait()
    meta = jnp.concatenate([held[s, tok : tok + 8, :].astype(jnp.float32)[:1] for s in range(count)] * 2, axis=0)
    mask = jnp.zeros((2 * count, tok), jnp.float32)
    level = jnp.zeros((2 * count, tok), jnp.float32)
    for k in range(top):
        named = jnp.where(meta[:, k * tok : (k + 1) * tok] == wanted, live, 0.0)
        high = meta[:, (top + k) * tok : (top + k + 1) * tok]
        low = meta[:, (2 * top + k) * tok : (2 * top + k + 1) * tok]
        mask = mask + named
        level = level + named * ((high * 32.0 + low) / LEVELS)
    rank = jnp.dot(mask.astype(jnp.bfloat16), before, preferred_element_type=jnp.float32)
    place = jnp.where(mask > 0, rank + jnp.where(own, 0.0, float(capacity)), -1.0)
    place_rows = place.astype(jnp.int32)
    place_columns = place.T.astype(jnp.int32)

    spreads, weights = [], []
    for s in range(count):
        here, there = place_rows[s : s + 1], place_rows[count + s : count + s + 1]
        hit_here, hit_there = row_iota == here, row_iota == there
        pick = jnp.where(hit_here | hit_there, 1.0, 0.0).astype(jnp.bfloat16)
        weights.append(
            jnp.sum(
                jnp.where(hit_here, level[s : s + 1], 0.0)
                + jnp.where(hit_there, level[count + s : count + s + 1], 0.0),
                axis=1,
                keepdims=True,
            )
        )
        here, there = place_columns[:, s : s + 1], place_columns[:, count + s : count + s + 1]
        spreads.append(jnp.where((lane_iota == here) | (lane_iota == there), 1.0, 0.0).astype(jnp.bfloat16))
        for n in range(0, width, tile):
            got = jnp.dot(pick, held[s, :tok, n : n + tile], preferred_element_type=jnp.float32).astype(
                jnp.bfloat16
            )
            rows_in[s * capacity : (s + 1) * capacity, n : n + tile] = got[:capacity]
            spare_in[s * capacity : (s + 1) * capacity, n : n + tile] = got[capacity:]

    for i, n in enumerate(range(0, inner, tile)):
        gate_copies[i].wait()
        hidden[:, n : n + tile] = gated_unit(
            jnp.dot(rows_in[...], w_gate[:, n : n + tile], preferred_element_type=jnp.float32)
        ).astype(jnp.bfloat16)
    stores = []
    if adds:
        for copy in share_copies:
            copy.wait()
        total = summed[0].astype(jnp.float32) + summed[1].astype(jnp.float32)
        summed[0] = total.astype(jnp.bfloat16)
        stores.append(pltpu.make_async_copy(summed.at[0], far[0], stored.at[0]))
        stores[0].start()

    @pl.when(holds)
    def _():
        for copy in spare_copies:
            copy.wait()
        spare_hidden[...] = gated_unit(
            jnp.dot(spare_in[...], spare_gate[...], preferred_element_type=jnp.float32)
        ).astype(jnp.bfloat16)
        for n in range(0, width, tile):
            result = jnp.dot(
                spare_hidden[...], spare_down[:, n : n + tile], preferred_element_type=jnp.float32
            )
            for s in range(count):
                rows_out[s, capacity:, n : n + tile] = (
                    result[s * capacity : (s + 1) * capacity] * weights[s][capacity:]
                ).astype(jnp.bfloat16)

    @pl.when(jnp.logical_not(holds))
    def _():
        rows_out[:, capacity:, :] = jnp.zeros((count, capacity, width), jnp.bfloat16)

    for i, n in enumerate(range(0, width, tile)):
        down_copies[i].wait()
        result = jnp.dot(hidden[...], w_down[:, n : n + tile], preferred_element_type=jnp.float32)
        for s in range(count):
            rows_out[s, :capacity, n : n + tile] = (
                result[s * capacity : (s + 1) * capacity] * weights[s][:capacity]
            ).astype(jnp.bfloat16)
            dense[s, :, n : n + tile] = jnp.dot(
                spreads[s], rows_out[s, :, n : n + tile], preferred_element_type=jnp.float32
            ).astype(jnp.bfloat16)
            target = (keep0, keep1, send.at[0], send.at[1])[s]
            stores.append(
                pltpu.make_async_copy(
                    dense.at[s, :, n : n + tile], target.at[:, n : n + tile], stored.at[len(stores)]
                )
            )
            stores[-1].start()
    for copy in stores:
        copy.wait()


def run_group(failed, holders, blocks, weights, shares, earlier, tok, top, capacity):
    width, inner, spare = weights[0].shape[1], weights[0].shape[2], weights[2].shape[2]
    count, adds = len(blocks), len(shares) // 2
    rows = count * capacity
    hbm = pl.BlockSpec(memory_space=pl.ANY)
    smem = pl.BlockSpec(memory_space=pltpu.SMEM)
    block = pltpu.HBM((tok, width), jnp.bfloat16)
    return pl.pallas_call(
        functools.partial(
            group_kernel, others=len(earlier), adds=adds, tok=tok, top=top, capacity=capacity
        ),
        out_shape=(block, block, pltpu.HBM((2, tok, width), jnp.bfloat16)) + (block,) * adds,
        in_specs=[smem, smem] + [hbm] * (count + 4 + len(shares) + len(earlier)),
        out_specs=(hbm,) * (3 + adds),
        scratch_shapes=[
            pltpu.VMEM((count, *blocks[0].shape), jnp.bfloat16),
            pltpu.VMEM((width, inner), jnp.bfloat16),
            pltpu.VMEM((inner, width), jnp.bfloat16),
            pltpu.VMEM((width, spare), jnp.bfloat16),
            pltpu.VMEM((spare, width), jnp.bfloat16),
            pltpu.VMEM((rows, width), jnp.bfloat16),
            pltpu.VMEM((rows, width), jnp.bfloat16),
            pltpu.VMEM((rows, inner), jnp.bfloat16),
            pltpu.VMEM((rows, spare), jnp.bfloat16),
            pltpu.VMEM((count, 2 * capacity, width), jnp.bfloat16),
            pltpu.VMEM((count, tok, width), jnp.bfloat16),
            pltpu.VMEM((2, tok, width), jnp.bfloat16),
            pltpu.SemaphoreType.DMA((count + inner // 512 + width // 512 + 4,)),
            pltpu.SemaphoreType.DMA((1 + count * (width // 512),)),
        ],
        compiler_params=pltpu.CompilerParams(vmem_limit_bytes=VMEM_GRANT),
        cost_estimate=pl.CostEstimate(
            flops=rows * 4 * width * (inner + spare),
            bytes_accessed=4 * width * (inner + spare) + 4 * count * tok * width,
            transcendentals=rows * inner,
        ),
        name="group",
    )(failed, holders, *map(in_hbm, (*blocks, *weights, *shares, *earlier)))


def in_hbm(array):
    return pltpu.with_memory_space_constraint(array, pltpu.HBM)


def nothing(*refs):
    pass


def come_after(value, *others, flops=0):
    return pl.pallas_call(
        nothing,
        out_shape=pltpu.HBM(value.shape, value.dtype),
        in_specs=[pl.BlockSpec(memory_space=pl.ANY)] * (1 + len(others)),
        out_specs=pl.BlockSpec(memory_space=pl.ANY),
        input_output_aliases={0: 0},
        compiler_params=pltpu.CompilerParams(vmem_limit_bytes=VMEM_GRANT),
        cost_estimate=pl.CostEstimate(flops=flops, bytes_accessed=0, transcendentals=0),
        name="after",
    )(*map(in_hbm, (value, *others)))


def folded_ring(length):
    return [0] + list(range(1, length, 2)) + list(range(2, length, 2))[::-1]


def by_permutes(failed, holders, tokens, expert_ids, gate_levels, weights, owners, capacity):
    tok, top = expert_ids.shape
    width = tokens.shape[1]
    order = folded_ring(owners // 4)
    steps = len(order)
    after = {a: order[(i + 1) % steps] for i, a in enumerate(order)}
    round_ring = [(d, after[d // 4] * 4 + d % 4) for d in range(owners)]
    over_y = [(d, d ^ 2) for d in range(owners)]
    over_core = [(d, d ^ 1) for d in range(owners)]
    move = lambda a, pairs: lax.ppermute(a, "expert", pairs)
    f32 = lambda a: a.astype(jnp.float32)
    add = lambda a, b: (f32(a) + f32(b)).astype(jnp.bfloat16)

    meta = jnp.concatenate([expert_ids.T, gate_levels.T >> 5, gate_levels.T & 31], axis=0)
    meta = meta.astype(jnp.bfloat16).reshape(1, 3 * top * tok)
    meta = jnp.pad(meta, ((0, 7), (0, width - 3 * top * tok)))
    held = [jnp.concatenate([tokens, meta], axis=0)]
    held.append(move(held[0], round_ring))
    across, kept, got = [], [], []
    last = steps - 1

    def add_group(k, shares, *earlier):
        blocks = (held[k], across[k], move(held[k], over_core), move(across[k], over_core))
        keep0, keep1, send, *summed = run_group(
            failed, holders, blocks, weights, shares, earlier, tok, top, capacity
        )
        kept.append((keep0, keep1))
        return send, *summed

    def total(k, rows, *more):
        result = f32(kept[k][0][rows]) + f32(got[k][0, rows])
        for a in more:
            result = result + f32(a)
        return result.astype(jnp.bfloat16)

    across.append(move(held[0], over_y))
    (send,) = add_group(0, ())
    from_y, arrived, own = None, (), None
    every = slice(0, tok)
    for k in range(1, steps):
        across.append(move(across[-1], round_ring) if k == last else move(held[k], over_y))
        if k == 1:
            across[1] = come_after(across[1], kept[0][0])
        if k < last:
            held.append(come_after(move(held[k], round_ring), kept[k - 1][0]))
        got.append(move(come_after(send, across[k], held[min(k + 1, last)]), over_core))
        if k > 2:
            arrived = (move(total(k - 2, every, from_y, *arrived), round_ring),)
        if k > 1:
            from_y = move(add(kept[k - 1][1], got[k - 1][1]), over_y)
        if k == 2:
            send, own = add_group(k, (kept[0][1], got[0]), kept[k - 1][0])
        else:
            (send,) = add_group(k, (), kept[k - 1][0])
    got.append(move(send, over_core))

    halves = (slice(0, tok // 2), slice(tok // 2, tok))
    passing = [
        move(total(last - 1, rows, from_y[rows], *(a[rows] for a in arrived)), round_ring) for rows in halves
    ]
    shares = [move(add(kept[last][1][rows], got[last][1, rows]), over_y) for rows in halves]
    first, second = halves
    passed = total(last, first, shares[0], passing[0])
    follows = total(last, second, shares[1], come_after(passing[1], passed))
    own = move(come_after(own, passed), over_y)
    passed = come_after(move(passed, round_ring), flops=4 * 10**9)
    return total(0, every, own, jnp.concatenate([passed, move(follows, round_ring)], axis=0))


def shards(
    tokens,
    expert_ids,
    gate_levels,
    failed_device,
    replica_holders,
    w_gate,
    w_down,
    spare_gate,
    spare_down,
):
    owners = lax.axis_size("expert")
    tok_count, top_count = expert_ids.shape
    capacity = 2 * tok_count * top_count // owners
    my_index = lax.axis_index("expert").astype(jnp.int32)
    failed_id = failed_device[0]
    holder_row = lax.dynamic_index_in_dim(replica_holders, failed_id, 0, keepdims=False)
    holds = jnp.any(holder_row == my_index).astype(jnp.int32)
    scalars = jnp.stack([my_index, failed_id, holds])
    weights = (w_gate, w_down, spare_gate, spare_down)
    if 12 <= owners <= 32 and owners % 4 == 0 and 3 * top_count * tok_count <= tokens.shape[1]:
        return by_permutes(
            failed_device, replica_holders.T, tokens, expert_ids, gate_levels, weights, owners, capacity
        )
    codes = (expert_ids * LEVELS + gate_levels).T
    all_codes = lax.all_gather(codes, "expert", axis=0)
    all_tokens = lax.all_gather(tokens, "expert", axis=0, tiled=True)
    dense = run_experts(scalars, all_codes, all_tokens, *weights, capacity)
    return lax.psum_scatter(dense, "expert", scatter_dimension=0, tiled=True)


def solution(mesh):
    in_specs = (
        P(("group", "expert"), None),
        P(("group", "expert"), None),
        P(("group", "expert"), None),
        P(),
        P(),
        P("expert", None, None),
        P("expert", None, None),
        P("expert", None, None),
        P("expert", None, None),
    )
    out_specs = P(("group", "expert"), None)
    return jax.shard_map(shards, mesh=mesh, in_specs=in_specs, out_specs=out_specs, check_vma=False)
```

```python
import functools
import jax
import jax.numpy as jnp
from jax import lax
from jax.experimental import pallas as pl
from jax.experimental.pallas import tpu as pltpu
from jax.sharding import PartitionSpec as P

LEVELS = 1024
VMEM_GRANT = 65200 * 1024
TILE = 256


def gated_unit(values):
    return values * (0.5 + 0.5 * jnp.tanh(0.851 * values))


def expert_kernel(
    scalars,
    codes,
    tokens,
    w_gate,
    w_down,
    spare_gate,
    spare_down,
    out,
    rows_in,
    spare_in,
    hidden,
    spare_hidden,
    rows_out,
    *,
    subs,
    sources,
    capacity,
):
    tok = codes.shape[2]
    part = sources * tok
    rows = sources * capacity
    width = tokens.shape[1]
    tile = 512
    my_id, failed_id, holds = scalars[0], scalars[1], scalars[2]
    serves = my_id != failed_id

    before = (
        lax.broadcasted_iota(jnp.int32, (tok, tok), 0)
        < lax.broadcasted_iota(jnp.int32, (tok, tok), 1)
    ).astype(jnp.bfloat16)
    row_iota = lax.broadcasted_iota(jnp.int32, (rows, tok), 0)

    def picker(code, wanted, live):
        named = ((code // LEVELS) == wanted) & live
        mask = jnp.sum(named.astype(jnp.float32), axis=1)
        level = jnp.sum(jnp.where(named, (code % LEVELS), 0).astype(jnp.float32), axis=1) / LEVELS
        rank = jnp.dot(mask.astype(jnp.bfloat16), before, preferred_element_type=jnp.float32)
        picks, weights = [], None
        for s in range(sources):
            place = jnp.where(mask[s : s + 1] > 0, rank[s : s + 1].astype(jnp.int32) + s * capacity, -1)
            hit = row_iota == place
            scaled = jnp.sum(jnp.where(hit, level[s : s + 1], 0.0), axis=1, keepdims=True)
            weights = scaled if weights is None else weights + scaled
            picks.append(hit.astype(jnp.float32).astype(jnp.bfloat16))
        return jnp.concatenate(picks, axis=1), weights

    picks, weights, spare_weights = [], [], []
    for j in range(subs):
        code = codes[j * sources : (j + 1) * sources]
        pick, weight = picker(code, my_id, serves)
        spare_pick, spare_weight = picker(code, failed_id, holds > 0)
        both = jnp.concatenate([pick, spare_pick], axis=0)
        picks.append(both)
        weights.append(weight)
        spare_weights.append(spare_weight)
        for n in range(0, width, tile):
            got = jnp.dot(
                both, tokens[j * part : (j + 1) * part, n : n + tile], preferred_element_type=jnp.float32
            ).astype(jnp.bfloat16)
            rows_in[j * rows : (j + 1) * rows, n : n + tile] = got[:rows]
            spare_in[j * rows : (j + 1) * rows, n : n + tile] = got[rows:]

    for n in range(0, hidden.shape[1], tile):
        hidden[:, n : n + tile] = gated_unit(
            jnp.dot(rows_in[...], w_gate[0, :, n : n + tile], preferred_element_type=jnp.float32)
        ).astype(jnp.bfloat16)
    for n in range(0, width, tile):
        result = jnp.dot(hidden[...], w_down[0, :, n : n + tile], preferred_element_type=jnp.float32)
        result = result.astype(jnp.bfloat16).astype(jnp.float32)
        for j in range(subs):
            rows_out[j, :rows, n : n + tile] = (result[j * rows : (j + 1) * rows] * weights[j]).astype(
                jnp.bfloat16
            )

    @pl.when(holds > 0)
    def _():
        spare_hidden[...] = gated_unit(
            jnp.dot(spare_in[...], spare_gate[0], preferred_element_type=jnp.float32)
        ).astype(jnp.bfloat16)
        for n in range(0, width, tile):
            result = jnp.dot(
                spare_hidden[...], spare_down[0, :, n : n + tile], preferred_element_type=jnp.float32
            )
            for j in range(subs):
                rows_out[j, rows:, n : n + tile] = (
                    result[j * rows : (j + 1) * rows] * spare_weights[j]
                ).astype(jnp.bfloat16)

    @pl.when(holds <= 0)
    def _():
        rows_out[:, rows:, :] = jnp.zeros((subs, rows, width), jnp.bfloat16)

    for j in range(subs):
        for n in range(0, width, tile):
            out[j * part : (j + 1) * part, n : n + tile] = lax.dot_general(
                picks[j],
                rows_out[j, :, n : n + tile],
                (((0,), (0,)), ((), ())),
                preferred_element_type=jnp.float32,
            ).astype(jnp.bfloat16)


def run_experts(scalars, codes, tokens, w_gate, w_down, spare_gate, spare_down, capacity):
    owners, top, tok = codes.shape
    width, inner, spare = w_gate.shape[1], w_gate.shape[2], spare_gate.shape[2]
    sources = max(1, 128 // capacity)
    subs = 2 if sources * tok <= 512 else 1
    step = subs * sources
    rows = sources * capacity
    whole = lambda a: pl.BlockSpec(a.shape, lambda i: (0, 0, 0), pipeline_mode=pl.Buffered(1))
    return pl.pallas_call(
        functools.partial(expert_kernel, subs=subs, sources=sources, capacity=capacity),
        grid=(owners // step,),
        out_shape=jax.ShapeDtypeStruct((owners * tok, width), jnp.bfloat16),
        in_specs=[
            pl.BlockSpec(memory_space=pltpu.SMEM),
            pl.BlockSpec((step, top, tok), lambda i: (i, 0, 0)),
            pl.BlockSpec((step * tok, width), lambda i: (i, 0)),
            whole(w_gate),
            whole(w_down),
            whole(spare_gate),
            whole(spare_down),
        ],
        out_specs=pl.BlockSpec((step * tok, width), lambda i: (i, 0)),
        scratch_shapes=[
            pltpu.VMEM((subs * rows, width), jnp.bfloat16),
            pltpu.VMEM((subs * rows, width), jnp.bfloat16),
            pltpu.VMEM((subs * rows, inner), jnp.bfloat16),
            pltpu.VMEM((subs * rows, spare), jnp.bfloat16),
            pltpu.VMEM((subs, 2 * rows, width), jnp.bfloat16),
        ],
        compiler_params=pltpu.CompilerParams(vmem_limit_bytes=56 * 1024 * 1024),
        cost_estimate=pl.CostEstimate(
            flops=owners * capacity * 4 * width * (inner + spare),
            bytes_accessed=4 * width * (inner + spare) + 4 * owners * tok * width,
            transcendentals=owners * capacity * inner,
        ),
        name="experts",
    )(scalars, codes, tokens, w_gate, w_down, spare_gate, spare_down)


def group_kernel(failed, holders, *refs, others, adds, tok, top, capacity):
    blocks, weights_hbm, shares, refs = refs[:4], refs[4:8], refs[8 : 8 + 2 * adds], refs[8 + 2 * adds + others :]
    keep0, keep1, send = refs[:3]
    far, refs = refs[3 : 3 + adds], refs[3 + adds :]
    held, w_gate, w_down, spare_gate, spare_down = refs[:5]
    rows_in, spare_in, hidden, spare_hidden, rows_out, dense, summed, fetched, stored = refs[5:]
    width, inner = w_gate.shape
    tile = TILE
    my_id, failed_id = lax.axis_index("expert"), failed[0]
    holds = holders[0, failed_id] == my_id
    for j in range(1, holders.shape[0]):
        holds = holds | (holders[j, failed_id] == my_id)
    copies = []

    def fetch(source, target, start=True):
        copy = pltpu.make_async_copy(source, target, fetched.at[len(copies)])
        if start:
            copy.start()
        copies.append(copy)
        return copy

    gate_hbm, down_hbm, spare_gate_hbm, spare_down_hbm = weights_hbm
    block_copies = [fetch(block, held.at[s]) for s, block in enumerate(blocks)]
    gate_copies = [
        fetch(gate_hbm.at[0, :, n : n + tile], w_gate.at[:, n : n + tile]) for n in range(0, inner, tile)
    ]
    share_copies = []
    if adds:
        share_copies = [fetch(shares[0], summed.at[0]), fetch(shares[1].at[1], summed.at[1])]
    spare_copies = [
        fetch(spare_gate_hbm.at[0], spare_gate, False),
        fetch(spare_down_hbm.at[0], spare_down, False),
    ]

    @pl.when(holds)
    def _():
        for copy in spare_copies:
            copy.start()

    down_copies = [
        fetch(down_hbm.at[0, :, n : n + tile], w_down.at[:, n : n + tile]) for n in range(0, width, tile)
    ]

    count = len(blocks)
    before = (
        lax.broadcasted_iota(jnp.int32, (tok, tok), 0)
        < lax.broadcasted_iota(jnp.int32, (tok, tok), 1)
    ).astype(jnp.float32).astype(jnp.bfloat16)
    own = lax.broadcasted_iota(jnp.int32, (2 * count, tok), 0) < count
    wanted = jnp.where(own, my_id, failed_id).astype(jnp.float32)
    serves = jnp.where(my_id != failed_id, 1.0, 0.0)
    live = jnp.where(own, serves, jnp.where(holds, 1.0, 0.0))
    slots = 2 * capacity
    row_iota = lax.broadcasted_iota(jnp.int32, (slots, tok), 0)
    lane_iota = lax.broadcasted_iota(jnp.int32, (tok, slots), 1)

    for copy in block_copies:
        copy.wait()
    meta = jnp.concatenate([held[s, tok : tok + 8, :].astype(jnp.float32)[:1] for s in range(count)] * 2, axis=0)
    mask = jnp.zeros((2 * count, tok), jnp.float32)
    level = jnp.zeros((2 * count, tok), jnp.float32)
    for k in range(top):
        named = jnp.where(meta[:, k * tok : (k + 1) * tok] == wanted, live, 0.0)
        high = meta[:, (top + k) * tok : (top + k + 1) * tok]
        low = meta[:, (2 * top + k) * tok : (2 * top + k + 1) * tok]
        mask = mask + named
        level = level + named * ((high * 32.0 + low) / LEVELS)
    rank = jnp.dot(mask.astype(jnp.bfloat16), before, preferred_element_type=jnp.float32)
    place = jnp.where(mask > 0, rank + jnp.where(own, 0.0, float(capacity)), -1.0)
    place_rows = place.astype(jnp.int32)
    place_columns = place.T.astype(jnp.int32)

    spreads, weights = [], []
    for s in range(count):
        here, there = place_rows[s : s + 1], place_rows[count + s : count + s + 1]
        hit_here, hit_there = row_iota == here, row_iota == there
        pick = jnp.where(hit_here | hit_there, 1.0, 0.0).astype(jnp.bfloat16)
        weights.append(
            jnp.sum(
                jnp.where(hit_here, level[s : s + 1], 0.0)
                + jnp.where(hit_there, level[count + s : count + s + 1], 0.0),
                axis=1,
                keepdims=True,
            )
        )
        here, there = place_columns[:, s : s + 1], place_columns[:, count + s : count + s + 1]
        spreads.append(jnp.where((lane_iota == here) | (lane_iota == there), 1.0, 0.0).astype(jnp.bfloat16))
        for n in range(0, width, tile):
            got = jnp.dot(pick, held[s, :tok, n : n + tile], preferred_element_type=jnp.float32).astype(
                jnp.bfloat16
            )
            rows_in[s * capacity : (s + 1) * capacity, n : n + tile] = got[:capacity]
            spare_in[s * capacity : (s + 1) * capacity, n : n + tile] = got[capacity:]

    for i, n in enumerate(range(0, inner, tile)):
        gate_copies[i].wait()
        hidden[:, n : n + tile] = gated_unit(
            jnp.dot(rows_in[...], w_gate[:, n : n + tile], preferred_element_type=jnp.float32)
        ).astype(jnp.bfloat16)
    stores = []
    if adds:
        for copy in share_copies:
            copy.wait()
        total = summed[0].astype(jnp.float32) + summed[1].astype(jnp.float32)
        summed[0] = total.astype(jnp.bfloat16)
        stores.append(pltpu.make_async_copy(summed.at[0], far[0], stored.at[0]))
        stores[0].start()

    @pl.when(holds)
    def _():
        for copy in spare_copies:
            copy.wait()
        spare_hidden[...] = gated_unit(
            jnp.dot(spare_in[...], spare_gate[...], preferred_element_type=jnp.float32)
        ).astype(jnp.bfloat16)
        for n in range(0, width, tile):
            result = jnp.dot(
                spare_hidden[...], spare_down[:, n : n + tile], preferred_element_type=jnp.float32
            )
            for s in range(count):
                rows_out[s, capacity:, n : n + tile] = (
                    result[s * capacity : (s + 1) * capacity] * weights[s][capacity:]
                ).astype(jnp.bfloat16)

    @pl.when(jnp.logical_not(holds))
    def _():
        rows_out[:, capacity:, :] = jnp.zeros((count, capacity, width), jnp.bfloat16)

    for i, n in enumerate(range(0, width, tile)):
        down_copies[i].wait()
        result = jnp.dot(hidden[...], w_down[:, n : n + tile], preferred_element_type=jnp.float32)
        result = result.astype(jnp.bfloat16).astype(jnp.float32)
        for s in range(count):
            rows_out[s, :capacity, n : n + tile] = (
                result[s * capacity : (s + 1) * capacity] * weights[s][:capacity]
            ).astype(jnp.bfloat16)
            dense[s, :, n : n + tile] = jnp.dot(
                spreads[s], rows_out[s, :, n : n + tile], preferred_element_type=jnp.float32
            ).astype(jnp.bfloat16)
            target = (keep0, keep1, send.at[0], send.at[1])[s]
            stores.append(
                pltpu.make_async_copy(
                    dense.at[s, :, n : n + tile], target.at[:, n : n + tile], stored.at[len(stores)]
                )
            )
            stores[-1].start()
    for copy in stores:
        copy.wait()


def run_group(failed, holders, blocks, weights, shares, earlier, tok, top, capacity):
    width, inner, spare = weights[0].shape[1], weights[0].shape[2], weights[2].shape[2]
    count, adds = len(blocks), len(shares) // 2
    rows = count * capacity
    hbm = pl.BlockSpec(memory_space=pl.ANY)
    smem = pl.BlockSpec(memory_space=pltpu.SMEM)
    block = pltpu.HBM((tok, width), jnp.bfloat16)
    return pl.pallas_call(
        functools.partial(
            group_kernel, others=len(earlier), adds=adds, tok=tok, top=top, capacity=capacity
        ),
        out_shape=(block, block, pltpu.HBM((2, tok, width), jnp.bfloat16)) + (block,) * adds,
        in_specs=[smem, smem] + [hbm] * (count + 4 + len(shares) + len(earlier)),
        out_specs=(hbm,) * (3 + adds),
        scratch_shapes=[
            pltpu.VMEM((count, *blocks[0].shape), jnp.bfloat16),
            pltpu.VMEM((width, inner), jnp.bfloat16),
            pltpu.VMEM((inner, width), jnp.bfloat16),
            pltpu.VMEM((width, spare), jnp.bfloat16),
            pltpu.VMEM((spare, width), jnp.bfloat16),
            pltpu.VMEM((rows, width), jnp.bfloat16),
            pltpu.VMEM((rows, width), jnp.bfloat16),
            pltpu.VMEM((rows, inner), jnp.bfloat16),
            pltpu.VMEM((rows, spare), jnp.bfloat16),
            pltpu.VMEM((count, 2 * capacity, width), jnp.bfloat16),
            pltpu.VMEM((count, tok, width), jnp.bfloat16),
            pltpu.VMEM((2, tok, width), jnp.bfloat16),
            pltpu.SemaphoreType.DMA((count + inner // TILE + width // TILE + 4,)),
            pltpu.SemaphoreType.DMA((1 + count * (width // TILE),)),
        ],
        compiler_params=pltpu.CompilerParams(vmem_limit_bytes=VMEM_GRANT),
        cost_estimate=pl.CostEstimate(
            flops=rows * 4 * width * (inner + spare),
            bytes_accessed=4 * width * (inner + spare) + 4 * count * tok * width,
            transcendentals=rows * inner,
        ),
        name="group",
    )(failed, holders, *map(in_hbm, (*blocks, *weights, *shares, *earlier)))


def in_hbm(array):
    return pltpu.with_memory_space_constraint(array, pltpu.HBM)


def nothing(*refs):
    pass


def come_after(value, *others, flops=0):
    return pl.pallas_call(
        nothing,
        out_shape=pltpu.HBM(value.shape, value.dtype),
        in_specs=[pl.BlockSpec(memory_space=pl.ANY)] * (1 + len(others)),
        out_specs=pl.BlockSpec(memory_space=pl.ANY),
        input_output_aliases={0: 0},
        compiler_params=pltpu.CompilerParams(vmem_limit_bytes=VMEM_GRANT),
        cost_estimate=pl.CostEstimate(flops=flops, bytes_accessed=0, transcendentals=0),
        name="after",
    )(*map(in_hbm, (value, *others)))


def folded_ring(length):
    return [0] + list(range(1, length, 2)) + list(range(2, length, 2))[::-1]


def by_permutes(failed, holders, tokens, expert_ids, gate_levels, weights, owners, capacity):
    tok, top = expert_ids.shape
    width = tokens.shape[1]
    order = folded_ring(owners // 4)
    steps = len(order)
    after = {a: order[(i + 1) % steps] for i, a in enumerate(order)}
    round_ring = [(d, after[d // 4] * 4 + d % 4) for d in range(owners)]
    over_y = [(d, d ^ 2) for d in range(owners)]
    over_core = [(d, d ^ 1) for d in range(owners)]
    move = lambda a, pairs: lax.ppermute(a, "expert", pairs)
    f32 = lambda a: a.astype(jnp.float32)
    add = lambda a, b: (f32(a) + f32(b)).astype(jnp.bfloat16)

    meta = jnp.concatenate([expert_ids.T, gate_levels.T >> 5, gate_levels.T & 31], axis=0)
    meta = meta.astype(jnp.bfloat16).reshape(1, 3 * top * tok)
    meta = jnp.pad(meta, ((0, 7), (0, width - 3 * top * tok)))
    held = [jnp.concatenate([tokens, meta], axis=0)]
    held.append(move(held[0], round_ring))
    across, kept, got = [], [], []
    last = steps - 1

    def add_group(k, shares, *earlier):
        blocks = (held[k], across[k], move(held[k], over_core), move(across[k], over_core))
        keep0, keep1, send, *summed = run_group(
            failed, holders, blocks, weights, shares, earlier, tok, top, capacity
        )
        kept.append((keep0, keep1))
        return send, *summed

    def total(k, rows, *more):
        result = f32(kept[k][0][rows]) + f32(got[k][0, rows])
        for a in more:
            result = result + f32(a)
        return result.astype(jnp.bfloat16)

    across.append(move(held[0], over_y))
    (send,) = add_group(0, ())
    from_y, arrived, own = None, (), None
    every = slice(0, tok)
    for k in range(1, steps):
        across.append(move(across[-1], round_ring) if k == last else move(held[k], over_y))
        if k == 1:
            across[1] = come_after(across[1], kept[0][0])
        if k < last:
            held.append(come_after(move(held[k], round_ring), kept[k - 1][0]))
        got.append(move(come_after(send, across[k], held[min(k + 1, last)]), over_core))
        if k > 2:
            arrived = (move(total(k - 2, every, from_y, *arrived), round_ring),)
        if k > 1:
            from_y = move(add(kept[k - 1][1], got[k - 1][1]), over_y)
        if k == 2:
            send, own = add_group(k, (kept[0][1], got[0]), kept[k - 1][0])
        else:
            (send,) = add_group(k, (), kept[k - 1][0])
    got.append(move(send, over_core))

    halves = (slice(0, tok // 2), slice(tok // 2, tok))
    passing = [
        move(total(last - 1, rows, from_y[rows], *(a[rows] for a in arrived)), round_ring) for rows in halves
    ]
    shares = [move(add(kept[last][1][rows], got[last][1, rows]), over_y) for rows in halves]
    first, second = halves
    passed = total(last, first, shares[0], passing[0])
    follows = total(last, second, shares[1], come_after(passing[1], passed))
    own = move(come_after(own, passed), over_y)
    passed = come_after(move(passed, round_ring), flops=4 * 10**9)
    return total(0, every, own, jnp.concatenate([passed, move(follows, round_ring)], axis=0))


def shards(
    tokens,
    expert_ids,
    gate_levels,
    failed_device,
    replica_holders,
    w_gate,
    w_down,
    spare_gate,
    spare_down,
):
    owners = lax.axis_size("expert")
    tok_count, top_count = expert_ids.shape
    capacity = 2 * tok_count * top_count // owners
    my_index = lax.axis_index("expert").astype(jnp.int32)
    failed_id = failed_device[0]
    holder_row = lax.dynamic_index_in_dim(replica_holders, failed_id, 0, keepdims=False)
    holds = jnp.any(holder_row == my_index).astype(jnp.int32)
    scalars = jnp.stack([my_index, failed_id, holds])
    weights = (w_gate, w_down, spare_gate, spare_down)
    if 12 <= owners <= 32 and owners % 4 == 0 and 3 * top_count * tok_count <= tokens.shape[1]:
        return by_permutes(
            failed_device, replica_holders.T, tokens, expert_ids, gate_levels, weights, owners, capacity
        )
    codes = (expert_ids * LEVELS + gate_levels).T
    all_codes = lax.all_gather(codes, "expert", axis=0)
    all_tokens = lax.all_gather(tokens, "expert", axis=0, tiled=True)
    dense = run_experts(scalars, all_codes, all_tokens, *weights, capacity)
    return lax.psum_scatter(dense, "expert", scatter_dimension=0, tiled=True)


def solution(mesh):
    in_specs = (
        P(("group", "expert"), None),
        P(("group", "expert"), None),
        P(("group", "expert"), None),
        P(),
        P(),
        P("expert", None, None),
        P("expert", None, None),
        P("expert", None, None),
        P("expert", None, None),
    )
    out_specs = P(("group", "expert"), None)
    return jax.shard_map(shards, mesh=mesh, in_specs=in_specs, out_specs=out_specs, check_vma=False)
```

```python
import functools
import jax
import jax.numpy as jnp
from jax import lax
from jax.experimental import pallas as pl
from jax.experimental.pallas import tpu as pltpu
from jax.sharding import PartitionSpec as P

LEVELS = 1024
VMEM_GRANT = 65200 * 1024


def gated_unit(values):
    return values * (0.5 + 0.5 * jnp.tanh(0.851 * values))


def expert_kernel(
    scalars,
    codes,
    tokens,
    w_gate,
    w_down,
    spare_gate,
    spare_down,
    out,
    rows_in,
    spare_in,
    hidden,
    spare_hidden,
    rows_out,
    *,
    subs,
    sources,
    capacity,
):
    tok = codes.shape[2]
    part = sources * tok
    rows = sources * capacity
    width = tokens.shape[1]
    tile = 512
    my_id, failed_id, holds = scalars[0], scalars[1], scalars[2]
    serves = my_id != failed_id

    before = (
        lax.broadcasted_iota(jnp.int32, (tok, tok), 0)
        < lax.broadcasted_iota(jnp.int32, (tok, tok), 1)
    ).astype(jnp.bfloat16)
    row_iota = lax.broadcasted_iota(jnp.int32, (rows, tok), 0)

    def picker(code, wanted, live):
        named = ((code // LEVELS) == wanted) & live
        mask = jnp.sum(named.astype(jnp.float32), axis=1)
        level = jnp.sum(jnp.where(named, (code % LEVELS), 0).astype(jnp.float32), axis=1) / LEVELS
        rank = jnp.dot(mask.astype(jnp.bfloat16), before, preferred_element_type=jnp.float32)
        picks, weights = [], None
        for s in range(sources):
            place = jnp.where(mask[s : s + 1] > 0, rank[s : s + 1].astype(jnp.int32) + s * capacity, -1)
            hit = row_iota == place
            scaled = jnp.sum(jnp.where(hit, level[s : s + 1], 0.0), axis=1, keepdims=True)
            weights = scaled if weights is None else weights + scaled
            picks.append(hit.astype(jnp.float32).astype(jnp.bfloat16))
        return jnp.concatenate(picks, axis=1), weights

    picks, weights, spare_weights = [], [], []
    for j in range(subs):
        code = codes[j * sources : (j + 1) * sources]
        pick, weight = picker(code, my_id, serves)
        spare_pick, spare_weight = picker(code, failed_id, holds > 0)
        both = jnp.concatenate([pick, spare_pick], axis=0)
        picks.append(both)
        weights.append(weight)
        spare_weights.append(spare_weight)
        for n in range(0, width, tile):
            got = jnp.dot(
                both, tokens[j * part : (j + 1) * part, n : n + tile], preferred_element_type=jnp.float32
            ).astype(jnp.bfloat16)
            rows_in[j * rows : (j + 1) * rows, n : n + tile] = got[:rows]
            spare_in[j * rows : (j + 1) * rows, n : n + tile] = got[rows:]

    for n in range(0, hidden.shape[1], tile):
        hidden[:, n : n + tile] = gated_unit(
            jnp.dot(rows_in[...], w_gate[0, :, n : n + tile], preferred_element_type=jnp.float32)
        ).astype(jnp.bfloat16)
    for n in range(0, width, tile):
        result = jnp.dot(hidden[...], w_down[0, :, n : n + tile], preferred_element_type=jnp.float32)
        result = result.astype(jnp.bfloat16).astype(jnp.float32)
        for j in range(subs):
            rows_out[j, :rows, n : n + tile] = (result[j * rows : (j + 1) * rows] * weights[j]).astype(
                jnp.bfloat16
            )

    @pl.when(holds > 0)
    def _():
        spare_hidden[...] = gated_unit(
            jnp.dot(spare_in[...], spare_gate[0], preferred_element_type=jnp.float32)
        ).astype(jnp.bfloat16)
        for n in range(0, width, tile):
            result = jnp.dot(
                spare_hidden[...], spare_down[0, :, n : n + tile], preferred_element_type=jnp.float32
            )
            for j in range(subs):
                rows_out[j, rows:, n : n + tile] = (
                    result[j * rows : (j + 1) * rows] * spare_weights[j]
                ).astype(jnp.bfloat16)

    @pl.when(holds <= 0)
    def _():
        rows_out[:, rows:, :] = jnp.zeros((subs, rows, width), jnp.bfloat16)

    for j in range(subs):
        for n in range(0, width, tile):
            out[j * part : (j + 1) * part, n : n + tile] = lax.dot_general(
                picks[j],
                rows_out[j, :, n : n + tile],
                (((0,), (0,)), ((), ())),
                preferred_element_type=jnp.float32,
            ).astype(jnp.bfloat16)


def run_experts(scalars, codes, tokens, w_gate, w_down, spare_gate, spare_down, capacity):
    owners, top, tok = codes.shape
    width, inner, spare = w_gate.shape[1], w_gate.shape[2], spare_gate.shape[2]
    sources = max(1, 128 // capacity)
    subs = 2 if sources * tok <= 512 else 1
    step = subs * sources
    rows = sources * capacity
    whole = lambda a: pl.BlockSpec(a.shape, lambda i: (0, 0, 0), pipeline_mode=pl.Buffered(1))
    return pl.pallas_call(
        functools.partial(expert_kernel, subs=subs, sources=sources, capacity=capacity),
        grid=(owners // step,),
        out_shape=jax.ShapeDtypeStruct((owners * tok, width), jnp.bfloat16),
        in_specs=[
            pl.BlockSpec(memory_space=pltpu.SMEM),
            pl.BlockSpec((step, top, tok), lambda i: (i, 0, 0)),
            pl.BlockSpec((step * tok, width), lambda i: (i, 0)),
            whole(w_gate),
            whole(w_down),
            whole(spare_gate),
            whole(spare_down),
        ],
        out_specs=pl.BlockSpec((step * tok, width), lambda i: (i, 0)),
        scratch_shapes=[
            pltpu.VMEM((subs * rows, width), jnp.bfloat16),
            pltpu.VMEM((subs * rows, width), jnp.bfloat16),
            pltpu.VMEM((subs * rows, inner), jnp.bfloat16),
            pltpu.VMEM((subs * rows, spare), jnp.bfloat16),
            pltpu.VMEM((subs, 2 * rows, width), jnp.bfloat16),
        ],
        compiler_params=pltpu.CompilerParams(vmem_limit_bytes=56 * 1024 * 1024),
        cost_estimate=pl.CostEstimate(
            flops=owners * capacity * 4 * width * (inner + spare),
            bytes_accessed=4 * width * (inner + spare) + 4 * owners * tok * width,
            transcendentals=owners * capacity * inner,
        ),
        name="experts",
    )(scalars, codes, tokens, w_gate, w_down, spare_gate, spare_down)


def group_kernel(failed, holders, *refs, others, adds, tok, top, capacity):
    blocks, weights_hbm, shares, refs = refs[:4], refs[4:8], refs[8 : 8 + 2 * adds], refs[8 + 2 * adds + others :]
    keep0, keep1, send = refs[:3]
    far, refs = refs[3 : 3 + adds], refs[3 + adds :]
    held, w_gate, w_down, spare_gate, spare_down = refs[:5]
    rows_in, spare_in, hidden, spare_hidden, rows_out, dense, summed, fetched, stored = refs[5:]
    width, inner = w_gate.shape
    tile = 512
    my_id, failed_id = lax.axis_index("expert"), failed[0]
    holds = holders[0, failed_id] == my_id
    for j in range(1, holders.shape[0]):
        holds = holds | (holders[j, failed_id] == my_id)
    copies = []

    def fetch(source, target, start=True):
        copy = pltpu.make_async_copy(source, target, fetched.at[len(copies)])
        if start:
            copy.start()
        copies.append(copy)
        return copy

    gate_hbm, down_hbm, spare_gate_hbm, spare_down_hbm = weights_hbm
    block_copies = [fetch(block, held.at[s]) for s, block in enumerate(blocks)]
    gate_copies = [
        fetch(gate_hbm.at[0, n : n + tile], w_gate.at[n : n + tile]) for n in range(0, width, tile)
    ]
    share_copies = []
    if adds:
        share_copies = [fetch(shares[0], summed.at[0]), fetch(shares[1].at[1], summed.at[1])]
    spare_copies = [
        fetch(spare_gate_hbm.at[0], spare_gate, False),
        fetch(spare_down_hbm.at[0], spare_down, False),
    ]

    @pl.when(holds)
    def _():
        for copy in spare_copies:
            copy.start()

    down_copies = [
        fetch(down_hbm.at[0, n : n + tile], w_down.at[n : n + tile]) for n in range(0, inner, tile)
    ]

    count = len(blocks)
    before = (
        lax.broadcasted_iota(jnp.int32, (tok, tok), 0)
        < lax.broadcasted_iota(jnp.int32, (tok, tok), 1)
    ).astype(jnp.float32).astype(jnp.bfloat16)
    own = lax.broadcasted_iota(jnp.int32, (2 * count, tok), 0) < count
    wanted = jnp.where(own, my_id, failed_id).astype(jnp.float32)
    serves = jnp.where(my_id != failed_id, 1.0, 0.0)
    live = jnp.where(own, serves, jnp.where(holds, 1.0, 0.0))
    slots = 2 * capacity
    row_iota = lax.broadcasted_iota(jnp.int32, (slots, tok), 0)
    lane_iota = lax.broadcasted_iota(jnp.int32, (tok, slots), 1)

    for copy in block_copies:
        copy.wait()
    meta = jnp.concatenate([held[s, tok : tok + 8, :].astype(jnp.float32)[:1] for s in range(count)] * 2, axis=0)
    mask = jnp.zeros((2 * count, tok), jnp.float32)
    level = jnp.zeros((2 * count, tok), jnp.float32)
    for k in range(top):
        named = jnp.where(meta[:, k * tok : (k + 1) * tok] == wanted, live, 0.0)
        high = meta[:, (top + k) * tok : (top + k + 1) * tok]
        low = meta[:, (2 * top + k) * tok : (2 * top + k + 1) * tok]
        mask = mask + named
        level = level + named * ((high * 32.0 + low) / LEVELS)
    rank = jnp.dot(mask.astype(jnp.bfloat16), before, preferred_element_type=jnp.float32)
    place = jnp.where(mask > 0, rank + jnp.where(own, 0.0, float(capacity)), -1.0)
    place_rows = place.astype(jnp.int32)
    place_columns = place.T.astype(jnp.int32)

    spreads, weights = [], []
    for s in range(count):
        here, there = place_rows[s : s + 1], place_rows[count + s : count + s + 1]
        hit_here, hit_there = row_iota == here, row_iota == there
        pick = jnp.where(hit_here | hit_there, 1.0, 0.0).astype(jnp.bfloat16)
        weights.append(
            jnp.sum(
                jnp.where(hit_here, level[s : s + 1], 0.0)
                + jnp.where(hit_there, level[count + s : count + s + 1], 0.0),
                axis=1,
                keepdims=True,
            )
        )
        here, there = place_columns[:, s : s + 1], place_columns[:, count + s : count + s + 1]
        spreads.append(jnp.where((lane_iota == here) | (lane_iota == there), 1.0, 0.0).astype(jnp.bfloat16))
        for n in range(0, width, tile):
            got = jnp.dot(pick, held[s, :tok, n : n + tile], preferred_element_type=jnp.float32).astype(
                jnp.bfloat16
            )
            rows_in[s * capacity : (s + 1) * capacity, n : n + tile] = got[:capacity]
            spare_in[s * capacity : (s + 1) * capacity, n : n + tile] = got[capacity:]

    for copy in gate_copies:
        copy.wait()
    for n in range(0, inner, tile):
        hidden[:, n : n + tile] = gated_unit(
            jnp.dot(rows_in[...], w_gate[:, n : n + tile], preferred_element_type=jnp.float32)
        ).astype(jnp.bfloat16)
    stores = []
    if adds:
        for copy in share_copies:
            copy.wait()
        total = summed[0].astype(jnp.float32) + summed[1].astype(jnp.float32)
        summed[0] = total.astype(jnp.bfloat16)
        stores.append(pltpu.make_async_copy(summed.at[0], far[0], stored.at[0]))
        stores[0].start()

    @pl.when(holds)
    def _():
        for copy in spare_copies:
            copy.wait()
        spare_hidden[...] = gated_unit(
            jnp.dot(spare_in[...], spare_gate[...], preferred_element_type=jnp.float32)
        ).astype(jnp.bfloat16)
        for n in range(0, width, tile):
            result = jnp.dot(
                spare_hidden[...], spare_down[:, n : n + tile], preferred_element_type=jnp.float32
            )
            for s in range(count):
                rows_out[s, capacity:, n : n + tile] = (
                    result[s * capacity : (s + 1) * capacity] * weights[s][capacity:]
                ).astype(jnp.bfloat16)

    @pl.when(jnp.logical_not(holds))
    def _():
        rows_out[:, capacity:, :] = jnp.zeros((count, capacity, width), jnp.bfloat16)

    for copy in down_copies:
        copy.wait()
    for n in range(0, width, tile):
        result = jnp.dot(hidden[...], w_down[:, n : n + tile], preferred_element_type=jnp.float32)
        result = result.astype(jnp.bfloat16).astype(jnp.float32)
        for s in range(count):
            rows_out[s, :capacity, n : n + tile] = (
                result[s * capacity : (s + 1) * capacity] * weights[s][:capacity]
            ).astype(jnp.bfloat16)
            dense[s, :, n : n + tile] = jnp.dot(
                spreads[s], rows_out[s, :, n : n + tile], preferred_element_type=jnp.float32
            ).astype(jnp.bfloat16)
            target = (keep0, keep1, send.at[0], send.at[1])[s]
            stores.append(
                pltpu.make_async_copy(
                    dense.at[s, :, n : n + tile], target.at[:, n : n + tile], stored.at[len(stores)]
                )
            )
            stores[-1].start()
    for copy in stores:
        copy.wait()


def run_group(failed, holders, blocks, weights, shares, earlier, tok, top, capacity):
    width, inner, spare = weights[0].shape[1], weights[0].shape[2], weights[2].shape[2]
    count, adds = len(blocks), len(shares) // 2
    rows = count * capacity
    hbm = pl.BlockSpec(memory_space=pl.ANY)
    smem = pl.BlockSpec(memory_space=pltpu.SMEM)
    block = pltpu.HBM((tok, width), jnp.bfloat16)
    return pl.pallas_call(
        functools.partial(
            group_kernel, others=len(earlier), adds=adds, tok=tok, top=top, capacity=capacity
        ),
        out_shape=(block, block, pltpu.HBM((2, tok, width), jnp.bfloat16)) + (block,) * adds,
        in_specs=[smem, smem] + [hbm] * (count + 4 + len(shares) + len(earlier)),
        out_specs=(hbm,) * (3 + adds),
        scratch_shapes=[
            pltpu.VMEM((count, *blocks[0].shape), jnp.bfloat16),
            pltpu.VMEM((width, inner), jnp.bfloat16),
            pltpu.VMEM((inner, width), jnp.bfloat16),
            pltpu.VMEM((width, spare), jnp.bfloat16),
            pltpu.VMEM((spare, width), jnp.bfloat16),
            pltpu.VMEM((rows, width), jnp.bfloat16),
            pltpu.VMEM((rows, width), jnp.bfloat16),
            pltpu.VMEM((rows, inner), jnp.bfloat16),
            pltpu.VMEM((rows, spare), jnp.bfloat16),
            pltpu.VMEM((count, 2 * capacity, width), jnp.bfloat16),
            pltpu.VMEM((count, tok, width), jnp.bfloat16),
            pltpu.VMEM((2, tok, width), jnp.bfloat16),
            pltpu.SemaphoreType.DMA((count + inner // 512 + width // 512 + 4,)),
            pltpu.SemaphoreType.DMA((1 + count * (width // 512),)),
        ],
        compiler_params=pltpu.CompilerParams(vmem_limit_bytes=VMEM_GRANT),
        cost_estimate=pl.CostEstimate(
            flops=rows * 4 * width * (inner + spare),
            bytes_accessed=4 * width * (inner + spare) + 4 * count * tok * width,
            transcendentals=rows * inner,
        ),
        name="group",
    )(failed, holders, *map(in_hbm, (*blocks, *weights, *shares, *earlier)))


def in_hbm(array):
    return pltpu.with_memory_space_constraint(array, pltpu.HBM)


def nothing(*refs):
    pass


def come_after(value, *others, flops=0):
    return pl.pallas_call(
        nothing,
        out_shape=pltpu.HBM(value.shape, value.dtype),
        in_specs=[pl.BlockSpec(memory_space=pl.ANY)] * (1 + len(others)),
        out_specs=pl.BlockSpec(memory_space=pl.ANY),
        input_output_aliases={0: 0},
        compiler_params=pltpu.CompilerParams(vmem_limit_bytes=VMEM_GRANT),
        cost_estimate=pl.CostEstimate(flops=flops, bytes_accessed=0, transcendentals=0),
        name="after",
    )(*map(in_hbm, (value, *others)))


def folded_ring(length):
    return [0] + list(range(1, length, 2)) + list(range(2, length, 2))[::-1]


def by_permutes(failed, holders, tokens, expert_ids, gate_levels, weights, owners, capacity):
    tok, top = expert_ids.shape
    width = tokens.shape[1]
    order = folded_ring(owners // 4)
    steps = len(order)
    after = {a: order[(i + 1) % steps] for i, a in enumerate(order)}
    round_ring = [(d, after[d // 4] * 4 + d % 4) for d in range(owners)]
    over_y = [(d, d ^ 2) for d in range(owners)]
    over_core = [(d, d ^ 1) for d in range(owners)]
    move = lambda a, pairs: lax.ppermute(a, "expert", pairs)
    f32 = lambda a: a.astype(jnp.float32)
    add = lambda a, b: (f32(a) + f32(b)).astype(jnp.bfloat16)

    meta = jnp.concatenate([expert_ids.T, gate_levels.T >> 5, gate_levels.T & 31], axis=0)
    meta = meta.astype(jnp.bfloat16).reshape(1, 3 * top * tok)
    meta = jnp.pad(meta, ((0, 7), (0, width - 3 * top * tok)))
    held = [jnp.concatenate([tokens, meta], axis=0)]
    held.append(move(held[0], round_ring))
    across, kept, got = [], [], []
    last = steps - 1

    def add_group(k, shares, *earlier):
        blocks = (held[k], across[k], move(held[k], over_core), move(across[k], over_core))
        keep0, keep1, send, *summed = run_group(
            failed, holders, blocks, weights, shares, earlier, tok, top, capacity
        )
        kept.append((keep0, keep1))
        return send, *summed

    def total(k, rows, *more):
        result = f32(kept[k][0][rows]) + f32(got[k][0, rows])
        for a in more:
            result = result + f32(a)
        return result.astype(jnp.bfloat16)

    across.append(move(held[0], over_y))
    (send,) = add_group(0, ())
    from_y, arrived, own = None, (), None
    every = slice(0, tok)
    for k in range(1, steps):
        across.append(move(across[-1], round_ring) if k == last else move(held[k], over_y))
        if k == 1:
            across[1] = come_after(across[1], kept[0][0])
        if k < last:
            held.append(come_after(move(held[k], round_ring), kept[k - 1][0]))
        got.append(move(come_after(send, across[k], held[min(k + 1, last)]), over_core))
        if k > 2:
            arrived = (move(total(k - 2, every, from_y, *arrived), round_ring),)
        if k > 1:
            from_y = move(add(kept[k - 1][1], got[k - 1][1]), over_y)
        if k == 2:
            send, own = add_group(k, (kept[0][1], got[0]), kept[k - 1][0])
        else:
            (send,) = add_group(k, (), kept[k - 1][0])
    got.append(move(send, over_core))

    halves = (slice(0, tok // 2), slice(tok // 2, tok))
    passing = [
        move(total(last - 1, rows, from_y[rows], *(a[rows] for a in arrived)), round_ring) for rows in halves
    ]
    shares = [move(add(kept[last][1][rows], got[last][1, rows]), over_y) for rows in halves]
    first, second = halves
    passed = total(last, first, shares[0], passing[0])
    follows = total(last, second, shares[1], come_after(passing[1], passed))
    own = move(come_after(own, passed), over_y)
    passed = come_after(move(passed, round_ring), flops=4 * 10**9)
    return total(0, every, own, jnp.concatenate([passed, move(follows, round_ring)], axis=0))


def shards(
    tokens,
    expert_ids,
    gate_levels,
    failed_device,
    replica_holders,
    w_gate,
    w_down,
    spare_gate,
    spare_down,
):
    owners = lax.axis_size("expert")
    tok_count, top_count = expert_ids.shape
    capacity = 2 * tok_count * top_count // owners
    my_index = lax.axis_index("expert").astype(jnp.int32)
    failed_id = failed_device[0]
    holder_row = lax.dynamic_index_in_dim(replica_holders, failed_id, 0, keepdims=False)
    holds = jnp.any(holder_row == my_index).astype(jnp.int32)
    scalars = jnp.stack([my_index, failed_id, holds])
    weights = (w_gate, w_down, spare_gate, spare_down)
    if 12 <= owners <= 32 and owners % 4 == 0 and 3 * top_count * tok_count <= tokens.shape[1]:
        return by_permutes(
            failed_device, replica_holders.T, tokens, expert_ids, gate_levels, weights, owners, capacity
        )
    codes = (expert_ids * LEVELS + gate_levels).T
    all_codes = lax.all_gather(codes, "expert", axis=0)
    all_tokens = lax.all_gather(tokens, "expert", axis=0, tiled=True)
    dense = run_experts(scalars, all_codes, all_tokens, *weights, capacity)
    return lax.psum_scatter(dense, "expert", scatter_dimension=0, tiled=True)


def solution(mesh):
    in_specs = (
        P(("group", "expert"), None),
        P(("group", "expert"), None),
        P(("group", "expert"), None),
        P(),
        P(),
        P("expert", None, None),
        P("expert", None, None),
        P("expert", None, None),
        P("expert", None, None),
    )
    out_specs = P(("group", "expert"), None)
    return jax.shard_map(shards, mesh=mesh, in_specs=in_specs, out_specs=out_specs, check_vma=False)
```

```python
import functools
import jax
import jax.numpy as jnp
from jax import lax
from jax.experimental import pallas as pl
from jax.experimental.pallas import tpu as pltpu
from jax.sharding import PartitionSpec as P

LEVELS = 1024
VMEM_GRANT = 65200 * 1024


def gated_unit(values):
    return values * (0.5 + 0.5 * jnp.tanh(0.851 * values))


def expert_kernel(
    scalars,
    codes,
    tokens,
    w_gate,
    w_down,
    spare_gate,
    spare_down,
    out,
    rows_in,
    spare_in,
    hidden,
    spare_hidden,
    rows_out,
    *,
    subs,
    sources,
    capacity,
):
    tok = codes.shape[2]
    part = sources * tok
    rows = sources * capacity
    width = tokens.shape[1]
    tile = 512
    my_id, failed_id, holds = scalars[0], scalars[1], scalars[2]
    serves = my_id != failed_id

    before = (
        lax.broadcasted_iota(jnp.int32, (tok, tok), 0)
        < lax.broadcasted_iota(jnp.int32, (tok, tok), 1)
    ).astype(jnp.bfloat16)
    row_iota = lax.broadcasted_iota(jnp.int32, (rows, tok), 0)

    def picker(code, wanted, live):
        named = ((code // LEVELS) == wanted) & live
        mask = jnp.sum(named.astype(jnp.float32), axis=1)
        level = jnp.sum(jnp.where(named, (code % LEVELS), 0).astype(jnp.float32), axis=1) / LEVELS
        rank = jnp.dot(mask.astype(jnp.bfloat16), before, preferred_element_type=jnp.float32)
        picks, weights = [], None
        for s in range(sources):
            place = jnp.where(mask[s : s + 1] > 0, rank[s : s + 1].astype(jnp.int32) + s * capacity, -1)
            hit = row_iota == place
            scaled = jnp.sum(jnp.where(hit, level[s : s + 1], 0.0), axis=1, keepdims=True)
            weights = scaled if weights is None else weights + scaled
            picks.append(hit.astype(jnp.float32).astype(jnp.bfloat16))
        return jnp.concatenate(picks, axis=1), weights

    picks, weights, spare_weights = [], [], []
    for j in range(subs):
        code = codes[j * sources : (j + 1) * sources]
        pick, weight = picker(code, my_id, serves)
        spare_pick, spare_weight = picker(code, failed_id, holds > 0)
        both = jnp.concatenate([pick, spare_pick], axis=0)
        picks.append(both)
        weights.append(weight)
        spare_weights.append(spare_weight)
        for n in range(0, width, tile):
            got = jnp.dot(
                both, tokens[j * part : (j + 1) * part, n : n + tile], preferred_element_type=jnp.float32
            ).astype(jnp.bfloat16)
            rows_in[j * rows : (j + 1) * rows, n : n + tile] = got[:rows]
            spare_in[j * rows : (j + 1) * rows, n : n + tile] = got[rows:]

    for n in range(0, hidden.shape[1], tile):
        hidden[:, n : n + tile] = gated_unit(
            jnp.dot(rows_in[...], w_gate[0, :, n : n + tile], preferred_element_type=jnp.float32)
        ).astype(jnp.bfloat16)
    for n in range(0, width, tile):
        result = jnp.dot(hidden[...], w_down[0, :, n : n + tile], preferred_element_type=jnp.float32)
        result = result.astype(jnp.bfloat16).astype(jnp.float32)
        for j in range(subs):
            rows_out[j, :rows, n : n + tile] = (result[j * rows : (j + 1) * rows] * weights[j]).astype(
                jnp.bfloat16
            )

    @pl.when(holds > 0)
    def _():
        spare_hidden[...] = gated_unit(
            jnp.dot(spare_in[...], spare_gate[0], preferred_element_type=jnp.float32)
        ).astype(jnp.bfloat16)
        for n in range(0, width, tile):
            result = jnp.dot(
                spare_hidden[...], spare_down[0, :, n : n + tile], preferred_element_type=jnp.float32
            )
            for j in range(subs):
                rows_out[j, rows:, n : n + tile] = (
                    result[j * rows : (j + 1) * rows] * spare_weights[j]
                ).astype(jnp.bfloat16)

    @pl.when(holds <= 0)
    def _():
        rows_out[:, rows:, :] = jnp.zeros((subs, rows, width), jnp.bfloat16)

    for j in range(subs):
        for n in range(0, width, tile):
            out[j * part : (j + 1) * part, n : n + tile] = lax.dot_general(
                picks[j],
                rows_out[j, :, n : n + tile],
                (((0,), (0,)), ((), ())),
                preferred_element_type=jnp.float32,
            ).astype(jnp.bfloat16)


def run_experts(scalars, codes, tokens, w_gate, w_down, spare_gate, spare_down, capacity):
    owners, top, tok = codes.shape
    width, inner, spare = w_gate.shape[1], w_gate.shape[2], spare_gate.shape[2]
    sources = max(1, 128 // capacity)
    subs = 2 if sources * tok <= 512 else 1
    step = subs * sources
    rows = sources * capacity
    whole = lambda a: pl.BlockSpec(a.shape, lambda i: (0, 0, 0), pipeline_mode=pl.Buffered(1))
    return pl.pallas_call(
        functools.partial(expert_kernel, subs=subs, sources=sources, capacity=capacity),
        grid=(owners // step,),
        out_shape=jax.ShapeDtypeStruct((owners * tok, width), jnp.bfloat16),
        in_specs=[
            pl.BlockSpec(memory_space=pltpu.SMEM),
            pl.BlockSpec((step, top, tok), lambda i: (i, 0, 0)),
            pl.BlockSpec((step * tok, width), lambda i: (i, 0)),
            whole(w_gate),
            whole(w_down),
            whole(spare_gate),
            whole(spare_down),
        ],
        out_specs=pl.BlockSpec((step * tok, width), lambda i: (i, 0)),
        scratch_shapes=[
            pltpu.VMEM((subs * rows, width), jnp.bfloat16),
            pltpu.VMEM((subs * rows, width), jnp.bfloat16),
            pltpu.VMEM((subs * rows, inner), jnp.bfloat16),
            pltpu.VMEM((subs * rows, spare), jnp.bfloat16),
            pltpu.VMEM((subs, 2 * rows, width), jnp.bfloat16),
        ],
        compiler_params=pltpu.CompilerParams(vmem_limit_bytes=56 * 1024 * 1024),
        cost_estimate=pl.CostEstimate(
            flops=owners * capacity * 4 * width * (inner + spare),
            bytes_accessed=4 * width * (inner + spare) + 4 * owners * tok * width,
            transcendentals=owners * capacity * inner,
        ),
        name="experts",
    )(scalars, codes, tokens, w_gate, w_down, spare_gate, spare_down)


def group_kernel(failed, holders, *refs, others, adds, tok, top, capacity):
    blocks, weights_hbm, shares, refs = refs[:4], refs[4:8], refs[8 : 8 + 2 * adds], refs[8 + 2 * adds + others :]
    keep0, keep1, send = refs[:3]
    far, refs = refs[3 : 3 + adds], refs[3 + adds :]
    held, w_gate, w_down, spare_gate, spare_down = refs[:5]
    rows_in, spare_in, hidden, spare_hidden, rows_out, dense, summed, fetched, stored = refs[5:]
    width, inner = w_gate.shape
    tile = 768
    my_id, failed_id = lax.axis_index("expert"), failed[0]
    holds = holders[0, failed_id] == my_id
    for j in range(1, holders.shape[0]):
        holds = holds | (holders[j, failed_id] == my_id)
    copies = []

    def fetch(source, target, start=True):
        copy = pltpu.make_async_copy(source, target, fetched.at[len(copies)])
        if start:
            copy.start()
        copies.append(copy)
        return copy

    gate_hbm, down_hbm, spare_gate_hbm, spare_down_hbm = weights_hbm
    block_copies = [fetch(block, held.at[s]) for s, block in enumerate(blocks)]
    gate_copies = [
        fetch(gate_hbm.at[0, n : n + tile], w_gate.at[n : n + tile]) for n in range(0, width, tile)
    ]
    share_copies = []
    if adds:
        share_copies = [fetch(shares[0], summed.at[0]), fetch(shares[1].at[1], summed.at[1])]
    spare_copies = [
        fetch(spare_gate_hbm.at[0], spare_gate, False),
        fetch(spare_down_hbm.at[0], spare_down, False),
    ]

    @pl.when(holds)
    def _():
        for copy in spare_copies:
            copy.start()

    down_copies = [
        fetch(down_hbm.at[0, n : n + tile], w_down.at[n : n + tile]) for n in range(0, inner, tile)
    ]

    count = len(blocks)
    before = (
        lax.broadcasted_iota(jnp.int32, (tok, tok), 0)
        < lax.broadcasted_iota(jnp.int32, (tok, tok), 1)
    ).astype(jnp.float32).astype(jnp.bfloat16)
    own = lax.broadcasted_iota(jnp.int32, (2 * count, tok), 0) < count
    wanted = jnp.where(own, my_id, failed_id).astype(jnp.float32)
    serves = jnp.where(my_id != failed_id, 1.0, 0.0)
    live = jnp.where(own, serves, jnp.where(holds, 1.0, 0.0))
    slots = 2 * capacity
    row_iota = lax.broadcasted_iota(jnp.int32, (slots, tok), 0)
    lane_iota = lax.broadcasted_iota(jnp.int32, (tok, slots), 1)

    for copy in block_copies:
        copy.wait()
    meta = jnp.concatenate([held[s, tok : tok + 8, :].astype(jnp.float32)[:1] for s in range(count)] * 2, axis=0)
    mask = jnp.zeros((2 * count, tok), jnp.float32)
    level = jnp.zeros((2 * count, tok), jnp.float32)
    for k in range(top):
        named = jnp.where(meta[:, k * tok : (k + 1) * tok] == wanted, live, 0.0)
        high = meta[:, (top + k) * tok : (top + k + 1) * tok]
        low = meta[:, (2 * top + k) * tok : (2 * top + k + 1) * tok]
        mask = mask + named
        level = level + named * ((high * 32.0 + low) / LEVELS)
    rank = jnp.dot(mask.astype(jnp.bfloat16), before, preferred_element_type=jnp.float32)
    place = jnp.where(mask > 0, rank + jnp.where(own, 0.0, float(capacity)), -1.0)
    place_rows = place.astype(jnp.int32)
    place_columns = place.T.astype(jnp.int32)

    spreads, weights = [], []
    for s in range(count):
        here, there = place_rows[s : s + 1], place_rows[count + s : count + s + 1]
        hit_here, hit_there = row_iota == here, row_iota == there
        pick = jnp.where(hit_here | hit_there, 1.0, 0.0).astype(jnp.bfloat16)
        weights.append(
            jnp.sum(
                jnp.where(hit_here, level[s : s + 1], 0.0)
                + jnp.where(hit_there, level[count + s : count + s + 1], 0.0),
                axis=1,
                keepdims=True,
            )
        )
        here, there = place_columns[:, s : s + 1], place_columns[:, count + s : count + s + 1]
        spreads.append(jnp.where((lane_iota == here) | (lane_iota == there), 1.0, 0.0).astype(jnp.bfloat16))
        for n in range(0, width, tile):
            got = jnp.dot(pick, held[s, :tok, n : n + tile], preferred_element_type=jnp.float32).astype(
                jnp.bfloat16
            )
            rows_in[s * capacity : (s + 1) * capacity, n : n + tile] = got[:capacity]
            spare_in[s * capacity : (s + 1) * capacity, n : n + tile] = got[capacity:]

    for copy in gate_copies:
        copy.wait()
    for n in range(0, inner, tile):
        hidden[:, n : n + tile] = gated_unit(
            jnp.dot(rows_in[...], w_gate[:, n : n + tile], preferred_element_type=jnp.float32)
        ).astype(jnp.bfloat16)
    stores = []
    if adds:
        for copy in share_copies:
            copy.wait()
        total = summed[0].astype(jnp.float32) + summed[1].astype(jnp.float32)
        summed[0] = total.astype(jnp.bfloat16)
        stores.append(pltpu.make_async_copy(summed.at[0], far[0], stored.at[0]))
        stores[0].start()

    @pl.when(holds)
    def _():
        for copy in spare_copies:
            copy.wait()
        spare_hidden[...] = gated_unit(
            jnp.dot(spare_in[...], spare_gate[...], preferred_element_type=jnp.float32)
        ).astype(jnp.bfloat16)
        for n in range(0, width, tile):
            result = jnp.dot(
                spare_hidden[...], spare_down[:, n : n + tile], preferred_element_type=jnp.float32
            )
            for s in range(count):
                rows_out[s, capacity:, n : n + tile] = (
                    result[s * capacity : (s + 1) * capacity] * weights[s][capacity:]
                ).astype(jnp.bfloat16)

    @pl.when(jnp.logical_not(holds))
    def _():
        rows_out[:, capacity:, :] = jnp.zeros((count, capacity, width), jnp.bfloat16)

    for copy in down_copies:
        copy.wait()
    for n in range(0, width, tile):
        result = jnp.dot(hidden[...], w_down[:, n : n + tile], preferred_element_type=jnp.float32)
        result = result.astype(jnp.bfloat16).astype(jnp.float32)
        for s in range(count):
            rows_out[s, :capacity, n : n + tile] = (
                result[s * capacity : (s + 1) * capacity] * weights[s][:capacity]
            ).astype(jnp.bfloat16)
            dense[s, :, n : n + tile] = jnp.dot(
                spreads[s], rows_out[s, :, n : n + tile], preferred_element_type=jnp.float32
            ).astype(jnp.bfloat16)
            target = (keep0, keep1, send.at[0], send.at[1])[s]
            stores.append(
                pltpu.make_async_copy(
                    dense.at[s, :, n : n + tile], target.at[:, n : n + tile], stored.at[len(stores)]
                )
            )
            stores[-1].start()
    for copy in stores:
        copy.wait()


def run_group(failed, holders, blocks, weights, shares, earlier, tok, top, capacity):
    width, inner, spare = weights[0].shape[1], weights[0].shape[2], weights[2].shape[2]
    count, adds = len(blocks), len(shares) // 2
    rows = count * capacity
    hbm = pl.BlockSpec(memory_space=pl.ANY)
    smem = pl.BlockSpec(memory_space=pltpu.SMEM)
    block = pltpu.HBM((tok, width), jnp.bfloat16)
    return pl.pallas_call(
        functools.partial(
            group_kernel, others=len(earlier), adds=adds, tok=tok, top=top, capacity=capacity
        ),
        out_shape=(block, block, pltpu.HBM((2, tok, width), jnp.bfloat16)) + (block,) * adds,
        in_specs=[smem, smem] + [hbm] * (count + 4 + len(shares) + len(earlier)),
        out_specs=(hbm,) * (3 + adds),
        scratch_shapes=[
            pltpu.VMEM((count, *blocks[0].shape), jnp.bfloat16),
            pltpu.VMEM((width, inner), jnp.bfloat16),
            pltpu.VMEM((inner, width), jnp.bfloat16),
            pltpu.VMEM((width, spare), jnp.bfloat16),
            pltpu.VMEM((spare, width), jnp.bfloat16),
            pltpu.VMEM((rows, width), jnp.bfloat16),
            pltpu.VMEM((rows, width), jnp.bfloat16),
            pltpu.VMEM((rows, inner), jnp.bfloat16),
            pltpu.VMEM((rows, spare), jnp.bfloat16),
            pltpu.VMEM((count, 2 * capacity, width), jnp.bfloat16),
            pltpu.VMEM((count, tok, width), jnp.bfloat16),
            pltpu.VMEM((2, tok, width), jnp.bfloat16),
            pltpu.SemaphoreType.DMA((count + inner // 512 + width // 512 + 4,)),
            pltpu.SemaphoreType.DMA((1 + count * (width // 512),)),
        ],
        compiler_params=pltpu.CompilerParams(vmem_limit_bytes=VMEM_GRANT),
        cost_estimate=pl.CostEstimate(
            flops=rows * 4 * width * (inner + spare),
            bytes_accessed=4 * width * (inner + spare) + 4 * count * tok * width,
            transcendentals=rows * inner,
        ),
        name="group",
    )(failed, holders, *map(in_hbm, (*blocks, *weights, *shares, *earlier)))


def in_hbm(array):
    return pltpu.with_memory_space_constraint(array, pltpu.HBM)


def nothing(*refs):
    pass


def come_after(value, *others, flops=0):
    return pl.pallas_call(
        nothing,
        out_shape=pltpu.HBM(value.shape, value.dtype),
        in_specs=[pl.BlockSpec(memory_space=pl.ANY)] * (1 + len(others)),
        out_specs=pl.BlockSpec(memory_space=pl.ANY),
        input_output_aliases={0: 0},
        compiler_params=pltpu.CompilerParams(vmem_limit_bytes=VMEM_GRANT),
        cost_estimate=pl.CostEstimate(flops=flops, bytes_accessed=0, transcendentals=0),
        name="after",
    )(*map(in_hbm, (value, *others)))


def folded_ring(length):
    return [0] + list(range(1, length, 2)) + list(range(2, length, 2))[::-1]


def by_permutes(failed, holders, tokens, expert_ids, gate_levels, weights, owners, capacity):
    tok, top = expert_ids.shape
    width = tokens.shape[1]
    order = folded_ring(owners // 4)
    steps = len(order)
    after = {a: order[(i + 1) % steps] for i, a in enumerate(order)}
    round_ring = [(d, after[d // 4] * 4 + d % 4) for d in range(owners)]
    over_y = [(d, d ^ 2) for d in range(owners)]
    over_core = [(d, d ^ 1) for d in range(owners)]
    move = lambda a, pairs: lax.ppermute(a, "expert", pairs)
    f32 = lambda a: a.astype(jnp.float32)
    add = lambda a, b: (f32(a) + f32(b)).astype(jnp.bfloat16)

    meta = jnp.concatenate([expert_ids.T, gate_levels.T >> 5, gate_levels.T & 31], axis=0)
    meta = meta.astype(jnp.bfloat16).reshape(1, 3 * top * tok)
    meta = jnp.pad(meta, ((0, 7), (0, width - 3 * top * tok)))
    held = [jnp.concatenate([tokens, meta], axis=0)]
    held.append(move(held[0], round_ring))
    across, kept, got = [], [], []
    last = steps - 1

    def add_group(k, shares, *earlier):
        blocks = (held[k], across[k], move(held[k], over_core), move(across[k], over_core))
        keep0, keep1, send, *summed = run_group(
            failed, holders, blocks, weights, shares, earlier, tok, top, capacity
        )
        kept.append((keep0, keep1))
        return send, *summed

    def total(k, rows, *more):
        result = f32(kept[k][0][rows]) + f32(got[k][0, rows])
        for a in more:
            result = result + f32(a)
        return result.astype(jnp.bfloat16)

    across.append(move(held[0], over_y))
    (send,) = add_group(0, ())
    from_y, arrived, own = None, (), None
    every = slice(0, tok)
    for k in range(1, steps):
        across.append(move(across[-1], round_ring) if k == last else move(held[k], over_y))
        if k == 1:
            across[1] = come_after(across[1], kept[0][0])
        if k < last:
            held.append(come_after(move(held[k], round_ring), kept[k - 1][0]))
        got.append(move(come_after(send, across[k], held[min(k + 1, last)]), over_core))
        if k > 2:
            arrived = (move(total(k - 2, every, from_y, *arrived), round_ring),)
        if k > 1:
            from_y = move(add(kept[k - 1][1], got[k - 1][1]), over_y)
        if k == 2:
            send, own = add_group(k, (kept[0][1], got[0]), kept[k - 1][0])
        else:
            (send,) = add_group(k, (), kept[k - 1][0])
    got.append(move(send, over_core))

    halves = (slice(0, tok // 2), slice(tok // 2, tok))
    passing = [
        move(total(last - 1, rows, from_y[rows], *(a[rows] for a in arrived)), round_ring) for rows in halves
    ]
    shares = [move(add(kept[last][1][rows], got[last][1, rows]), over_y) for rows in halves]
    first, second = halves
    passed = total(last, first, shares[0], passing[0])
    follows = total(last, second, shares[1], come_after(passing[1], passed))
    own = move(come_after(own, passed), over_y)
    passed = come_after(move(passed, round_ring), flops=4 * 10**9)
    return total(0, every, own, jnp.concatenate([passed, move(follows, round_ring)], axis=0))


def shards(
    tokens,
    expert_ids,
    gate_levels,
    failed_device,
    replica_holders,
    w_gate,
    w_down,
    spare_gate,
    spare_down,
):
    owners = lax.axis_size("expert")
    tok_count, top_count = expert_ids.shape
    capacity = 2 * tok_count * top_count // owners
    my_index = lax.axis_index("expert").astype(jnp.int32)
    failed_id = failed_device[0]
    holder_row = lax.dynamic_index_in_dim(replica_holders, failed_id, 0, keepdims=False)
    holds = jnp.any(holder_row == my_index).astype(jnp.int32)
    scalars = jnp.stack([my_index, failed_id, holds])
    weights = (w_gate, w_down, spare_gate, spare_down)
    if 12 <= owners <= 32 and owners % 4 == 0 and 3 * top_count * tok_count <= tokens.shape[1]:
        return by_permutes(
            failed_device, replica_holders.T, tokens, expert_ids, gate_levels, weights, owners, capacity
        )
    codes = (expert_ids * LEVELS + gate_levels).T
    all_codes = lax.all_gather(codes, "expert", axis=0)
    all_tokens = lax.all_gather(tokens, "expert", axis=0, tiled=True)
    dense = run_experts(scalars, all_codes, all_tokens, *weights, capacity)
    return lax.psum_scatter(dense, "expert", scatter_dimension=0, tiled=True)


def solution(mesh):
    in_specs = (
        P(("group", "expert"), None),
        P(("group", "expert"), None),
        P(("group", "expert"), None),
        P(),
        P(),
        P("expert", None, None),
        P("expert", None, None),
        P("expert", None, None),
        P("expert", None, None),
    )
    out_specs = P(("group", "expert"), None)
    return jax.shard_map(shards, mesh=mesh, in_specs=in_specs, out_specs=out_specs, check_vma=False)
```
